32 devices in a mesh: seq: 8 (over z, x), row: 4 (over y, core).
Axes of the slice: x: 2, y: 2, z: 4, core: 2. Of those that a mesh axis runs over, the one named last changes fastest.
Arguments:
- pixels: bfloat16 [16, 8192, 261], P('seq', 'row'), may hold values from -6 to 6
- pixel_seg: int32 [16, 8192], P('seq', 'row'), may hold values from -1 to 7, as said below
- latent_seg: int32 [16, 512], P('seq', 'row'), may hold values from 0 to 7
- latent_init: bfloat16 [512, 1024], P('row'), may hold values from -6 to 6
- cotangent: bfloat16 [16, 512, 1024], P('seq', 'row'), may hold values from -6 to 6
- pixel_gain: float32 [261], replicated, may hold values from 0.1 to 1.9
- query_gain: float32 [1024], replicated, may hold values from 0.1 to 1.9
- query_weight: bfloat16 [1024, 1024], replicated, may hold values from -0.1875 to 0.1875
- key_weight: bfloat16 [261, 1024], replicated, may hold values from -0.375 to 0.375
- value_weight: bfloat16 [261, 1024], replicated, may hold values from -0.375 to 0.375
- output_weight: bfloat16 [1024, 1024], replicated, may hold values from -6 to 6
- mlp_gain: float32 [1024], replicated, may hold values from 0.1 to 1.9
- up_weight: bfloat16 [1024, 1024], replicated, may hold values from -0.1875 to 0.1875
- down_weight: bfloat16 [1024, 1024], replicated, may hold values from -0.1875 to 0.1875
- self_gain: float32 [1024], replicated, may hold values from 0.1 to 1.9
- self_query: bfloat16 [1024, 1024], replicated, may hold values from -0.1875 to 0.1875
- self_key: bfloat16 [1024, 1024], replicated, may hold values from -0.1875 to 0.1875
- self_value: bfloat16 [1024, 1024], replicated, may hold values from -0.1875 to 0.1875
- self_output: bfloat16 [1024, 1024], replicated, may hold values from -1.5 to 1.5
- second_gain: float32 [1024], replicated, may hold values from 0.1 to 1.9
- second_up: bfloat16 [1024, 1024], replicated, may hold values from -0.1875 to 0.1875
- second_down: bfloat16 [1024, 1024], replicated, may hold values from -0.1875 to 0.1875
Outputs:
- latents: bfloat16 [16, 512, 1024], P('seq', 'row')
- pixel_grad: float32 [16, 8192, 261], P('seq', 'row')
- init_grad: float32 [512, 1024], P('row', 'seq')
- pixel_gain_grad: float32 [261], replicated
- query_gain_grad: float32 [1024], replicated
- mlp_gain_grad: float32 [1024], replicated
- self_gain_grad: float32 [1024], replicated
- second_gain_grad: float32 [1024], replicated
- query_weight_grad: float32 [1024, 1024], P(None, 'seq')
- key_weight_grad: float32 [261, 1024], P(None, 'seq')
- value_weight_grad: float32 [261, 1024], P(None, 'seq')
- output_weight_grad: float32 [1024, 1024], P(None, 'seq')
- up_weight_grad: float32 [1024, 1024], P(None, 'seq')
- down_weight_grad: float32 [1024, 1024], P(None, 'seq')
- self_query_grad: float32 [1024, 1024], P(None, 'seq')
- self_key_grad: float32 [1024, 1024], P(None, 'seq')
- self_value_grad: float32 [1024, 1024], P(None, 'seq')
- self_output_grad: float32 [1024, 1024], P(None, 'seq')
- second_up_grad: float32 [1024, 1024], P(None, 'seq')
- second_down_grad: float32 [1024, 1024], P(None, 'seq')
The draws below stay inside these ranges and needn't reach their ends.
Inputs may be any that keep to these rules, and one draw needn't show every extreme that they name: `pixel_seg`: slot p of a sequence is empty (-1) or holds image p // 1024; each image fills the first half or more of its 1024 slots, and the last slot of each region is empty. `latent_seg`: every latent's image has pixels in its sequence.
All inputs are finite; a program needn't handle non-finite values.
Results may differ from the reference program's by a relative error of at most 0.023.
Values may be sent and summed in bfloat16 or wider, within the bound.
A program may use at most 512 MiB of HBM per device.

```python
import jax
import jax.numpy as jnp
from jax import lax

D = 1024
FEAT = 261
HEADS = 8
LAT = 512
PIX = 8192
IMGS = 8
SEQS = 16


def draw_pixel_seg(key, part):
    key = jax.random.fold_in(key, 11)
    region = PIX // IMGS
    counts = jax.random.randint(key, (SEQS, IMGS), region // 2, region)
    places = jnp.arange(region, dtype=jnp.int32)
    owners = jnp.arange(IMGS, dtype=jnp.int32)
    labels = jnp.where(places[None, None, :] < counts[:, :, None], owners[None, :, None], -1)
    return labels.reshape(SEQS, PIX).astype(jnp.int32)


def with_ends(entries, own_key, low, largest):
    extent = entries.shape
    index_at = [jax.random.randint(jax.random.fold_in(own_key, axis), (), 0, extent[axis]) for axis in range(len(extent))]
    entries = entries.at[tuple(index_at)].set(low)
    longest = extent.index(max(extent))
    index_at[longest] = (index_at[longest] + 1) % extent[longest]
    return entries.at[tuple(index_at)].set(largest)


def level_of(own_key, shape, shards, smallest, top_value):
    factor_of, own = 1.0, jax.random.fold_in(own_key, 6)
    for axis_at, shards_of in shards:
        steps = jnp.exp(jax.random.uniform(jax.random.fold_in(own, axis_at), (shards_of,), jnp.float32, smallest / len(shards), top_value / len(shards)))
        factor_of = factor_of * jnp.repeat(steps, shape[axis_at] // shards_of).reshape([-1 if axis == axis_at else 1 for axis in range(len(shape))])
    return factor_of


def gaussian(key, shape, width, reach, shards=(), kind=jnp.bfloat16):
    values = jax.random.normal(key, shape, jnp.float32) * width
    if len(shards) > 0:
        values = level_of(key, shape, shards, -0.22, 0.18) * values
    return jnp.clip(values, min=-reach, max=reach).astype(kind)


def setup_inputs(seed: int = 0) -> dict:
    key_of = jax.random.split(jax.random.key(seed), 23)
    return {
        "pixels": gaussian(key_of[0], (SEQS, PIX, FEAT), 1.0, 6.0, ((0, 8), (1, 4))),
        "pixel_seg": draw_pixel_seg(jax.random.fold_in(key_of[22], 71), 0),
        "latent_seg": with_ends(jax.random.randint(key_of[2], (SEQS, LAT), 0, IMGS), jax.random.fold_in(key_of[2], 1), 0, IMGS - 1).astype(jnp.int32),
        "latent_init": gaussian(key_of[3], (LAT, D), 1.0, 6.0, ((0, 4),)),
        "cotangent": gaussian(key_of[4], (SEQS, LAT, D), 1.0, 6.0, ((0, 8), (1, 4))),
        "pixel_gain": jnp.clip(1.0 + 0.18 * jax.random.normal(key_of[5], (FEAT,), jnp.float32), 0.1, 1.9),
        "query_gain": jnp.clip(1.0 + 0.18 * jax.random.normal(key_of[6], (D,), jnp.float32), 0.1, 1.9),
        "query_weight": gaussian(key_of[7], (D, D), D ** -0.5, 0.1875),
        "key_weight": gaussian(key_of[8], (FEAT, D), FEAT ** -0.5, 0.375),
        "value_weight": gaussian(key_of[9], (FEAT, D), FEAT ** -0.5, 0.375),
        "output_weight": gaussian(key_of[10], (D, D), (max(1, D * IMGS // PIX)) ** -0.5, 6.0),
        "mlp_gain": jnp.clip(1.0 + 0.18 * jax.random.normal(key_of[11], (D,), jnp.float32), 0.1, 1.9),
        "up_weight": gaussian(key_of[12], (D, D), D ** -0.5, 0.1875),
        "down_weight": gaussian(key_of[13], (D, D), D ** -0.5, 0.1875),
        "self_gain": jnp.clip(1.0 + 0.18 * jax.random.normal(key_of[14], (D,), jnp.float32), 0.1, 1.9),
        "self_query": gaussian(key_of[15], (D, D), D ** -0.5, 0.1875),
        "self_key": gaussian(key_of[16], (D, D), D ** -0.5, 0.1875),
        "self_value": gaussian(key_of[17], (D, D), D ** -0.5, 0.1875),
        "self_output": gaussian(key_of[18], (D, D), (max(1, D * IMGS // LAT)) ** -0.5, 1.5),
        "second_gain": jnp.clip(1.0 + 0.18 * jax.random.normal(key_of[19], (D,), jnp.float32), 0.1, 1.9),
        "second_up": gaussian(key_of[20], (D, D), D ** -0.5, 0.1875),
        "second_down": gaussian(key_of[21], (D, D), D ** -0.5, 0.1875),
    }


@jax.custom_vjp
def low(v):
    return lax.optimization_barrier(v.astype(jnp.bfloat16)).astype(jnp.float32)

@jax.custom_vjp
def low_back(v):
    return v

def low_keep(v):
    return (low(v), None)

def low_pass(kept, grad):
    return (grad,)

def back_keep(v):
    return (v, None)

def back_low(kept, grad):
    return (low(grad),)
low.defvjp(low_keep, low_pass)
low_back.defvjp(back_keep, back_low)
EPSILON = 1e-05
NEGATIVE = -1000000000.0

def layer_norm(values, norm_gain):
    centre = values - lax.optimization_barrier(jnp.mean(values, axis=-1, keepdims=True))
    spread = lax.optimization_barrier(jnp.mean(centre * centre, axis=-1, keepdims=True))
    return centre * lax.rsqrt(spread + EPSILON) * norm_gain

def product(former, latter):
    return jnp.dot(former, latter, precision=lax.Precision.HIGHEST)

def attend(queries, keys, values, query_ids, key_ids, scale):
    scores = jnp.einsum('qhd,khd->hqk', queries, keys, precision=lax.Precision.HIGHEST) * scale
    scores = low_back(scores)
    same = (query_ids[:, None] == key_ids[None, :])[None]
    scores = jnp.where(same, scores, NEGATIVE)
    probs = low(jax.nn.softmax(scores, axis=-1))
    mixed = jnp.einsum('hqk,khd->qhd', probs, values, precision=lax.Precision.HIGHEST)
    return low(low_back(mixed))

def feed_forward(stream, norm_gain, up_matrix, down_matrix):
    normed = low(layer_norm(stream, norm_gain))
    hidden = low_back(product(normed, up_matrix))
    active = low(low_back(jax.nn.gelu(hidden, approximate=False)))
    return stream + low_back(product(active, down_matrix))

def one_sequence(pixel_rows, pixel_ids, latent_ids, start_latents, params):
    pixel_gain, query_gain, query_weight, key_weight, value_weight, output_weight, mlp_gain, up_weight, down_weight, self_gain, self_query, self_key, self_value, self_output, second_gain, second_up, second_down = params
    pixel_normed = low(layer_norm(pixel_rows, pixel_gain))
    query_normed = low(layer_norm(start_latents, query_gain))
    cross_q = low(low_back(product(query_normed, query_weight)))
    cross_k = low(low_back(product(pixel_normed, key_weight)))
    cross_v = low(low_back(product(pixel_normed, value_weight)))
    attended = attend(cross_q[:, None, :], cross_k[:, None, :], cross_v[:, None, :], latent_ids, pixel_ids, D ** (-0.5))
    attended = attended.reshape(LAT, D)
    stream_one = start_latents + low_back(product(attended, output_weight))
    stream_two = feed_forward(stream_one, mlp_gain, up_weight, down_weight)
    self_normed = low(layer_norm(stream_two, self_gain))
    self_q = low(low_back(product(self_normed, self_query))).reshape(LAT, HEADS, D // HEADS)
    self_k = low(low_back(product(self_normed, self_key))).reshape(LAT, HEADS, D // HEADS)
    self_v = low(low_back(product(self_normed, self_value))).reshape(LAT, HEADS, D // HEADS)
    self_mixed = attend(self_q, self_k, self_v, latent_ids, latent_ids, (D // HEADS) ** (-0.5)).reshape(LAT, D)
    stream_three = stream_two + low_back(product(self_mixed, self_output))
    return feed_forward(stream_three, second_gain, second_up, second_down)

def reference(pixels, pixel_seg, latent_seg, latent_init, cotangent, pixel_gain, query_gain, query_weight, key_weight, value_weight, output_weight, mlp_gain, up_weight, down_weight, self_gain, self_query, self_key, self_value, self_output, second_gain, second_up, second_down):
    params = tuple((item.astype(jnp.float32) for item in (pixel_gain, query_gain, query_weight, key_weight, value_weight, output_weight, mlp_gain, up_weight, down_weight, self_gain, self_query, self_key, self_value, self_output, second_gain, second_up, second_down)))
    pixel_float = pixels.astype(jnp.float32)
    init_float = latent_init.astype(jnp.float32)
    checked = jax.checkpoint(one_sequence)

    def forward(pixel_all, start_latents, *weights):

        def per_sequence(items):
            return checked(items[0], items[1], items[2], start_latents, weights)
        return lax.map(per_sequence, (pixel_all, pixel_seg, latent_seg))
    result, pullback = jax.vjp(forward, pixel_float, init_float, *params)
    grads = pullback(cotangent.astype(jnp.float32))
    return (result.astype(jnp.bfloat16), grads[0], grads[1], grads[2], grads[3], grads[8], grads[11], grads[16], grads[4], grads[5], grads[6], grads[7], grads[9], grads[10], grads[12], grads[13], grads[14], grads[15], grads[17], grads[18])
```

```python
import functools
import math

import jax
import jax.numpy as jnp
from jax import lax
from jax.experimental import pallas as pl
from jax.experimental.pallas import tpu as pltpu
from jax.sharding import PartitionSpec as P

HEADS = 8
EPSILON = 1e-05
NEGATIVE = -1e9
BF = jnp.bfloat16
F32 = jnp.float32
LANES = 128
FEAT_PAD = 384
MAIN = 256
CAT = 2 * MAIN + LANES
MESH = pl.DeviceIdType.MESH


def dot(a, b):
    return jnp.dot(a, b, preferred_element_type=F32)


def dot_tn(a, b):
    return lax.dot_general(a, b, (((0,), (0,)), ((), ())), preferred_element_type=F32)


def dot_nt(a, b):
    return lax.dot_general(a, b, (((1,), (1,)), ((), ())), preferred_element_type=F32)


def fill_rest(rest, matrix):
    rest[...] = jnp.zeros(rest.shape, rest.dtype)
    rest[: matrix.shape[0] - MAIN, :] = matrix[MAIN:, :]


def norm_parts(values):
    centre = values - jnp.mean(values, axis=-1, keepdims=True)
    rs = lax.rsqrt(jnp.mean(centre * centre, axis=-1, keepdims=True) + EPSILON)
    return centre * rs, rs


def norm_back(unit, rs, gain, upstream):
    scaled = upstream * gain
    grad = rs * (
        scaled
        - jnp.mean(scaled, axis=-1, keepdims=True)
        - unit * jnp.mean(scaled * unit, axis=-1, keepdims=True)
    )
    return grad, jnp.sum(upstream * unit, axis=0)


def gelu_parts(hidden):
    cdf = 0.5 * (1.0 + lax.erf(hidden * math.sqrt(0.5)))
    pdf = jnp.exp(-0.5 * hidden * hidden) * (1.0 / math.sqrt(2.0 * math.pi))
    return hidden * cdf, cdf + hidden * pdf


NORMED1, ACTIVE1, SELFN, MIXED, NORMED2, ACTIVE2 = range(6)
DOWN2, UP2, SOUT, SQ, SK, SV, DOWN1, UP1 = range(8)
LEFT = {
    DOWN2: ACTIVE2, UP2: NORMED2, SOUT: MIXED, SQ: SELFN, SK: SELFN, SV: SELFN,
    DOWN1: ACTIVE1, UP1: NORMED1,
}
MATS = 8
FEATURE_UNIT = 2 * MATS
INIT_UNIT = FEATURE_UNIT + 1
UNITS = INIT_UNIT + 1


class Remote:
    def __init__(self, log, src, dst, send_sem, recv_sem, device):
        self.copy = pltpu.make_async_remote_copy(
            src_ref=src, dst_ref=dst, send_sem=send_sem, recv_sem=recv_sem,
            device_id=device, device_id_type=MESH,
        )
        self.copy.start()
        self.arrived = self.sent = False
        log.append(self)

    def wait_recv(self):
        if not self.arrived:
            self.copy.wait_recv()
        self.arrived = True

    def wait_send(self):
        if not self.sent:
            self.copy.wait_send()
        self.sent = True

    def finish(self):
        self.wait_recv()
        self.wait_send()


def unit_orders(bits):
    rest = list(range(bits))
    head, tail = rest[:2], rest[2:]
    by_y = ["y"] + rest
    by_first = head + ["y"] + tail
    by_second = head[::-1] + ["y"] + tail
    kinds = [by_y, by_first, by_second]
    return [kinds[u % 3] for u in range(UNITS)]


def stage_shapes(order, width):
    shapes, planes, size = [], 2, width
    for axis in order:
        if axis == "y":
            planes = 1
            shapes.append((size, LANES))
        else:
            size //= 2
            shapes.append((2, size, LANES) if planes == 2 else (size, LANES))
    return shapes


def main_kernel(cfg, *refs):
    shards, width, count, sizes = cfg
    bits = shards.bit_length() - 1
    share = width // shards
    half = width // 2
    block = count // 2
    lat = 2 * count
    head_width = width // HEADS
    cross_scale = 1.0 / math.sqrt(width)
    self_scale = 1.0 / math.sqrt(head_width)
    orders = unit_orders(bits)
    it = iter(refs)

    def take(n=None):
        return next(it) if n is None else [next(it) for _ in range(n)]

    (z_hbm, pixel_gain, pseg_ref, init_ref, cot_hbm, seg_ref, wk_hbm, wv_hbm) = take(8)
    gain_refs = take(4)
    w_hbm = take(10)
    (lat_ref, sm_out, gat_ref, initg_ref, fold, zall, y_ref, pspill) = take(8)
    (wslots, wkv, w_rest, zbuf, ain1, asum, ain2, amix, amix_in, amat, fbuf, rsb, acts, acts_in, slopes,
     qbuf, kv, pbuf, dmix, dkv_in, gall, gcd_in, fin, da_all, bsum, gsum, idrow,
     sm, xcat, flat, rest0, pixel_rs, gain_col, fin_in, part) = take(35)
    recv = [take(len(orders[u])) for u in range(UNITS)]
    smr = take(sizes["small_stages"])
    (wsem, zsem, usend, urecv, csend, crecv) = take(6)

    j = lax.axis_index("seq")
    row = lax.axis_index("row")
    core, chip = row % 2, row // 2
    peer = {"row": row + 1 - 2 * core}
    across = {"row": row + 2 - 4 * chip}
    diagonal = {"row": 3 - row}
    bit_of = [(j // (1 << b)) % 2 for b in range(bits)]
    partner = {b: {"seq": j + (1 - 2 * bit_of[b]) * (1 << b)} for b in range(bits)}
    partner["y"] = across
    stream = fbuf.at[pl.ds(0, count)]
    upstr = fbuf.at[pl.ds(count, count)]
    dnorm = stream

    def act(k):
        return pl.ds(k * count, count)

    WQ, WO, UP, DOWN, QW, KW, VW, SO, UPB, DOWNB = range(10)
    uses = [WQ, WO, UP, DOWN, KW, VW, QW, SO, UPB, DOWNB, DOWNB, UPB, SO, QW, KW, VW, DOWN, UP, WO]
    nslots = wslots.shape[0]
    at_use = [0]

    def weight_copy(i):
        return pltpu.make_async_copy(w_hbm[uses[i]], wslots.at[i % nslots], wsem.at[i % nslots])

    def weight(expect):
        i = at_use[0]
        assert uses[i] == expect
        at_use[0] += 1
        weight_copy(i).wait()
        return wslots.at[i % nslots]

    def weight_done():
        i = at_use[0] - 1 + nslots
        if i < len(uses):
            weight_copy(i).start()

    features = wk_hbm.shape[0]
    pixel_copies = []
    for i, lo in enumerate(range(0, z_hbm.shape[0], width)):
        rows = min(width, z_hbm.shape[0] - lo)
        pixel_copies.append(pltpu.make_async_copy(
            z_hbm.at[pl.ds(lo, rows)], part.at[i, pl.ds(0, rows)], zsem.at[i]
        ))
    weight_copy(0).start()
    wk_copy = pltpu.make_async_copy(wk_hbm, wkv, wsem.at[nslots])
    wk_copy.start()
    for i in range(1, nslots):
        weight_copy(i).start()
    wv_copy = pltpu.make_async_copy(wv_hbm, wkv, wsem.at[nslots + 1])
    for copy in pixel_copies:
        copy.start()

    barrier = pltpu.get_barrier_semaphore()
    partners = [peer, across, diagonal] + [partner[b] for b in range(bits)]
    for p in partners:
        pl.semaphore_signal(barrier, inc=1, device_id=p, device_id_type=MESH)
    copies = []
    slot_count = [0]

    def remote(src, dst, device):
        slot = slot_count[0]
        slot_count[0] += 1
        return Remote(copies, src, dst, csend.at[slot], crecv.at[slot], device)

    def local(src, dst, slot):
        copy = pltpu.make_async_copy(src, dst, wsem.at[nslots + 2 + slot])
        copy.start()
        return copy

    def rows_loop(body, step=64, total=None):
        def run(i, carry):
            body(pl.ds(pl.multiple_of(i * step, step), step))
            return carry
        lax.fori_loop(0, (total or count) // step, run, 0, unroll=2)

    def columns_loop(body, step=256, total=width):
        def run(i, carry):
            body(pl.ds(pl.multiple_of(i * step, step), step))
            return carry
        lax.fori_loop(0, total // step, run, 0, unroll=2)

    def layer(k, into):
        def body(rows):
            unit, rs = norm_parts(stream[rows, :])
            rsb[k, rows, :] = jnp.broadcast_to(rs, (rs.shape[0], LANES))
            place = pl.ds(pl.multiple_of(into * count + rows.start, rows.size), rows.size)
            acts[place, :] = (unit * gain_refs[k][...]).astype(BF)
        rows_loop(body)

    def layer_back(k, normed, into, start=None):
        gain = gain_refs[k][...]
        inverse = 1.0 / gain

        def body(i, total):
            rows = pl.ds(pl.multiple_of(i * 64, 64), 64)
            place = pl.ds(pl.multiple_of(normed * count + i * 64, 64), 64)
            dn = dnorm[rows, :]
            unit = acts[place, :].astype(F32) * inverse
            scaled = dn * gain
            rs = rsb[k, rows, :][:, :1]
            mean = jnp.mean(scaled, axis=-1, keepdims=True)
            along = jnp.mean(scaled * unit, axis=-1, keepdims=True)
            before = upstr[rows, :] if start is None else gall[start, 0, rows, :].astype(F32)
            after = before + rs * (scaled - mean - unit * along)
            upstr[rows, :] = after
            gall[into, 0, rows, :] = after.astype(BF)
            return total + jnp.sum(dn * unit, axis=0, keepdims=True)
        gsum[pl.ds(k, 1), :] = lax.fori_loop(
            0, count // 64, body, jnp.zeros((1, width), F32), unroll=2
        )

    act_copies, grad_copies = {}, {}

    def share_act(k):
        away = pl.ds(pl.multiple_of((1 - core) * half, half), half)
        act_copies[k] = remote(acts.at[act(k), away], acts_in.at[k], peer)

    def share_grad(m):
        grad_copies[m] = remote(gall.at[m, 0], gall.at[m, 1], peer)

    clock = [0.0]
    small = dict(lo=0, size=lat, stage=0, up=[], copy=None, due=1e9)
    axes = [(core, peer), (chip, across)] + [(bit_of[b], partner[b]) for b in range(bits)]

    def small_send():
        bit, device = axes[small["stage"]]
        size = small["size"]
        if size > 16:
            size //= 2
            away = pl.multiple_of(small["lo"] + (1 - bit) * size, 16)
            keep = pl.multiple_of(small["lo"] + bit * size, 16)
            small["up"].append((device, keep, size))
            small["lo"], small["size"] = keep, size
        else:
            away = small["lo"]
        small["copy"] = remote(sm.at[pl.ds(away, size)], smr[small["stage"]], device)
        small["due"] = clock[0] + 2.5 + size * 512 * 4 / 75e3

    def small_grow():
        device, lo, size = small["up"].pop()
        rows = pl.ds(lo, size)
        small["copy"] = remote(sm_out.at[rows], sm_out.at[rows], device)
        small["due"] = clock[0] + 2.5 + size * 512 * 4 / 75e3

    def small_step():
        copy, size = small["copy"], small["size"]
        copy.wait_recv()
        if small["stage"] < len(axes):
            copy.wait_send()
            rows = pl.ds(small["lo"], size)
            sm[rows, :] = sm[rows, :] + smr[small["stage"]][...]
            small["stage"] += 1
            if small["stage"] < len(axes):
                small_send()
                return
            sm_out[rows, :] = sm[rows, :]
        if small["up"]:
            small_grow()
        else:
            small["due"] = 1e9

    state = {}
    free = {}
    pending = []

    def region(u, planes, lo, size):
        if planes == 2:
            return part.at[pl.ds(2 * u, 2), pl.ds(lo, size)]
        return part.at[2 * u + chip, pl.ds(lo, size)]

    def send_stage(u):
        s = state[u]
        axis = orders[u][s["stage"]]
        k = s["stage"]
        if axis == "y":
            src = part.at[2 * u + 1 - chip, pl.ds(s["lo"], s["size"])]
            s["planes"] = 1
        else:
            size = s["size"] // 2
            keep = s["lo"] + bit_of[axis] * size
            away = s["lo"] + (1 - bit_of[axis]) * size
            src = region(u, s["planes"], pl.multiple_of(away, share), size)
            s["lo"], s["size"] = pl.multiple_of(keep, share), size
        slot = sum(len(orders[v]) for v in range(u)) + k
        s["copy"] = Remote(copies, src, recv[u][k], usend.at[slot], urecv.at[slot], partner[axis])
        link = {"y": "y", 0: "x"}.get(axis, "z%s" % axis)
        begin = max(clock[0], free.get(link, 0.0))
        took = s["size"] * s["planes"] * LANES * 2 * (2 if link in ("x", "y", "z1") else 4) / 75e3
        free[link] = begin + took
        s["due"] = begin + took + 4.0
        pending.append(u)

    def finish_stage(u):
        s = state[u]
        k = s["stage"]
        s["copy"].wait_recv()
        last = k == len(orders[u]) - 1
        if last:
            total = part[pl.ds(2 * u + chip, 1), pl.ds(s["lo"], s["size"])][0] + recv[u][k][...]
            if u == INIT_UNIT:
                initg_ref[...] = total
            else:
                fin[u] = total
            s["done"] = True
            done_units.append(u)
            gather_ready()
            return
        step = min(s["size"], 256)
        for p in range(s["planes"]):
            def add(i, carry):
                off = pl.multiple_of(i * step, step)
                mine = pl.ds(pl.multiple_of(s["lo"] + off, share), step)
                if s["planes"] == 2:
                    got = recv[u][k][p, pl.ds(off, step), :]
                    part[2 * u + p, mine, :] = part[2 * u + p, mine, :] + got
                else:
                    got = recv[u][k][pl.ds(off, step), :]
                    at = pl.ds(2 * u + chip, 1)
                    part[at, mine, :] = part[at, mine, :] + got[None]
                return carry
            lax.fori_loop(0, s["size"] // step, add, 0)
        s["stage"] += 1
        send_stage(u)

    done_units, gathers = [], []
    groups = [list(range(0, 6)), list(range(6, 12)), list(range(12, FEATURE_UNIT + 1))]

    def gather_ready():
        while len(gathers) < len(groups) and all(u in done_units for u in groups[len(gathers)]):
            g = groups[len(gathers)]
            span = pl.ds(g[0], len(g))
            from_chip = remote(fin.at[span], fin_in.at[span], across)
            remote(fin.at[span], gat_ref.at[row, span], peer)
            gathers.append((g, from_chip, local(fin.at[span], gat_ref.at[row, span], len(gathers))))

    def serve():
        at = min((state[u]["due"], u) for u in pending) if pending else (1e9, None)
        if small["due"] <= at[0]:
            clock[0] = max(clock[0], small["due"])
            small_step()
        else:
            clock[0] = max(clock[0], at[0]) + 0.3
            pending.remove(at[1])
            finish_stage(at[1])

    def next_due():
        return min([small["due"]] + [state[u]["due"] for u in pending])

    def tick(us):
        clock[0] += 1.6 * us
        while next_due() <= clock[0]:
            serve()

    def begin_unit(u):
        state[u] = dict(stage=0, planes=2, lo=0, size=width, done=False)
        send_stage(u)

    def position(u, block):
        seq_bits = [a for a in orders[u] if a != "y"]
        pos = 0
        for at, b in enumerate(seq_bits):
            pos = pos + ((block // (1 << b)) % 2) * (1 << (bits - 1 - at))
        return pos

    def store_plane(u, plane, value):
        if share != LANES:
            value = value.astype(F32).T.astype(BF)
        for block_at in range(shards):
            place = pl.ds(position(u, block_at) * share, share)
            if share == LANES:
                part[pl.ds(2 * u + plane, 1), place, :] = value[:, block_at * share : (block_at + 1) * share][None]
            else:
                part[pl.ds(2 * u + plane, 1), place, :] = value[block_at * share : (block_at + 1) * share][None]

    def weight_grad(m):
        left = LEFT[m]
        act_copies[left].wait_recv()
        grad_copies[m].wait_recv()

        def run(plane, carry):
            own = pl.ds(pl.multiple_of(core * half + plane * MAIN, MAIN), MAIN)
            theirs = pl.ds(pl.multiple_of(plane * MAIN, MAIN), MAIN)
            lefts = jnp.concatenate([acts[act(left), own], acts_in[left, :, theirs]], axis=0)
            total = dot_tn(lefts, gall[m].reshape(2 * count, width)).astype(BF)
            store_plane(2 * m, plane, total[:LANES])
            store_plane(2 * m + 1, plane, total[LANES:])
            return carry
        lax.fori_loop(0, 2, run, 0)
        begin_unit(2 * m)
        begin_unit(2 * m + 1)

    cot_rows = pl.ds(pl.multiple_of(chip * block, block), block)
    c_own = local(cot_hbm.at[chip], gall.at[DOWN2, 0, cot_rows], 3)
    zbuf[pl.ds(chip, 1)] = init_ref[...][None]
    unit, unused = norm_parts(init_ref[...].astype(F32))
    own_normed = (unit * gain_refs[3][...]).astype(BF)
    w = weight(WQ)
    queries = dot(own_normed, w[...]).astype(BF)
    weight_done()
    wk_copy.wait()
    fill_rest(w_rest, wkv)
    fold_main = dot_nt(queries, wkv[:MAIN, :]) * cross_scale
    fold_rest = dot_nt(queries, w_rest[...]) * cross_scale
    own_rows = pl.ds(pl.multiple_of(row * block, block), block)
    seg = seg_ref[...].astype(F32)
    ids = jnp.concatenate([seg, jnp.zeros((LANES - 2, block), F32)], axis=0).T
    ids = pltpu.roll(ids, 5, 1)
    fold[own_rows, :MAIN] = fold_main.astype(BF)
    fold[own_rows, MAIN:] = (fold_rest + ids).astype(BF)
    wv_copy.start()
    pl.semaphore_wait(barrier, len(partners))
    fold_copies = [remote(fold.at[own_rows], fold.at[own_rows], p) for p in (across, diagonal, peer)]
    z_copy = remote(init_ref, zbuf.at[chip], across)
    c_copy = remote(cot_hbm.at[1 - chip], gall.at[DOWN2, 0, cot_rows], across)
    group = pixel_rs.shape[0]
    blocks = group // 4
    tall = gain_col.shape[0]

    fold_in = width // group

    def pixel_row(f, lo=0, rows=group):
        at = pl.ds(pl.multiple_of((f % fold_in) * group + lo, rows), rows)
        return part[pl.ds(f // fold_in, 1), at, :][0].astype(F32)

    zero = jnp.zeros((group, LANES), F32)
    for copy in pixel_copies:
        copy.wait()
    mean = lax.fori_loop(0, features, lambda f, acc: acc + pixel_row(f), zero, unroll=9)
    mean = mean * (1.0 / features)

    def spread(f, acc):
        centre = pixel_row(f) - mean
        return acc + centre * centre
    spread_sum = lax.fori_loop(0, features, spread, zero, unroll=9)
    rs_all = lax.rsqrt(spread_sum * (1.0 / features) + EPSILON)
    pixel_rs[...] = rs_all
    gain_col[...] = jnp.ones(gain_col.shape, F32)
    flat[features * group // 2 :, :] = jnp.zeros(((tall - features) * group // 2, LANES), F32)
    for s in range(2):
        xcat[s, 2 * MAIN + 16 :, :] = jnp.zeros((LANES - 16, xcat.shape[2]), BF)
    for k in range(2):
        half_rows = slice(k * (group // 2), (k + 1) * (group // 2))
        half_mean, half_rs = mean[half_rows], rs_all[half_rows]

        def scale(f, carry, k=k, half_mean=half_mean, half_rs=half_rs):
            value = pixel_row(f, k * (group // 2), group // 2)
            rows = pl.ds(pl.multiple_of(f * (group // 2), group // 2), group // 2)
            flat[rows, :] = (value - half_mean) * (half_rs * pixel_gain[f])
            if k == 0:
                gain_col[pl.ds(f, 1), :] = jnp.full((1, LANES), pixel_gain[f], F32)
            return carry
        lax.fori_loop(0, features, scale, 0, unroll=9)
        for s in range(2):
            for jb in range(blocks):
                cols = pl.ds(jb * LANES, LANES)
                value = flat[pl.ds(2 * jb + s, tall, stride=group // 2), :]
                xcat[s, k * MAIN : (k + 1) * MAIN, cols] = value[:MAIN].astype(BF)
                if k == 0:
                    rest0[s, :, cols] = value[MAIN:]
                else:
                    both = jnp.concatenate([rest0[s, :, cols], value[MAIN:]], axis=0)
                    xcat[s, 2 * MAIN : 2 * MAIN + 16, cols] = both.astype(BF)
    for copy in fold_copies:
        copy.wait_recv()

    lane = lax.broadcasted_iota(jnp.int32, (1, LANES), 1)
    image = (2 * row).astype(F32)

    def selectors(s, rows):
        ids = fold[rows, MAIN:].astype(F32)
        ids = jnp.where(s == 0, ids[:, 5:6], ids[:, 6:7])
        return jnp.where(ids == image, 1.0, 0.0), jnp.where(ids == image + 1.0, 1.0, 0.0)

    def spread_out(source, s, rows):
        first, second = selectors(s, rows)
        main = source[:, :MAIN].astype(F32)
        rest = jnp.where(lane < 5, source[:, MAIN:].astype(F32), 0.0)
        rest = rest * first + pltpu.roll(rest, 8, 1) * second
        return jnp.concatenate([main * first, main * second, rest], axis=1).astype(BF)

    def pull_in(s, rows, zero, one, rest):
        first, second = selectors(s, rows)
        rest = jnp.where(lane < 5, rest * first + pltpu.roll(rest, LANES - 8, 1) * second, 0.0)
        return zero * first + one * second, rest

    slots = xcat.shape[2]
    core_copies = []

    def send_core(turn):
        core_copies.append(remote(amat.at[turn, :, 1 - core], ain1.at[turn], peer))

    def core_sum(turn):
        core_copies[turn].wait_recv()
        return amat[turn, :, pl.ds(core, 1)][:, 0] + ain1[turn]

    for turn in range(2):
        s = 1 - chip if turn == 0 else chip
        seq = pl.ds(s, 1)
        for i in range(4):
            rows = pl.ds(i * block, block)
            gall[2 + 2 * turn + i // 2, 0, (i % 2) * block : (i % 2 + 1) * block, :CAT] = spread_out(
                fold[rows, :], s, rows
            )
        first_ok = jnp.where(pseg_ref[seq, :slots] == 2 * row, 1.0, 0.0)
        second_ok = jnp.where(pseg_ref[seq, slots:] == 2 * row + 1, 1.0, 0.0)

        def score_cols(cols, seq=seq, turn=turn):
            queries_cat = jnp.concatenate(
                [gall[2 + 2 * turn, 0, :, :CAT], gall[3 + 2 * turn, 0, :, :CAT]], axis=0
            )
            fbuf[:, cols] = dot(queries_cat, xcat[seq, :, cols][0])
        columns_loop(score_cols, 256, slots)
        if turn == 1:
            asum[...] = core_sum(0)
            step2 = remote(asum, ain2, across)

        def soften(rows, s=s, seq=seq, first_ok=first_ok, second_ok=second_ok):
            first, unused = selectors(s, rows)
            allowed = second_ok + first * (first_ok - second_ok)
            scores = jnp.where(allowed > 0.5, fbuf[rows, :], NEGATIVE)
            weights = jnp.exp(scores - jnp.max(scores, axis=1, keepdims=True))
            prob = (weights * (1.0 / jnp.sum(weights, axis=1, keepdims=True))).astype(BF)
            pbuf[seq, rows, :] = prob[None]
        rows_loop(soften, 64, lat)
        probs = pbuf[seq][0]
        zero = dot_nt(probs, xcat[seq, :MAIN, :][0])
        one = dot_nt(probs, xcat[seq, MAIN : 2 * MAIN, :][0])
        rest = dot_nt(probs, xcat[seq, 2 * MAIN :, :][0])
        main, rest = pull_in(s, pl.ds(0, lat), zero, one, rest)
        amat[turn, :, :, :, :MAIN] = main.astype(BF).reshape(2, 2, block, MAIN)
        amat[turn, :, :, :, MAIN:] = rest.astype(BF).reshape(2, 2, block, LANES)
        send_core(turn)
    spill = local(pbuf, pspill, 4)

    for at in range(4):
        who = core if at < 2 else 1 - core
        rows = pl.ds(pl.multiple_of((2 * (at % 2) + who) * block, block), block)
        turned = fold[rows, MAIN:].astype(F32).T
        idrow[:, at * block : (at + 1) * block] = jnp.where(chip == 0, turned[5:6], turned[6:7])
    own_ids = []
    for h in range(2):
        rows = pl.ds(pl.multiple_of((2 * h + core) * block, block), block)
        ids = fold[rows, MAIN:].astype(F32)
        own_ids.append(jnp.where(chip == 0, ids[:, 5:6], ids[:, 6:7]))
    idcol = jnp.concatenate(own_ids, axis=0)
    z_copy.wait_recv()
    remote(init_ref, zall.at[row], peer)
    other_row = row + 2 - 4 * chip
    remote(zbuf.at[1 - chip], zall.at[other_row], peer)
    z_local = [local(init_ref, zall.at[row], 5), local(zbuf.at[1 - chip], zall.at[other_row], 6)]
    c_copy.wait_recv()
    c_own.wait()
    share_grad(DOWN2)
    wv_copy.wait()
    fill_rest(w_rest, wkv)
    step2.wait_recv()
    amix[...] = (core_sum(1) + ain2[...]).reshape(count, FEAT_PAD)
    amix_copy = remote(amix, amix_in, peer)

    def attended_cols(cols):
        value = dot(amix[:, :MAIN], wkv[:MAIN, cols]) + dot(amix[:, MAIN:], w_rest[:, cols])
        qbuf[:, cols] = value.astype(BF)
    columns_loop(attended_cols)
    w = weight(WO)

    def one_cols(cols):
        start = zbuf[:, :, cols].reshape(count, cols.size).astype(F32)
        stream[:, cols] = start + dot(qbuf[...], w[:, cols])
    columns_loop(one_cols)
    weight_done()

    def mlp(k, normed, active, up_id, down_id):
        layer(k, normed)
        share_act(normed)
        w_up = weight(up_id)

        def up_cols(cols):
            value, slope = gelu_parts(dot(acts[act(normed), :], w_up[:, cols]))
            acts[act(active), cols] = value.astype(BF)
            slopes[active // 4, :, cols] = slope.astype(BF)
        columns_loop(up_cols)
        weight_done()
        share_act(active)
        w_down = weight(down_id)

        def down_cols(cols):
            stream[:, cols] += dot(acts[act(active), :], w_down[:, cols])
        columns_loop(down_cols)
        weight_done()

    mlp(0, NORMED1, ACTIVE1, UP, DOWN)
    layer(1, SELFN)
    share_act(SELFN)
    kv_copies = {}
    for index, dst in ((KW, 0), (VW, 1), (QW, None)):
        w_now = weight(index)

        def project(cols, dst=dst, w_now=w_now):
            value = dot(acts[act(SELFN), :], w_now[:, cols]).astype(BF)
            if dst is None:
                qbuf[:, cols] = value
            else:
                kv[dst, 0, :, cols] = value
        columns_loop(project)
        weight_done()
        if dst is not None:
            kv_copies[dst] = remote(kv.at[dst, 0], kv.at[dst, 1], peer)
    spill.wait()
    kv_copies[0].wait_recv()
    kv_copies[1].wait_recv()

    def heads(body):
        def run(pair, carry):
            for side in range(2):
                cols = pl.ds(pl.multiple_of((2 * pair + side) * head_width, head_width), head_width)
                rows = pl.ds(pl.multiple_of((pair % 2) * count, count), count)
                body(cols, (pl.ds(pair // 2, 1), rows, pl.ds(side * lat, lat)))
            return carry
        lax.fori_loop(0, HEADS // 2, run, 0)

    def attend(cols, keep):
        keys = kv[0, :, :, cols].reshape(lat, head_width)
        values = kv[1, :, :, cols].reshape(lat, head_width)
        scores = dot_nt(qbuf[:, cols], keys) * self_scale
        scores = jnp.where(idcol == idrow[...], scores, NEGATIVE)
        weights = jnp.exp(scores - jnp.max(scores, axis=1, keepdims=True))
        prob = (weights * (1.0 / jnp.sum(weights, axis=1, keepdims=True))).astype(BF)
        pbuf[keep] = prob[None]
        acts[act(MIXED), cols] = dot(prob, values).astype(BF)
    heads(attend)
    share_act(MIXED)
    w_so = weight(SO)

    def three_cols(cols):
        stream[:, cols] += dot(acts[act(MIXED), :], w_so[:, cols])
    columns_loop(three_cols)
    weight_done()
    mlp(2, NORMED2, ACTIVE2, UPB, DOWNB)
    dmix[...] = stream[...].astype(BF)
    lat_ref[pl.ds(chip, 1)] = dmix[pl.ds(pl.multiple_of(chip * block, block), block), :][None]
    lat_copy = remote(
        dmix.at[pl.ds(pl.multiple_of((1 - chip) * block, block), block)], lat_ref.at[chip], across
    )

    weight_grad(DOWN2)
    tick(2.0)

    def mlp_back(k, normed, active, m_down, m_up, up_id, down_id, into, start=None):
        w_down = weight(down_id)

        def act_cols(cols):
            grad = dot_nt(gall[m_down, 0], w_down[cols, :]).astype(BF).astype(F32)
            gall[m_up, 0, :, cols] = (grad * slopes[active // 4, :, cols].astype(F32)).astype(BF)
        columns_loop(act_cols)
        weight_done()
        share_grad(m_up)
        tick(1.0)
        w_up = weight(up_id)

        def norm_cols(cols):
            dnorm[:, cols] = dot_nt(gall[m_up, 0], w_up[cols, :])
        columns_loop(norm_cols)
        weight_done()
        if into == 0:
            grad_copies[DOWN2].wait_send()
            grad_copies[UP2].wait_send()
        layer_back(k, normed, into, start)
        tick(1.5)

    mlp_back(2, NORMED2, ACTIVE2, DOWN2, UP2, UPB, DOWNB, SOUT, DOWN2)

    share_grad(SOUT)
    weight_grad(UP2)
    tick(1.5)
    w_so2 = weight(SO)
    lat_copy.wait_send()

    def mixed_cols(cols):
        dmix[:, cols] = dot_nt(gall[SOUT, 0], w_so2[cols, :]).astype(BF)
    columns_loop(mixed_cols)
    weight_done()

    def attend_back(cols, keep):
        keys = kv[0, :, :, cols].reshape(lat, head_width)
        values = kv[1, :, :, cols].reshape(lat, head_width)
        dm = dmix[:, cols]
        prob_b = pbuf[keep][0]
        prob = prob_b.astype(F32)
        grad = dot_nt(dm, values)
        delta = jnp.sum(prob * grad, axis=1, keepdims=True)
        score = (prob * (grad - delta)).astype(BF)
        gall[SQ, 0, :, cols] = (dot(score, keys) * self_scale).astype(BF)
        dk = (dot_tn(score, qbuf[:, cols]) * self_scale).astype(BF)
        dv = dot_tn(prob_b, dm).astype(BF)
        gall[SK, 0, :, cols] = dk[:count]
        gall[SV, 0, :, cols] = dv[:count]
        kv[0, 1, :, cols] = dk[count:]
        kv[1, 1, :, cols] = dv[count:]
    heads(attend_back)
    unspill = local(pspill, pbuf, 4)
    share_dkv = remote(kv.at[:, 1], dkv_in, peer)
    share_grad(SQ)
    tick(4.0)
    weight_grad(SOUT)
    tick(1.0)
    share_dkv.wait_recv()

    def add_kv(rows):
        for at, m in ((0, SK), (1, SV)):
            gall[m, 0, rows, :] = gall[m, 0, rows, :] + dkv_in[at, rows, :]
    rows_loop(add_kv)
    share_grad(SK)
    share_grad(SV)
    for at, (m, index) in enumerate(((SQ, QW), (SK, KW), (SV, VW))):
        w_now = weight(index)

        def normed_cols(cols, at=at, m=m, w_now=w_now):
            value = dot_nt(gall[m, 0], w_now[cols, :])
            if at == 0:
                dnorm[:, cols] = value
            else:
                dnorm[:, cols] += value
        columns_loop(normed_cols)
        weight_done()
    layer_back(1, SELFN, DOWN1)
    share_grad(DOWN1)
    tick(3.0)
    weight_grad(SQ)
    tick(1.0)
    weight_grad(SK)
    tick(1.0)
    mlp_back(0, NORMED1, ACTIVE1, DOWN1, UP1, UP, DOWN, 0)

    w_o = weight(WO)

    def attended_back(cols):
        gall[1, 0, :, cols] = dot_nt(gall[0, 0], w_o[cols, :]).astype(BF)
    columns_loop(attended_back)
    weight_done()
    share_cd = remote(gall.at[1 - core, 0], gcd_in, peer)
    folded = jnp.concatenate([dot_nt(gall[1, 0], wkv[:MAIN, :]), dot_nt(gall[1, 0], w_rest[...])], axis=1)
    along = jnp.sum(folded * amix[...].astype(F32), axis=0, keepdims=True)
    gsum[3:4, :FEAT_PAD] = along
    gsum[3:4, FEAT_PAD:] = jnp.zeros((1, width - FEAT_PAD), F32)
    da_all[pl.ds(chip, 1), :, pl.ds(core, 1)] = folded.astype(BF).reshape(1, 2, 1, block, FEAT_PAD)
    mine = da_all.at[chip, :, core]
    da_across = remote(mine, mine, across)
    da_peer = remote(mine, mine, peer)
    tick(2.0)
    weight_grad(SV)
    tick(1.0)
    da_across.wait_recv()
    other = da_all.at[1 - chip, :, core]
    da_other = remote(other, other, peer)
    weight_grad(DOWN1)
    tick(1.0)
    weight_grad(UP1)
    tick(1.0)

    share_cd.wait_recv()
    amix_copy.wait_recv()
    lefts = jnp.concatenate([amix[:, :MAIN], amix_in[:, :MAIN]], axis=0)
    grads = jnp.concatenate([gall[pl.ds(core, 1), 0][0], gcd_in[...]], axis=0)
    total = dot_tn(lefts, grads).astype(BF)
    for plane in range(2):
        store_plane(FEATURE_UNIT, plane, total[plane * LANES : (plane + 1) * LANES])
    begin_unit(FEATURE_UNIT)
    for plane in range(2):
        store_plane(INIT_UNIT, plane, upstr[plane * block : (plane + 1) * block, :].astype(BF))
    begin_unit(INIT_UNIT)
    gsum[4:, :] = jnp.zeros((gsum.shape[0] - 4, width), F32)
    rests = [dot_tn(amix[:, MAIN:], gall[side, 0])[:8] for side in range(2)]
    for i in range(8):
        cols = slice(i * LANES, (i + 1) * LANES)
        both = jnp.concatenate([rests[0][:, cols], rests[1][:, cols]], axis=0)
        sm[16 * i : 16 * (i + 1), FEAT_PAD:] = both.astype(BF)
        sm[128 + 16 * i : 128 + 16 * (i + 1), FEAT_PAD:] = gsum[:, cols].astype(BF)
    sm[256:, FEAT_PAD:] = jnp.zeros((lat - 256, LANES), BF)
    tick(2.0)

    da_peer.wait_recv()
    da_other.wait_recv()
    unspill.wait()

    def score_rows(s):
        return wslots.at[s, pl.ds(0, lat)]

    def da_rows(s):
        return wslots.at[s, pl.ds(lat, lat), pl.ds(0, CAT)]

    def q_rows(s):
        return wslots.at[2, pl.ds(s * lat, lat), pl.ds(0, CAT)]

    for s in range(2):
        for i in range(4):
            rows = pl.ds(i * block, block)
            wslots[s, lat + i * block : lat + (i + 1) * block, :CAT] = spread_out(
                da_all[s, i // 2, i % 2], s, rows
            )
            wslots[2, s * lat + i * block : s * lat + (i + 1) * block, :CAT] = spread_out(
                fold[rows, :], s, rows
            )

        def back_cols(cols, s=s):
            fbuf[:, cols] = dot(wslots[s, lat:, :CAT], xcat[s, :, cols])
        columns_loop(back_cols, 256, slots)

        def score_back(rows, s=s):
            prob = pbuf[s, rows, :].astype(F32)
            grad = fbuf[rows, :]
            delta = jnp.sum(prob * grad, axis=1, keepdims=True)
            wslots[s, rows, :] = (prob * (grad - delta)).astype(BF)
        rows_loop(score_back, 64, lat)
        scores = wslots[s, :lat, :]
        zero = dot_nt(scores, xcat[s, :MAIN, :])
        one = dot_nt(scores, xcat[s, MAIN : 2 * MAIN, :])
        rest = dot_nt(scores, xcat[s, 2 * MAIN :, :])
        main, rest = pull_in(s, pl.ds(0, lat), zero, one, rest)
        if s == 0:
            bsum[:, :MAIN] = main
            bsum[:, MAIN:] = rest
        else:
            sm[:, :MAIN] = (bsum[:, :MAIN] + main).astype(BF)
            sm[:, MAIN:FEAT_PAD] = (bsum[:, MAIN:] + rest).astype(BF)
        tick(4.0)

    small_send()
    for copy in act_copies.values():
        copy.wait_send()
    for s in range(2):
        for at, (lo, size) in enumerate(((0, MAIN), (MAIN, MAIN), (2 * MAIN, LANES))):
            cols = pl.ds(lo, size)
            total = dot_tn(wslots[2, s * lat : (s + 1) * lat, cols], wslots[s, :lat, :])
            total = total + dot_tn(wslots[s, lat:, cols], pbuf[s])
            acts[pl.ds(s * CAT + lo, size), :] = total.astype(BF)
            tick(2.0)

    main_gain, rest_gain = gain_col[:MAIN, :], gain_col[MAIN:, :]
    y_copy = None
    for k in range(2):
        if y_copy is not None:
            y_copy.wait()
        for s in range(2):

            def pixel_step(jb, carry, k=k, s=s):
                cols = pl.ds(pl.multiple_of(jb * LANES, LANES), LANES)
                up_main = acts[s * CAT + k * MAIN : s * CAT + (k + 1) * MAIN, cols].astype(F32)
                up_rest = acts[s * CAT + 2 * MAIN : s * CAT + 2 * MAIN + 16, cols].astype(F32)
                up_rest = up_rest[8 * k : 8 * k + 8]
                x_main = xcat[s, k * MAIN : (k + 1) * MAIN, cols].astype(F32)
                x_rest = xcat[s, 2 * MAIN : 2 * MAIN + 16, cols].astype(F32)[8 * k : 8 * k + 8]
                rs = pixel_rs[pl.ds(k * (group // 2) + 2 * jb + s, 1), :]
                scaled_main, scaled_rest = up_main * main_gain, up_rest * rest_gain

                def mean_of(a, b):
                    whole = jnp.sum(a, axis=0, keepdims=True) + jnp.sum(b, axis=0, keepdims=True)
                    return whole * (1.0 / features)
                centre = mean_of(scaled_main, scaled_rest)
                along = mean_of(up_main * x_main, up_rest * x_rest)
                unit_main, unit_rest = x_main / main_gain, x_rest / rest_gain
                out_main = rs * (scaled_main - centre - unit_main * along)
                out_rest = rs * (scaled_rest - centre - unit_rest * along)
                flat[pl.ds(2 * jb + s, tall, stride=group // 2), :] = jnp.concatenate(
                    [out_main, out_rest], axis=0
                )
                return carry
            lax.fori_loop(0, blocks, pixel_step, 0)
            tick(2.0)
        y_copy = local(flat.at[pl.ds(0, features * group // 2)], y_ref.at[k], 7 + k)
    while next_due() < 1e9:
        serve()
    for g, from_chip, own in gathers:
        from_chip.wait_recv()
        span = pl.ds(g[0], len(g))
        remote(fin_in.at[span], gat_ref.at[other_row, span], peer)
        own.wait()
        z_local.append(local(fin_in.at[span], gat_ref.at[other_row, span], 9 + g[0] // 6))
    for copy in z_local + [y_copy]:
        copy.wait()
    for copy in copies:
        copy.finish()


def finish_kernel(*refs):
    it = iter(refs)

    def take(n=None):
        return next(it) if n is None else [next(it) for _ in range(n)]

    y_in, lat_in = take(2)
    ins = take(8)
    query_gain, pixel_gain = take(2)
    y_out, lat_out, init_out, pixel_gain_out, key_out, value_out = take(6)
    gain_outs = take(4)
    mat_outs = take(MATS + 2)
    held = take(8)
    summed, small, fold, init_all, wq, wk, wv, init_sum = held
    unit, normed, total, mats, wk_rest, wv_rest, y_buf, lat_buf, back = take(9)
    sem, out_sem = take(2)
    features, width = ins[5].shape
    lat = init_all.shape[0]
    block = lat // 4
    j = lax.axis_index("seq")
    row = lax.axis_index("row")
    cross_scale = 1.0 / math.sqrt(width)

    through = [
        (pltpu.make_async_copy(y_in.at[k], y_buf.at[:, pl.ds(k * y_in.shape[2], y_in.shape[2])], sem.at[8 + k]))
        for k in range(2)
    ] + [pltpu.make_async_copy(lat_in, lat_buf, sem.at[10])]
    copies = []
    for i, (src, dst) in enumerate(zip(ins, held)):
        copies.append(pltpu.make_async_copy(src, dst, sem.at[i]))
        copies[-1].start()
        if i == 0:
            for copy in through:
                copy.start()
    outs = []

    def put(src, dst):
        copy = pltpu.make_async_copy(src, dst, out_sem.at[len(outs)])
        copy.start()
        outs.append(copy)

    copies[0].wait()
    for m in range(MATS):
        for r in range(4):
            for h in range(2):
                at = (r % 2) * (width // 2) + (r // 2) * 2 * LANES + h * LANES
                mats[m, at : at + LANES, :] = summed[r, 2 * m + h].astype(F32)
        put(mats.at[m], mat_outs[m])
    for copy in through:
        copy.wait()
    put(y_buf, y_out)
    put(lat_buf, lat_out)

    copies[3].wait()
    query_rs = []
    for r in range(4):
        rows = pl.ds(r * block, block)
        value, scale = norm_parts(init_all[rows, :].astype(F32))
        unit[rows, :] = value
        normed[rows, :] = (value * query_gain[...]).astype(BF)
        query_rs.append(scale)
    for copy in copies[1:3] + copies[4:]:
        copy.wait()
    fill_rest(wv_rest, wv)
    fill_rest(wk_rest, wk)
    my_cols = pl.ds(pl.multiple_of(j * LANES, LANES), LANES)

    for n in range(width // 256):
        cols = pl.ds(n * 256, 256)
        value = dot(small[:, :MAIN], wk[:MAIN, cols]) + dot(small[:, MAIN:FEAT_PAD], wk_rest[:, cols])
        total[:, cols] = (value * cross_scale).astype(BF)

    def put_turned(index, value):
        for n in range(width // LANES):
            mats[index, n * LANES : (n + 1) * LANES, :] = value[:, n * LANES : (n + 1) * LANES].T
        put(mats.at[index], mat_outs[index])
    put_turned(MATS, dot_tn(total[:, my_cols], normed[...]))
    outer = [
        [summed[2 * y + c, FEATURE_UNIT].astype(F32) for y in range(2)] for c in range(2)
    ]
    rests = small[pl.ds(pl.multiple_of(j * 16, 16), 16), FEAT_PAD:]
    value_out[:LANES, :] = outer[1][0]
    value_out[LANES:MAIN, :] = outer[1][1]
    value_out[MAIN:, :] = rests.astype(F32)[8 : 8 + features - MAIN]
    summed_c = jnp.concatenate(outer[0], axis=0).astype(BF)
    put_turned(MATS + 1, dot_tn(summed_c, wv[:MAIN, :]) + dot_tn(rests, wv_rest[:16, :]))
    my_queries = dot(normed[...], wq[:, my_cols]).astype(BF)
    key_turned = dot_tn(my_queries, small[:, :FEAT_PAD]) * cross_scale
    key_out[...] = jnp.concatenate(
        [key_turned[:, n * LANES : (n + 1) * LANES].T for n in range(3)], axis=0
    )[:features]
    for i in range(8):
        chunk = small[128 + 16 * i : 128 + 16 * (i + 1), FEAT_PAD:].astype(F32)
        for g in range(3):
            gain_outs[g][i : i + 1, :] = chunk[g : g + 1]
    scores = small[:, :FEAT_PAD].astype(F32)
    part = jnp.sum(fold[...].astype(F32) * scores, axis=0, keepdims=True)
    rest_sum = [small[128 + 16 * i : 128 + 16 * (i + 1), FEAT_PAD:].astype(F32)[3:4] for i in range(3)]
    whole = (part + jnp.concatenate(rest_sum, axis=1))[:, :features]
    pixel_gain_out[...] = (whole / pixel_gain[...].reshape(1, features)).reshape(features)
    own = pl.ds(pl.multiple_of(row * block, block), block)
    own_rs = query_rs[0]
    for r in range(1, 4):
        own_rs = jnp.where(row == r, query_rs[r], own_rs)
    sums = jnp.zeros((block, 1), F32)
    alongs = jnp.zeros((block, 1), F32)
    for n in range(width // 256):
        cols = pl.ds(n * 256, 256)
        back[:, cols] = dot_nt(total[...], wq[cols, :])
        row_sum = jnp.sum(back[:, cols] * unit[:, cols], axis=0, keepdims=True)
        for i in range(2):
            gain_outs[3][2 * n + i : 2 * n + i + 1, :] = row_sum[:, i * LANES : (i + 1) * LANES]
        scaled = back[own, cols] * query_gain[:, cols]
        sums = sums + jnp.sum(scaled, axis=1, keepdims=True)
        alongs = alongs + jnp.sum(scaled * unit[own, cols], axis=1, keepdims=True)
    scaled = back[own, my_cols] * query_gain[:, my_cols]
    query_in = own_rs * (scaled - sums * (1.0 / width) - unit[own, my_cols] * (alongs * (1.0 / width)))
    init_out[...] = init_sum[...].astype(F32) + query_in
    for copy in outs:
        copy.wait()


def finish(y, latents, summed, small, init_sum, fold, init_all, wq, wk, wv, query_gain, pixel_gain):
    features, width = wk.shape
    lat = init_all.shape[0]
    block = lat // 4
    vmem = pl.BlockSpec(memory_space=pltpu.VMEM)
    hbm = pl.BlockSpec(memory_space=pl.ANY)

    def f32(*shape):
        return jax.ShapeDtypeStruct(shape, F32)

    outs = pl.pallas_call(
        finish_kernel,
        out_shape=[f32(features, 2 * y.shape[2], LANES), jax.ShapeDtypeStruct(latents.shape, BF), f32(block, LANES),
                   f32(features), f32(features, LANES), f32(features, LANES)]
        + [f32(width // LANES, LANES)] * 4 + [f32(width, LANES)] * (MATS + 2),
        in_specs=[hbm] * 10 + [vmem] * 2,
        out_specs=[hbm] * 2 + [vmem] * 8 + [hbm] * (MATS + 2),
        scratch_shapes=[
            pltpu.VMEM(shape, BF)
            for shape in (summed.shape, small.shape, fold.shape, init_all.shape,
                          wq.shape, wk.shape, wv.shape, init_sum.shape)
        ]
        + [
            pltpu.VMEM((lat, width), F32),
            pltpu.VMEM((lat, width), BF),
            pltpu.VMEM((lat, width), BF),
            pltpu.VMEM((MATS + 2, width, LANES), F32),
            pltpu.VMEM((LANES, width), BF),
            pltpu.VMEM((LANES, width), BF),
            pltpu.VMEM((features, 2 * y.shape[2], LANES), F32),
            pltpu.VMEM(latents.shape, BF),
            pltpu.VMEM((lat, width), F32),
            pltpu.SemaphoreType.DMA((11,)),
            pltpu.SemaphoreType.DMA((MATS + 4,)),
        ],
        compiler_params=pltpu.CompilerParams(vmem_limit_bytes=VMEM_LIMIT),
    )(y, latents, summed, small, fold, init_all, wq, wk, wv, init_sum, query_gain[None],
      pixel_gain)
    y, latents, init_grad, pixel_gain_grad, key_grad, value_grad = outs[:6]
    return (y, latents, init_grad, outs[6:10], pixel_gain_grad, key_grad, value_grad, outs[10:])


def whole_stack(shards, z, pixel_gain, pseg, init, cots, seg, wk, wv, gains, weights):
    width = init.shape[1]
    block = init.shape[0]
    count = 2 * block
    lat = 2 * count
    share = width // shards
    half = width // 2
    bits = shards.bit_length() - 1
    orders = unit_orders(bits)
    nslots = 3
    features = wk.shape[0]
    group = z.shape[0] // features
    slots = group * LANES // 4
    small, size = [], lat
    for i in range(bits + 2):
        size = size // 2 if size > 16 else size
        small.append((size, 512))
    scratch = [
        ((nslots, width, width), BF),
        (wk.shape, BF),
        ((LANES, width), BF),
        ((2, block, width), BF),
        ((2, 2, block, FEAT_PAD), BF),
        ((2, block, FEAT_PAD), BF),
        ((2, block, FEAT_PAD), BF),
        ((count, FEAT_PAD), BF),
        ((count, FEAT_PAD), BF),
        ((2, 2, 2, block, FEAT_PAD), BF),
        ((lat, width), F32),
        ((3, count, LANES), F32),
        ((6 * count, width), BF),
        ((6, count, half), BF),
        ((2, count, width), BF),
        ((count, width), BF),
        ((2, 2, count, width), BF),
        ((2, lat, slots), BF),
        ((count, width), BF),
        ((2, count, width), BF),
        ((MATS, 2, count, width), BF),
        ((count, width), BF),
        ((FEATURE_UNIT + 1, share, LANES), BF),
        ((2, 2, 2, block, FEAT_PAD), BF),
        ((lat, FEAT_PAD), F32),
        ((16, width), F32),
        ((1, lat), F32),
        ((lat, 512), BF),
        ((2, CAT, slots), BF),
        (((MAIN + 8) * group // 2, LANES), F32),
        ((2, 8, slots), F32),
        ((group, LANES), F32),
        ((MAIN + 8, LANES), F32),
        ((FEATURE_UNIT + 1, share, LANES), BF),
        ((UNITS * 2, width, LANES), BF),
    ]
    for order in orders:
        scratch += [(shape, BF) for shape in stage_shapes(order, width)]
    scratch += [(shape, BF) for shape in small]
    stages = sum(len(order) for order in orders)
    vmem = pl.BlockSpec(memory_space=pltpu.VMEM)
    hbm = pl.BlockSpec(memory_space=pl.ANY)
    return pl.pallas_call(
        functools.partial(
            main_kernel, (shards, width, count, dict(small_stages=len(small)))
        ),
        out_shape=[
            jax.ShapeDtypeStruct((2, block, width), BF),
            jax.ShapeDtypeStruct((lat, 512), BF),
            jax.ShapeDtypeStruct((4, FEATURE_UNIT + 1, share, LANES), BF),
            jax.ShapeDtypeStruct((share, LANES), BF),
            jax.ShapeDtypeStruct((lat, FEAT_PAD), BF),
            jax.ShapeDtypeStruct((4, block, width), BF),
            jax.ShapeDtypeStruct((2, features * group // 2, LANES), F32),
            jax.ShapeDtypeStruct((2, lat, slots), BF),
        ],
        in_specs=[hbm, pl.BlockSpec(memory_space=pltpu.SMEM), vmem, vmem, hbm, vmem]
        + [hbm] * 2 + [vmem] * 4 + [hbm] * 10,
        out_specs=[vmem, vmem, hbm, vmem, vmem, hbm, hbm, hbm],
        scratch_shapes=[pltpu.VMEM(shape, kind) for shape, kind in scratch]
        + [
            pltpu.SemaphoreType.DMA((nslots + 2 + 13,)),
            pltpu.SemaphoreType.DMA((-(-z.shape[0] // width),)),
            pltpu.SemaphoreType.DMA((stages,)),
            pltpu.SemaphoreType.DMA((stages,)),
            pltpu.SemaphoreType.DMA((80,)),
            pltpu.SemaphoreType.DMA((80,)),
        ],
        compiler_params=pltpu.CompilerParams(
            collective_id=0, has_side_effects=True, vmem_limit_bytes=VMEM_LIMIT
        ),
    )(z, pixel_gain, pseg, init, cots, seg, wk, wv, *[g[None] for g in gains], *weights)


VMEM_LIMIT = 63 * 1024 * 1024


def body(
    pixels, pixel_seg, latent_seg, latent_init, cotangent,
    pixel_gain, query_gain, query_weight, key_weight, value_weight, output_weight,
    mlp_gain, up_weight, down_weight,
    self_gain, self_query, self_key, self_value, self_output,
    second_gain, second_up, second_down,
):
    seqs, pix, features = pixels.shape
    block, width = latent_init.shape
    shards = lax.axis_size("seq")
    lat = block * lax.axis_size("row")
    row = lax.axis_index("row")
    cross_scale = 1.0 / math.sqrt(width)
    tiles = pix // LANES

    z = pixels.transpose(2, 0, 1).reshape(features, seqs, tiles, LANES)
    z = z.transpose(0, 2, 1, 3).reshape(features * seqs * tiles, LANES)
    latents, small, summed, init_sum, fold, init_all, y, unused = whole_stack(
        shards, z, pixel_gain, pixel_seg, latent_init, cotangent, latent_seg, key_weight, value_weight,
        (mlp_gain, self_gain, second_gain, query_gain),
        (query_weight, output_weight, up_weight, down_weight, self_query, self_key, self_value,
         self_output, second_up, second_down),
    )
    init_all = init_all.reshape(lat, width)
    y = y.reshape(2, features, tiles, LANES)
    if width // shards == LANES:
        y, latents, init_grad, gains, pixel_gain_grad, key_grad, value_grad, mats = finish(
            y, latents, summed, small, init_sum, fold, init_all, query_weight, key_weight,
            value_weight, query_gain, pixel_gain,
        )
    else:
        y = y.transpose(1, 0, 2, 3)
    pixel_grad = y.reshape(features, tiles, seqs, LANES).transpose(2, 1, 3, 0)
    pixel_grad = pixel_grad.reshape(seqs, pix, features)
    if width // shards == LANES:
        mlp_gain_grad, self_gain_grad, second_gain_grad, query_gain_grad = [
            g.reshape(width) for g in gains
        ]
        return (
            latents, pixel_grad, init_grad, pixel_gain_grad,
            query_gain_grad, mlp_gain_grad, self_gain_grad, second_gain_grad,
            mats[MATS], key_grad, value_grad, mats[MATS + 1], mats[UP1], mats[DOWN1],
            mats[SQ], mats[SK], mats[SV], mats[SOUT], mats[UP2], mats[DOWN2],
        )

    share = width // shards
    at = lax.axis_index("seq") * share

    def columns(arr):
        return lax.dynamic_slice_in_dim(arr, at, share, arr.ndim - 1)

    score_b = small[:, :features]
    side = small[:, FEAT_PAD:]
    rests = side[:128].reshape(8, 2, 8, LANES).transpose(1, 2, 0, 3).reshape(2, 8, width)
    sums = side[128:256].reshape(8, 16, LANES).transpose(1, 0, 2).reshape(16, width).astype(F32)
    pixel_gain_grad = (
        jnp.sum(fold[:, :features].astype(F32) * score_b.astype(F32), axis=0) + sums[3, :features]
    ) / pixel_gain
    units = summed.reshape(2, 2, FEATURE_UNIT + 1, share, LANES)
    mats = units[:, :, :FEATURE_UNIT].reshape(2, 2, MATS, 2, share, LANES)
    mats = mats.transpose(2, 1, 0, 3, 5, 4).reshape(MATS, width, share).astype(F32)
    outer = units[:, :, FEATURE_UNIT].transpose(1, 0, 3, 2).reshape(2, MAIN, share)
    outer = jnp.concatenate([outer, columns(rests)[:, : features - MAIN]], axis=1)
    value_grad = outer[1].astype(F32)
    output_grad = dot_tn(value_weight, outer[0])
    query_unit, query_rs = norm_parts(init_all.astype(F32))
    query_normed = (query_unit * query_gain).astype(BF)
    my_queries = dot(query_normed, columns(query_weight)).astype(BF)
    key_grad = dot_tn(score_b, my_queries) * cross_scale
    query_total = (dot(score_b, key_weight) * cross_scale).astype(BF)
    query_grad = dot_tn(query_normed, columns(query_total))
    query_in, query_gain_grad = norm_back(
        query_unit, query_rs, query_gain, dot_nt(query_total, query_weight)
    )
    init_grad = init_sum.T.astype(F32) + lax.dynamic_slice(query_in, (row * block, at), (block, share))
    return (
        latents, pixel_grad, init_grad,
        pixel_gain_grad, query_gain_grad, sums[0], sums[1], sums[2],
        query_grad, key_grad, value_grad, output_grad, mats[UP1], mats[DOWN1],
        mats[SQ], mats[SK], mats[SV], mats[SOUT], mats[UP2], mats[DOWN2],
    )


def solution(mesh):
    placed = (
        P("seq", "row", None), P("seq", "row"), P("seq", "row"), P("row", None),
        P("seq", "row", None),
    ) + (P(),) * 17
    cols = P(None, "seq")
    return jax.shard_map(
        body,
        mesh=mesh,
        in_specs=placed,
        out_specs=(P("seq", "row", None), P("seq", "row", None), P("row", "seq"))
        + (P(),) * 5 + (cols,) * 12,
        check_vma=False,
    )
```

```python
import functools
import math

import jax
import jax.numpy as jnp
from jax import lax
from jax.experimental import pallas as pl
from jax.experimental.pallas import tpu as pltpu
from jax.sharding import PartitionSpec as P

HEADS = 8
EPSILON = 1e-05
NEGATIVE = -1e9
BF = jnp.bfloat16
F32 = jnp.float32
LANES = 128
FEAT_PAD = 384
MAIN = 256
CAT = 2 * MAIN + LANES
MESH = pl.DeviceIdType.MESH


def dot(a, b):
    return jnp.dot(a, b, preferred_element_type=F32)


def dot_tn(a, b):
    return lax.dot_general(a, b, (((0,), (0,)), ((), ())), preferred_element_type=F32)


def dot_nt(a, b):
    return lax.dot_general(a, b, (((1,), (1,)), ((), ())), preferred_element_type=F32)


def fill_rest(rest, matrix):
    rest[...] = jnp.zeros(rest.shape, rest.dtype)
    rest[: matrix.shape[0] - MAIN, :] = matrix[MAIN:, :]


def norm_parts(values):
    centre = values - jnp.mean(values, axis=-1, keepdims=True)
    rs = lax.rsqrt(jnp.mean(centre * centre, axis=-1, keepdims=True) + EPSILON)
    return centre * rs, rs


def norm_back(unit, rs, gain, upstream):
    scaled = upstream * gain
    grad = rs * (
        scaled
        - jnp.mean(scaled, axis=-1, keepdims=True)
        - unit * jnp.mean(scaled * unit, axis=-1, keepdims=True)
    )
    return grad, jnp.sum(upstream * unit, axis=0)


def gelu_parts(hidden):
    cdf = 0.5 * (1.0 + lax.erf(hidden * math.sqrt(0.5)))
    pdf = jnp.exp(-0.5 * hidden * hidden) * (1.0 / math.sqrt(2.0 * math.pi))
    return hidden * cdf, cdf + hidden * pdf


NORMED1, ACTIVE1, SELFN, MIXED, NORMED2, ACTIVE2 = range(6)
DOWN2, UP2, SOUT, SQ, SK, SV, DOWN1, UP1 = range(8)
LEFT = {
    DOWN2: ACTIVE2, UP2: NORMED2, SOUT: MIXED, SQ: SELFN, SK: SELFN, SV: SELFN,
    DOWN1: ACTIVE1, UP1: NORMED1,
}
MATS = 8
FEATURE_UNIT = 2 * MATS
INIT_UNIT = FEATURE_UNIT + 1
UNITS = INIT_UNIT + 1


class Remote:
    def __init__(self, log, src, dst, send_sem, recv_sem, device):
        self.copy = pltpu.make_async_remote_copy(
            src_ref=src, dst_ref=dst, send_sem=send_sem, recv_sem=recv_sem,
            device_id=device, device_id_type=MESH,
        )
        self.copy.start()
        self.arrived = self.sent = False
        log.append(self)

    def wait_recv(self):
        if not self.arrived:
            self.copy.wait_recv()
        self.arrived = True

    def wait_send(self):
        if not self.sent:
            self.copy.wait_send()
        self.sent = True

    def finish(self):
        self.wait_recv()
        self.wait_send()


KINDS = "FCDFBCAEBACCBBAABA"


def unit_orders(bits):
    first, second, tail = [0], list(range(1, min(bits, 2))), list(range(2, bits))
    kinds = {
        "A": ["y"] + first + second + tail,
        "B": first + second + ["y"] + tail,
        "C": second + first + ["y"] + tail,
        "D": first + ["y"] + second + tail,
        "E": second + ["y"] + first + tail,
        "F": ["y"] + second + first + tail,
    }
    return [kinds[letter] for letter in KINDS]


def stage_shapes(order, width):
    shapes, planes, size = [], 2, width
    for axis in order:
        if axis == "y":
            planes = 1
            shapes.append((size, LANES))
        else:
            size //= 2
            shapes.append((2, size, LANES) if planes == 2 else (size, LANES))
    return shapes


def main_kernel(cfg, *refs):
    shards, width, count, sizes = cfg
    bits = shards.bit_length() - 1
    share = width // shards
    half = width // 2
    block = count // 2
    lat = 2 * count
    head_width = width // HEADS
    cross_scale = 1.0 / math.sqrt(width)
    self_scale = 1.0 / math.sqrt(head_width)
    orders = unit_orders(bits)
    it = iter(refs)

    def take(n=None):
        return next(it) if n is None else [next(it) for _ in range(n)]

    (z_hbm, pixel_gain, pseg_ref, init_ref, cot_hbm, seg_ref, wk_hbm, wv_hbm) = take(8)
    gain_refs = take(4)
    w_hbm = take(10)
    (lat_ref, sm_out, gat_ref, initg_ref, fold, zall, y_ref, pspill) = take(8)
    (wslots, wkv, w_rest, zbuf, ain1, asum, ain2, amix, amix_in, amat, fbuf, rsb, acts, acts_in, slopes,
     qbuf, kv, pbuf, dmix, dkv_in, gall, gcd_in, fin, da_all, bsum, gsum, idrow,
     sm, xcat, flat, rest0, pixel_rs, gain_col, fin_in, part) = take(35)
    recv = [take(len(orders[u])) for u in range(UNITS)]
    smr = take(sizes["small_stages"])
    (wsem, zsem, usend, urecv, csend, crecv) = take(6)

    j = lax.axis_index("seq")
    row = lax.axis_index("row")
    core, chip = row % 2, row // 2
    peer = {"row": row + 1 - 2 * core}
    across = {"row": row + 2 - 4 * chip}
    diagonal = {"row": 3 - row}
    bit_of = [(j // (1 << b)) % 2 for b in range(bits)]
    partner = {b: {"seq": j + (1 - 2 * bit_of[b]) * (1 << b)} for b in range(bits)}
    partner["y"] = across
    stream = fbuf.at[pl.ds(0, count)]
    upstr = fbuf.at[pl.ds(count, count)]
    dnorm = stream

    def act(k):
        return pl.ds(k * count, count)

    WQ, WO, UP, DOWN, QW, KW, VW, SO, UPB, DOWNB = range(10)
    uses = [WQ, WO, UP, DOWN, KW, VW, QW, SO, UPB, DOWNB, DOWNB, UPB, SO, QW, KW, VW, DOWN, UP, WO]
    nslots = wslots.shape[0]
    at_use = [0]

    def weight_copy(i):
        return pltpu.make_async_copy(w_hbm[uses[i]], wslots.at[i % nslots], wsem.at[i % nslots])

    def weight(expect):
        i = at_use[0]
        assert uses[i] == expect
        at_use[0] += 1
        weight_copy(i).wait()
        return wslots.at[i % nslots]

    def weight_done():
        i = at_use[0] - 1 + nslots
        if i < len(uses):
            weight_copy(i).start()

    features = wk_hbm.shape[0]
    pixel_copies = []
    for i, lo in enumerate(range(0, z_hbm.shape[0], width)):
        rows = min(width, z_hbm.shape[0] - lo)
        pixel_copies.append(pltpu.make_async_copy(
            z_hbm.at[pl.ds(lo, rows)], part.at[i, pl.ds(0, rows)], zsem.at[i]
        ))
    weight_copy(0).start()
    wk_copy = pltpu.make_async_copy(wk_hbm, wkv, wsem.at[nslots])
    wk_copy.start()
    for i in range(1, nslots):
        weight_copy(i).start()
    wv_copy = pltpu.make_async_copy(wv_hbm, wkv, wsem.at[nslots + 1])
    for copy in pixel_copies:
        copy.start()

    barrier = pltpu.get_barrier_semaphore()
    partners = [peer, across, diagonal] + [partner[b] for b in range(bits)]
    for p in partners:
        pl.semaphore_signal(barrier, inc=1, device_id=p, device_id_type=MESH)
    copies = []
    slot_count = [0]

    def remote(src, dst, device):
        slot = slot_count[0]
        slot_count[0] += 1
        return Remote(copies, src, dst, csend.at[slot], crecv.at[slot], device)

    def local(src, dst, slot):
        copy = pltpu.make_async_copy(src, dst, wsem.at[nslots + 2 + slot])
        copy.start()
        return copy

    def rows_loop(body, step=64, total=None):
        def run(i, carry):
            body(pl.ds(pl.multiple_of(i * step, step), step))
            return carry
        lax.fori_loop(0, (total or count) // step, run, 0, unroll=2)

    def columns_loop(body, step=256, total=width):
        def run(i, carry):
            body(pl.ds(pl.multiple_of(i * step, step), step))
            return carry
        lax.fori_loop(0, total // step, run, 0, unroll=2)

    def layer(k, into):
        def body(rows):
            unit, rs = norm_parts(stream[rows, :])
            rsb[k, rows, :] = jnp.broadcast_to(rs, (rs.shape[0], LANES))
            place = pl.ds(pl.multiple_of(into * count + rows.start, rows.size), rows.size)
            acts[place, :] = (unit * gain_refs[k][...]).astype(BF)
        rows_loop(body)

    def layer_back(k, normed, into, start=None):
        gain = gain_refs[k][...]
        inverse = 1.0 / gain

        def body(i, total):
            rows = pl.ds(pl.multiple_of(i * 64, 64), 64)
            place = pl.ds(pl.multiple_of(normed * count + i * 64, 64), 64)
            dn = dnorm[rows, :]
            unit = acts[place, :].astype(F32) * inverse
            scaled = dn * gain
            rs = rsb[k, rows, :][:, :1]
            mean = jnp.mean(scaled, axis=-1, keepdims=True)
            along = jnp.mean(scaled * unit, axis=-1, keepdims=True)
            before = upstr[rows, :] if start is None else gall[start, 0, rows, :].astype(F32)
            after = before + rs * (scaled - mean - unit * along)
            upstr[rows, :] = after
            gall[into, 0, rows, :] = after.astype(BF)
            return total + jnp.sum(dn * unit, axis=0, keepdims=True)
        gsum[pl.ds(k, 1), :] = lax.fori_loop(
            0, count // 64, body, jnp.zeros((1, width), F32), unroll=2
        )

    act_copies, grad_copies = {}, {}

    def share_act(k):
        away = pl.ds(pl.multiple_of((1 - core) * half, half), half)
        act_copies[k] = remote(acts.at[act(k), away], acts_in.at[k], peer)

    def share_grad(m):
        grad_copies[m] = remote(gall.at[m, 0], gall.at[m, 1], peer)

    clock = [0.0]
    small = dict(lo=0, size=lat, stage=0, up=[], copy=None, due=1e9)
    axes = [(core, peer), (chip, across)] + [(bit_of[b], partner[b]) for b in range(bits)]

    def small_send():
        bit, device = axes[small["stage"]]
        size = small["size"]
        if size > 16:
            size //= 2
            away = pl.multiple_of(small["lo"] + (1 - bit) * size, 16)
            keep = pl.multiple_of(small["lo"] + bit * size, 16)
            small["up"].append((device, keep, size))
            small["lo"], small["size"] = keep, size
        else:
            away = small["lo"]
        small["copy"] = remote(sm.at[pl.ds(away, size)], smr[small["stage"]], device)
        small["due"] = clock[0] + 2.5 + size * 512 * 4 / 75e3

    def small_grow():
        device, lo, size = small["up"].pop()
        rows = pl.ds(lo, size)
        small["copy"] = remote(sm_out.at[rows], sm_out.at[rows], device)
        small["due"] = clock[0] + 2.5 + size * 512 * 4 / 75e3

    def small_step():
        copy, size = small["copy"], small["size"]
        copy.wait_recv()
        if small["stage"] < len(axes):
            copy.wait_send()
            rows = pl.ds(small["lo"], size)
            sm[rows, :] = sm[rows, :] + smr[small["stage"]][...]
            small["stage"] += 1
            if small["stage"] < len(axes):
                small_send()
                return
            sm_out[rows, :] = sm[rows, :]
        if small["up"]:
            small_grow()
        else:
            small["due"] = 1e9

    state = {}
    free = {}
    pending = []

    def region(u, planes, lo, size):
        if planes == 2:
            return part.at[pl.ds(2 * u, 2), pl.ds(lo, size)]
        return part.at[2 * u + chip, pl.ds(lo, size)]

    def send_stage(u):
        s = state[u]
        axis = orders[u][s["stage"]]
        k = s["stage"]
        if axis == "y":
            src = part.at[2 * u + 1 - chip, pl.ds(s["lo"], s["size"])]
            s["planes"] = 1
        else:
            size = s["size"] // 2
            keep = s["lo"] + bit_of[axis] * size
            away = s["lo"] + (1 - bit_of[axis]) * size
            src = region(u, s["planes"], pl.multiple_of(away, share), size)
            s["lo"], s["size"] = pl.multiple_of(keep, share), size
        slot = sum(len(orders[v]) for v in range(u)) + k
        s["copy"] = Remote(copies, src, recv[u][k], usend.at[slot], urecv.at[slot], partner[axis])
        took = s["size"] * s["planes"] * LANES * 2 * 2 / 80e3
        links = {"y": {"y": 1}, 0: {"x": 1}, 1: {"inner": 1}}.get(axis, {"inner": 1, "middle": 2})
        begin = max([clock[0]] + [free.get(link, 0.0) for link in links])
        for link, share_of in links.items():
            free[link] = begin + took * share_of
        s["due"] = max(free[link] for link in links) + 4.0
        pending.append(u)

    def finish_stage(u):
        s = state[u]
        k = s["stage"]
        s["copy"].wait_recv()
        last = k == len(orders[u]) - 1
        if last:
            total = part[pl.ds(2 * u + chip, 1), pl.ds(s["lo"], s["size"])][0] + recv[u][k][...]
            if u == INIT_UNIT:
                initg_ref[...] = total
            else:
                fin[u] = total
            s["done"] = True
            done_units.append(u)
            gather_ready()
            return
        step = min(s["size"], 256)
        for p in range(s["planes"]):
            def add(i, carry):
                off = pl.multiple_of(i * step, step)
                mine = pl.ds(pl.multiple_of(s["lo"] + off, share), step)
                if s["planes"] == 2:
                    got = recv[u][k][p, pl.ds(off, step), :]
                    part[2 * u + p, mine, :] = part[2 * u + p, mine, :] + got
                else:
                    got = recv[u][k][pl.ds(off, step), :]
                    at = pl.ds(2 * u + chip, 1)
                    part[at, mine, :] = part[at, mine, :] + got[None]
                return carry
            lax.fori_loop(0, s["size"] // step, add, 0)
        s["stage"] += 1
        send_stage(u)

    done_units, gathers = [], []
    groups = [list(range(0, 6)), list(range(6, 12)), list(range(12, FEATURE_UNIT + 1))]

    def gather_ready():
        while len(gathers) < len(groups) and all(u in done_units for u in groups[len(gathers)]):
            g = groups[len(gathers)]
            span = pl.ds(g[0], len(g))
            from_chip = remote(fin.at[span], fin_in.at[span], across)
            remote(fin.at[span], gat_ref.at[row, span], peer)
            gathers.append((g, from_chip, local(fin.at[span], gat_ref.at[row, span], len(gathers))))

    def serve():
        at = min((state[u]["due"], u) for u in pending) if pending else (1e9, None)
        if small["due"] <= at[0]:
            clock[0] = max(clock[0], small["due"])
            small_step()
        else:
            clock[0] = max(clock[0], at[0]) + 0.3
            pending.remove(at[1])
            finish_stage(at[1])

    def next_due():
        return min([small["due"]] + [state[u]["due"] for u in pending])

    def tick(us):
        clock[0] += 1.6 * us
        while next_due() <= clock[0]:
            serve()

    def begin_unit(u):
        state[u] = dict(stage=0, planes=2, lo=0, size=width, done=False)
        send_stage(u)

    def position(u, block):
        seq_bits = [a for a in orders[u] if a != "y"]
        pos = 0
        for at, b in enumerate(seq_bits):
            pos = pos + ((block // (1 << b)) % 2) * (1 << (bits - 1 - at))
        return pos

    def store_plane(u, plane, value):
        if share != LANES:
            value = value.astype(F32).T.astype(BF)
        for block_at in range(shards):
            place = pl.ds(position(u, block_at) * share, share)
            if share == LANES:
                part[pl.ds(2 * u + plane, 1), place, :] = value[:, block_at * share : (block_at + 1) * share][None]
            else:
                part[pl.ds(2 * u + plane, 1), place, :] = value[block_at * share : (block_at + 1) * share][None]

    def weight_grad(m):
        left = LEFT[m]
        act_copies[left].wait_recv()
        grad_copies[m].wait_recv()

        def run(plane, carry):
            own = pl.ds(pl.multiple_of(core * half + plane * MAIN, MAIN), MAIN)
            theirs = pl.ds(pl.multiple_of(plane * MAIN, MAIN), MAIN)
            lefts = jnp.concatenate([acts[act(left), own], acts_in[left, :, theirs]], axis=0)
            total = dot_tn(lefts, gall[m].reshape(2 * count, width)).astype(BF)
            store_plane(2 * m, plane, total[:LANES])
            store_plane(2 * m + 1, plane, total[LANES:])
            return carry
        lax.fori_loop(0, 2, run, 0)
        begin_unit(2 * m)
        begin_unit(2 * m + 1)

    cot_rows = pl.ds(pl.multiple_of(chip * block, block), block)
    c_own = local(cot_hbm.at[chip], gall.at[DOWN2, 0, cot_rows], 3)
    zbuf[pl.ds(chip, 1)] = init_ref[...][None]
    unit, unused = norm_parts(init_ref[...].astype(F32))
    own_normed = (unit * gain_refs[3][...]).astype(BF)
    w = weight(WQ)
    queries = dot(own_normed, w[...]).astype(BF)
    weight_done()
    wk_copy.wait()
    fill_rest(w_rest, wkv)
    fold_main = dot_nt(queries, wkv[:MAIN, :]) * cross_scale
    fold_rest = dot_nt(queries, w_rest[...]) * cross_scale
    own_rows = pl.ds(pl.multiple_of(row * block, block), block)
    seg = seg_ref[...].astype(F32)
    ids = jnp.concatenate([seg, jnp.zeros((LANES - 2, block), F32)], axis=0).T
    ids = pltpu.roll(ids, 5, 1)
    fold[own_rows, :MAIN] = fold_main.astype(BF)
    fold[own_rows, MAIN:] = (fold_rest + ids).astype(BF)
    wv_copy.start()
    pl.semaphore_wait(barrier, len(partners))
    fold_copies = [remote(fold.at[own_rows], fold.at[own_rows], p) for p in (across, diagonal, peer)]
    z_copy = remote(init_ref, zbuf.at[chip], across)
    c_copy = remote(cot_hbm.at[1 - chip], gall.at[DOWN2, 0, cot_rows], across)
    group = pixel_rs.shape[0]
    blocks = group // 4
    tall = gain_col.shape[0]

    fold_in = width // group

    def pixel_row(f, lo=0, rows=group):
        at = pl.ds(pl.multiple_of((f % fold_in) * group + lo, rows), rows)
        return part[pl.ds(f // fold_in, 1), at, :][0].astype(F32)

    zero = jnp.zeros((group, LANES), F32)
    for copy in pixel_copies:
        copy.wait()
    mean = lax.fori_loop(0, features, lambda f, acc: acc + pixel_row(f), zero, unroll=9)
    mean = mean * (1.0 / features)

    def spread(f, acc):
        centre = pixel_row(f) - mean
        return acc + centre * centre
    spread_sum = lax.fori_loop(0, features, spread, zero, unroll=9)
    rs_all = lax.rsqrt(spread_sum * (1.0 / features) + EPSILON)
    pixel_rs[...] = rs_all
    gain_col[...] = jnp.ones(gain_col.shape, F32)
    flat[features * group // 2 :, :] = jnp.zeros(((tall - features) * group // 2, LANES), F32)
    for s in range(2):
        xcat[s, 2 * MAIN + 16 :, :] = jnp.zeros((LANES - 16, xcat.shape[2]), BF)
    for k in range(2):
        half_rows = slice(k * (group // 2), (k + 1) * (group // 2))
        half_mean, half_rs = mean[half_rows], rs_all[half_rows]

        def scale(f, carry, k=k, half_mean=half_mean, half_rs=half_rs):
            value = pixel_row(f, k * (group // 2), group // 2)
            rows = pl.ds(pl.multiple_of(f * (group // 2), group // 2), group // 2)
            flat[rows, :] = (value - half_mean) * (half_rs * pixel_gain[f])
            if k == 0:
                gain_col[pl.ds(f, 1), :] = jnp.full((1, LANES), pixel_gain[f], F32)
            return carry
        lax.fori_loop(0, features, scale, 0, unroll=9)
        for s in range(2):
            for jb in range(blocks):
                cols = pl.ds(jb * LANES, LANES)
                value = flat[pl.ds(2 * jb + s, tall, stride=group // 2), :]
                xcat[s, k * MAIN : (k + 1) * MAIN, cols] = value[:MAIN].astype(BF)
                if k == 0:
                    rest0[s, :, cols] = value[MAIN:]
                else:
                    both = jnp.concatenate([rest0[s, :, cols], value[MAIN:]], axis=0)
                    xcat[s, 2 * MAIN : 2 * MAIN + 16, cols] = both.astype(BF)
    for copy in fold_copies:
        copy.wait_recv()

    lane = lax.broadcasted_iota(jnp.int32, (1, LANES), 1)
    image = (2 * row).astype(F32)

    def selectors(s, rows):
        ids = fold[rows, MAIN:].astype(F32)
        ids = jnp.where(s == 0, ids[:, 5:6], ids[:, 6:7])
        return jnp.where(ids == image, 1.0, 0.0), jnp.where(ids == image + 1.0, 1.0, 0.0)

    def spread_out(source, s, rows):
        first, second = selectors(s, rows)
        main = source[:, :MAIN].astype(F32)
        rest = jnp.where(lane < 5, source[:, MAIN:].astype(F32), 0.0)
        rest = rest * first + pltpu.roll(rest, 8, 1) * second
        return jnp.concatenate([main * first, main * second, rest], axis=1).astype(BF)

    def pull_in(s, rows, zero, one, rest):
        first, second = selectors(s, rows)
        rest = jnp.where(lane < 5, rest * first + pltpu.roll(rest, LANES - 8, 1) * second, 0.0)
        return zero * first + one * second, rest

    slots = xcat.shape[2]
    core_copies = []

    def send_core(turn):
        core_copies.append(remote(amat.at[turn, :, 1 - core], ain1.at[turn], peer))

    def core_sum(turn):
        core_copies[turn].wait_recv()
        return amat[turn, :, pl.ds(core, 1)][:, 0] + ain1[turn]

    for turn in range(2):
        s = 1 - chip if turn == 0 else chip
        seq = pl.ds(s, 1)
        for i in range(4):
            rows = pl.ds(i * block, block)
            gall[2 + 2 * turn + i // 2, 0, (i % 2) * block : (i % 2 + 1) * block, :CAT] = spread_out(
                fold[rows, :], s, rows
            )
        first_ok = jnp.where(pseg_ref[seq, :slots] == 2 * row, 1.0, 0.0)
        second_ok = jnp.where(pseg_ref[seq, slots:] == 2 * row + 1, 1.0, 0.0)

        def score_cols(cols, seq=seq, turn=turn):
            queries_cat = jnp.concatenate(
                [gall[2 + 2 * turn, 0, :, :CAT], gall[3 + 2 * turn, 0, :, :CAT]], axis=0
            )
            fbuf[:, cols] = dot(queries_cat, xcat[seq, :, cols][0])
        columns_loop(score_cols, 256, slots)
        if turn == 1:
            asum[...] = core_sum(0)
            step2 = remote(asum, ain2, across)

        def soften(rows, s=s, seq=seq, first_ok=first_ok, second_ok=second_ok):
            first, unused = selectors(s, rows)
            allowed = second_ok + first * (first_ok - second_ok)
            scores = jnp.where(allowed > 0.5, fbuf[rows, :], NEGATIVE)
            weights = jnp.exp(scores - jnp.max(scores, axis=1, keepdims=True))
            prob = (weights * (1.0 / jnp.sum(weights, axis=1, keepdims=True))).astype(BF)
            pbuf[seq, rows, :] = prob[None]
        rows_loop(soften, 64, lat)
        probs = pbuf[seq][0]
        zero = dot_nt(probs, xcat[seq, :MAIN, :][0])
        one = dot_nt(probs, xcat[seq, MAIN : 2 * MAIN, :][0])
        rest = dot_nt(probs, xcat[seq, 2 * MAIN :, :][0])
        main, rest = pull_in(s, pl.ds(0, lat), zero, one, rest)
        amat[turn, :, :, :, :MAIN] = main.astype(BF).reshape(2, 2, block, MAIN)
        amat[turn, :, :, :, MAIN:] = rest.astype(BF).reshape(2, 2, block, LANES)
        send_core(turn)
    spill = local(pbuf, pspill, 4)

    for at in range(4):
        who = core if at < 2 else 1 - core
        rows = pl.ds(pl.multiple_of((2 * (at % 2) + who) * block, block), block)
        turned = fold[rows, MAIN:].astype(F32).T
        idrow[:, at * block : (at + 1) * block] = jnp.where(chip == 0, turned[5:6], turned[6:7])
    own_ids = []
    for h in range(2):
        rows = pl.ds(pl.multiple_of((2 * h + core) * block, block), block)
        ids = fold[rows, MAIN:].astype(F32)
        own_ids.append(jnp.where(chip == 0, ids[:, 5:6], ids[:, 6:7]))
    idcol = jnp.concatenate(own_ids, axis=0)
    z_copy.wait_recv()
    remote(init_ref, zall.at[row], peer)
    other_row = row + 2 - 4 * chip
    remote(zbuf.at[1 - chip], zall.at[other_row], peer)
    z_local = [local(init_ref, zall.at[row], 5), local(zbuf.at[1 - chip], zall.at[other_row], 6)]
    c_copy.wait_recv()
    c_own.wait()
    share_grad(DOWN2)
    wv_copy.wait()
    fill_rest(w_rest, wkv)
    step2.wait_recv()
    amix[...] = (core_sum(1) + ain2[...]).reshape(count, FEAT_PAD)
    amix_copy = remote(amix, amix_in, peer)

    def attended_cols(cols):
        value = dot(amix[:, :MAIN], wkv[:MAIN, cols]) + dot(amix[:, MAIN:], w_rest[:, cols])
        qbuf[:, cols] = value.astype(BF)
    columns_loop(attended_cols)
    w = weight(WO)

    def one_cols(cols):
        start = zbuf[:, :, cols].reshape(count, cols.size).astype(F32)
        stream[:, cols] = start + dot(qbuf[...], w[:, cols])
    columns_loop(one_cols)
    weight_done()

    def mlp(k, normed, active, up_id, down_id):
        layer(k, normed)
        share_act(normed)
        w_up = weight(up_id)

        def up_cols(cols):
            value, slope = gelu_parts(dot(acts[act(normed), :], w_up[:, cols]))
            acts[act(active), cols] = value.astype(BF)
            slopes[active // 4, :, cols] = slope.astype(BF)
        columns_loop(up_cols)
        weight_done()
        share_act(active)
        w_down = weight(down_id)

        def down_cols(cols):
            stream[:, cols] += dot(acts[act(active), :], w_down[:, cols])
        columns_loop(down_cols)
        weight_done()

    mlp(0, NORMED1, ACTIVE1, UP, DOWN)
    layer(1, SELFN)
    share_act(SELFN)
    kv_copies = {}
    for index, dst in ((KW, 0), (VW, 1), (QW, None)):
        w_now = weight(index)

        def project(cols, dst=dst, w_now=w_now):
            value = dot(acts[act(SELFN), :], w_now[:, cols]).astype(BF)
            if dst is None:
                qbuf[:, cols] = value
            else:
                kv[dst, 0, :, cols] = value
        columns_loop(project)
        weight_done()
        if dst is not None:
            kv_copies[dst] = remote(kv.at[dst, 0], kv.at[dst, 1], peer)
    spill.wait()
    kv_copies[0].wait_recv()
    kv_copies[1].wait_recv()

    def heads(body):
        def run(pair, carry):
            for side in range(2):
                cols = pl.ds(pl.multiple_of((2 * pair + side) * head_width, head_width), head_width)
                rows = pl.ds(pl.multiple_of((pair % 2) * count, count), count)
                body(cols, (pl.ds(pair // 2, 1), rows, pl.ds(side * lat, lat)))
            return carry
        lax.fori_loop(0, HEADS // 2, run, 0)

    def attend(cols, keep):
        keys = kv[0, :, :, cols].reshape(lat, head_width)
        values = kv[1, :, :, cols].reshape(lat, head_width)
        scores = dot_nt(qbuf[:, cols], keys) * self_scale
        scores = jnp.where(idcol == idrow[...], scores, NEGATIVE)
        weights = jnp.exp(scores - jnp.max(scores, axis=1, keepdims=True))
        prob = (weights * (1.0 / jnp.sum(weights, axis=1, keepdims=True))).astype(BF)
        pbuf[keep] = prob[None]
        acts[act(MIXED), cols] = dot(prob, values).astype(BF)
    heads(attend)
    share_act(MIXED)
    w_so = weight(SO)

    def three_cols(cols):
        stream[:, cols] += dot(acts[act(MIXED), :], w_so[:, cols])
    columns_loop(three_cols)
    weight_done()
    mlp(2, NORMED2, ACTIVE2, UPB, DOWNB)
    dmix[...] = stream[...].astype(BF)
    lat_ref[pl.ds(chip, 1)] = dmix[pl.ds(pl.multiple_of(chip * block, block), block), :][None]
    lat_copy = remote(
        dmix.at[pl.ds(pl.multiple_of((1 - chip) * block, block), block)], lat_ref.at[chip], across
    )

    weight_grad(DOWN2)
    tick(2.0)

    def mlp_back(k, normed, active, m_down, m_up, up_id, down_id, into, start=None):
        w_down = weight(down_id)

        def act_cols(cols):
            grad = dot_nt(gall[m_down, 0], w_down[cols, :]).astype(BF).astype(F32)
            gall[m_up, 0, :, cols] = (grad * slopes[active // 4, :, cols].astype(F32)).astype(BF)
        columns_loop(act_cols)
        weight_done()
        share_grad(m_up)
        tick(1.0)
        w_up = weight(up_id)

        def norm_cols(cols):
            dnorm[:, cols] = dot_nt(gall[m_up, 0], w_up[cols, :])
        columns_loop(norm_cols)
        weight_done()
        if into == 0:
            grad_copies[DOWN2].wait_send()
            grad_copies[UP2].wait_send()
        layer_back(k, normed, into, start)
        tick(1.5)

    mlp_back(2, NORMED2, ACTIVE2, DOWN2, UP2, UPB, DOWNB, SOUT, DOWN2)

    share_grad(SOUT)
    weight_grad(UP2)
    tick(1.5)
    w_so2 = weight(SO)
    lat_copy.wait_send()

    def mixed_cols(cols):
        dmix[:, cols] = dot_nt(gall[SOUT, 0], w_so2[cols, :]).astype(BF)
    columns_loop(mixed_cols)
    weight_done()

    def attend_back(cols, keep):
        keys = kv[0, :, :, cols].reshape(lat, head_width)
        values = kv[1, :, :, cols].reshape(lat, head_width)
        dm = dmix[:, cols]
        prob_b = pbuf[keep][0]
        prob = prob_b.astype(F32)
        grad = dot_nt(dm, values)
        delta = jnp.sum(prob * grad, axis=1, keepdims=True)
        score = (prob * (grad - delta)).astype(BF)
        gall[SQ, 0, :, cols] = (dot(score, keys) * self_scale).astype(BF)
        dk = (dot_tn(score, qbuf[:, cols]) * self_scale).astype(BF)
        dv = dot_tn(prob_b, dm).astype(BF)
        gall[SK, 0, :, cols] = dk[:count]
        gall[SV, 0, :, cols] = dv[:count]
        kv[0, 1, :, cols] = dk[count:]
        kv[1, 1, :, cols] = dv[count:]
    weight_grad(SOUT)
    tick(1.0)
    heads(attend_back)
    unspill = local(pspill, pbuf, 4)
    share_dkv = remote(kv.at[:, 1], dkv_in, peer)
    share_grad(SQ)
    tick(4.0)
    share_dkv.wait_recv()

    def add_kv(rows):
        for at, m in ((0, SK), (1, SV)):
            gall[m, 0, rows, :] = gall[m, 0, rows, :] + dkv_in[at, rows, :]
    rows_loop(add_kv)
    share_grad(SK)
    share_grad(SV)
    for at, (m, index) in enumerate(((SQ, QW), (SK, KW), (SV, VW))):
        w_now = weight(index)

        def normed_cols(cols, at=at, m=m, w_now=w_now):
            value = dot_nt(gall[m, 0], w_now[cols, :])
            if at == 0:
                dnorm[:, cols] = value
            else:
                dnorm[:, cols] += value
        columns_loop(normed_cols)
        weight_done()
    layer_back(1, SELFN, DOWN1)
    share_grad(DOWN1)
    tick(3.0)
    weight_grad(SQ)
    tick(1.0)
    weight_grad(SK)
    tick(1.0)
    mlp_back(0, NORMED1, ACTIVE1, DOWN1, UP1, UP, DOWN, 0)

    w_o = weight(WO)

    def attended_back(cols):
        gall[1, 0, :, cols] = dot_nt(gall[0, 0], w_o[cols, :]).astype(BF)
    columns_loop(attended_back)
    weight_done()
    share_cd = remote(gall.at[1 - core, 0], gcd_in, peer)
    folded = jnp.concatenate([dot_nt(gall[1, 0], wkv[:MAIN, :]), dot_nt(gall[1, 0], w_rest[...])], axis=1)
    along = jnp.sum(folded * amix[...].astype(F32), axis=0, keepdims=True)
    gsum[3:4, :FEAT_PAD] = along
    gsum[3:4, FEAT_PAD:] = jnp.zeros((1, width - FEAT_PAD), F32)
    da_all[pl.ds(chip, 1), :, pl.ds(core, 1)] = folded.astype(BF).reshape(1, 2, 1, block, FEAT_PAD)
    mine = da_all.at[chip, :, core]
    da_across = remote(mine, mine, across)
    da_peer = remote(mine, mine, peer)
    tick(2.0)
    weight_grad(SV)
    tick(1.0)
    da_across.wait_recv()
    other = da_all.at[1 - chip, :, core]
    da_other = remote(other, other, peer)
    weight_grad(DOWN1)
    tick(1.0)
    weight_grad(UP1)
    tick(1.0)

    share_cd.wait_recv()
    amix_copy.wait_recv()
    lefts = jnp.concatenate([amix[:, :MAIN], amix_in[:, :MAIN]], axis=0)
    grads = jnp.concatenate([gall[pl.ds(core, 1), 0][0], gcd_in[...]], axis=0)
    total = dot_tn(lefts, grads).astype(BF)
    for plane in range(2):
        store_plane(FEATURE_UNIT, plane, total[plane * LANES : (plane + 1) * LANES])
    begin_unit(FEATURE_UNIT)
    for plane in range(2):
        store_plane(INIT_UNIT, plane, upstr[plane * block : (plane + 1) * block, :].astype(BF))
    begin_unit(INIT_UNIT)
    gsum[4:, :] = jnp.zeros((gsum.shape[0] - 4, width), F32)
    rests = [dot_tn(amix[:, MAIN:], gall[side, 0])[:8] for side in range(2)]
    for i in range(8):
        cols = slice(i * LANES, (i + 1) * LANES)
        both = jnp.concatenate([rests[0][:, cols], rests[1][:, cols]], axis=0)
        sm[16 * i : 16 * (i + 1), FEAT_PAD:] = both.astype(BF)
        sm[128 + 16 * i : 128 + 16 * (i + 1), FEAT_PAD:] = gsum[:, cols].astype(BF)
    sm[256:, FEAT_PAD:] = jnp.zeros((lat - 256, LANES), BF)
    tick(2.0)

    da_peer.wait_recv()
    da_other.wait_recv()
    unspill.wait()

    def score_rows(s):
        return wslots.at[s, pl.ds(0, lat)]

    def da_rows(s):
        return wslots.at[s, pl.ds(lat, lat), pl.ds(0, CAT)]

    def q_rows(s):
        return wslots.at[2, pl.ds(s * lat, lat), pl.ds(0, CAT)]

    for s in range(2):
        for i in range(4):
            rows = pl.ds(i * block, block)
            wslots[s, lat + i * block : lat + (i + 1) * block, :CAT] = spread_out(
                da_all[s, i // 2, i % 2], s, rows
            )
            wslots[2, s * lat + i * block : s * lat + (i + 1) * block, :CAT] = spread_out(
                fold[rows, :], s, rows
            )

        def back_cols(cols, s=s):
            fbuf[:, cols] = dot(wslots[s, lat:, :CAT], xcat[s, :, cols])
        columns_loop(back_cols, 256, slots)

        def score_back(rows, s=s):
            prob = pbuf[s, rows, :].astype(F32)
            grad = fbuf[rows, :]
            delta = jnp.sum(prob * grad, axis=1, keepdims=True)
            wslots[s, rows, :] = (prob * (grad - delta)).astype(BF)
        rows_loop(score_back, 64, lat)
        scores = wslots[s, :lat, :]
        zero = dot_nt(scores, xcat[s, :MAIN, :])
        one = dot_nt(scores, xcat[s, MAIN : 2 * MAIN, :])
        rest = dot_nt(scores, xcat[s, 2 * MAIN :, :])
        main, rest = pull_in(s, pl.ds(0, lat), zero, one, rest)
        if s == 0:
            bsum[:, :MAIN] = main
            bsum[:, MAIN:] = rest
        else:
            sm[:, :MAIN] = (bsum[:, :MAIN] + main).astype(BF)
            sm[:, MAIN:FEAT_PAD] = (bsum[:, MAIN:] + rest).astype(BF)
        tick(4.0)

    small_send()
    for copy in act_copies.values():
        copy.wait_send()
    for s in range(2):
        for at, (lo, size) in enumerate(((0, MAIN), (MAIN, MAIN), (2 * MAIN, LANES))):
            cols = pl.ds(lo, size)
            total = dot_tn(wslots[2, s * lat : (s + 1) * lat, cols], wslots[s, :lat, :])
            total = total + dot_tn(wslots[s, lat:, cols], pbuf[s])
            acts[pl.ds(s * CAT + lo, size), :] = total.astype(BF)
            tick(2.0)

    main_gain, rest_gain = gain_col[:MAIN, :], gain_col[MAIN:, :]
    y_copy = None
    for k in range(2):
        if y_copy is not None:
            y_copy.wait()
        for s in range(2):

            def pixel_step(jb, carry, k=k, s=s):
                cols = pl.ds(pl.multiple_of(jb * LANES, LANES), LANES)
                up_main = acts[s * CAT + k * MAIN : s * CAT + (k + 1) * MAIN, cols].astype(F32)
                up_rest = acts[s * CAT + 2 * MAIN : s * CAT + 2 * MAIN + 16, cols].astype(F32)
                up_rest = up_rest[8 * k : 8 * k + 8]
                x_main = xcat[s, k * MAIN : (k + 1) * MAIN, cols].astype(F32)
                x_rest = xcat[s, 2 * MAIN : 2 * MAIN + 16, cols].astype(F32)[8 * k : 8 * k + 8]
                rs = pixel_rs[pl.ds(k * (group // 2) + 2 * jb + s, 1), :]
                scaled_main, scaled_rest = up_main * main_gain, up_rest * rest_gain

                def mean_of(a, b):
                    whole = jnp.sum(a, axis=0, keepdims=True) + jnp.sum(b, axis=0, keepdims=True)
                    return whole * (1.0 / features)
                centre = mean_of(scaled_main, scaled_rest)
                along = mean_of(up_main * x_main, up_rest * x_rest)
                unit_main, unit_rest = x_main / main_gain, x_rest / rest_gain
                out_main = rs * (scaled_main - centre - unit_main * along)
                out_rest = rs * (scaled_rest - centre - unit_rest * along)
                flat[pl.ds(2 * jb + s, tall, stride=group // 2), :] = jnp.concatenate(
                    [out_main, out_rest], axis=0
                )
                return carry
            lax.fori_loop(0, blocks, pixel_step, 0)
            tick(2.0)
        y_copy = local(flat.at[pl.ds(0, features * group // 2)], y_ref.at[k], 7 + k)
    while next_due() < 1e9:
        serve()
    for g, from_chip, own in gathers:
        from_chip.wait_recv()
        span = pl.ds(g[0], len(g))
        remote(fin_in.at[span], gat_ref.at[other_row, span], peer)
        own.wait()
        z_local.append(local(fin_in.at[span], gat_ref.at[other_row, span], 9 + g[0] // 6))
    for copy in z_local + [y_copy]:
        copy.wait()
    for copy in copies:
        copy.finish()


def finish_kernel(*refs):
    it = iter(refs)

    def take(n=None):
        return next(it) if n is None else [next(it) for _ in range(n)]

    y_in, lat_in = take(2)
    ins = take(8)
    query_gain, pixel_gain = take(2)
    y_out, lat_out, init_out, pixel_gain_out, key_out, value_out = take(6)
    gain_outs = take(4)
    mat_outs = take(MATS + 2)
    held = take(8)
    summed, small, fold, init_all, wq, wk, wv, init_sum = held
    unit, normed, total, mats, wk_rest, wv_rest, y_buf, lat_buf, back = take(9)
    sem, out_sem = take(2)
    features, width = ins[5].shape
    lat = init_all.shape[0]
    block = lat // 4
    j = lax.axis_index("seq")
    row = lax.axis_index("row")
    cross_scale = 1.0 / math.sqrt(width)

    through = [
        (pltpu.make_async_copy(y_in.at[k], y_buf.at[:, pl.ds(k * y_in.shape[2], y_in.shape[2])], sem.at[8 + k]))
        for k in range(2)
    ] + [pltpu.make_async_copy(lat_in, lat_buf, sem.at[10])]
    copies = []
    for i, (src, dst) in enumerate(zip(ins, held)):
        copies.append(pltpu.make_async_copy(src, dst, sem.at[i]))
        copies[-1].start()
        if i == 0:
            for copy in through:
                copy.start()
    outs = []

    def put(src, dst):
        copy = pltpu.make_async_copy(src, dst, out_sem.at[len(outs)])
        copy.start()
        outs.append(copy)

    copies[0].wait()
    for m in range(MATS):
        for r in range(4):
            for h in range(2):
                at = (r % 2) * (width // 2) + (r // 2) * 2 * LANES + h * LANES
                mats[m, at : at + LANES, :] = summed[r, 2 * m + h].astype(F32)
        put(mats.at[m], mat_outs[m])
    copies[3].wait()
    query_rs = []
    for r in range(4):
        rows = pl.ds(r * block, block)
        value, scale = norm_parts(init_all[rows, :].astype(F32))
        unit[rows, :] = value
        normed[rows, :] = (value * query_gain[...]).astype(BF)
        query_rs.append(scale)
    for copy in through:
        copy.wait()
    put(y_buf, y_out)
    put(lat_buf, lat_out)
    for copy in copies[1:3] + copies[4:]:
        copy.wait()
    fill_rest(wv_rest, wv)
    fill_rest(wk_rest, wk)
    my_cols = pl.ds(pl.multiple_of(j * LANES, LANES), LANES)

    for n in range(width // 256):
        cols = pl.ds(n * 256, 256)
        value = dot(small[:, :MAIN], wk[:MAIN, cols]) + dot(small[:, MAIN:FEAT_PAD], wk_rest[:, cols])
        total[:, cols] = (value * cross_scale).astype(BF)

    def put_turned(index, value):
        for n in range(width // LANES):
            mats[index, n * LANES : (n + 1) * LANES, :] = value[:, n * LANES : (n + 1) * LANES].T
        put(mats.at[index], mat_outs[index])
    put_turned(MATS, dot_tn(total[:, my_cols], normed[...]))
    outer = [
        [summed[2 * y + c, FEATURE_UNIT].astype(F32) for y in range(2)] for c in range(2)
    ]
    rests = small[pl.ds(pl.multiple_of(j * 16, 16), 16), FEAT_PAD:]
    value_out[:LANES, :] = outer[1][0]
    value_out[LANES:MAIN, :] = outer[1][1]
    value_out[MAIN:, :] = rests.astype(F32)[8 : 8 + features - MAIN]
    summed_c = jnp.concatenate(outer[0], axis=0).astype(BF)
    put_turned(MATS + 1, dot_tn(summed_c, wv[:MAIN, :]) + dot_tn(rests, wv_rest[:16, :]))
    my_queries = dot(normed[...], wq[:, my_cols]).astype(BF)
    key_turned = dot_tn(my_queries, small[:, :FEAT_PAD]) * cross_scale
    key_out[...] = jnp.concatenate(
        [key_turned[:, n * LANES : (n + 1) * LANES].T for n in range(3)], axis=0
    )[:features]
    for i in range(8):
        chunk = small[128 + 16 * i : 128 + 16 * (i + 1), FEAT_PAD:].astype(F32)
        for g in range(3):
            gain_outs[g][i : i + 1, :] = chunk[g : g + 1]
    scores = small[:, :FEAT_PAD].astype(F32)
    part = jnp.sum(fold[...].astype(F32) * scores, axis=0, keepdims=True)
    rest_sum = [small[128 + 16 * i : 128 + 16 * (i + 1), FEAT_PAD:].astype(F32)[3:4] for i in range(3)]
    whole = (part + jnp.concatenate(rest_sum, axis=1))[:, :features]
    pixel_gain_out[...] = (whole / pixel_gain[...].reshape(1, features)).reshape(features)
    own = pl.ds(pl.multiple_of(row * block, block), block)
    own_rs = query_rs[0]
    for r in range(1, 4):
        own_rs = jnp.where(row == r, query_rs[r], own_rs)
    sums = jnp.zeros((block, 1), F32)
    alongs = jnp.zeros((block, 1), F32)
    for n in range(width // 256):
        cols = pl.ds(n * 256, 256)
        back[:, cols] = dot_nt(total[...], wq[cols, :])
        row_sum = jnp.sum(back[:, cols] * unit[:, cols], axis=0, keepdims=True)
        for i in range(2):
            gain_outs[3][2 * n + i : 2 * n + i + 1, :] = row_sum[:, i * LANES : (i + 1) * LANES]
        scaled = back[own, cols] * query_gain[:, cols]
        sums = sums + jnp.sum(scaled, axis=1, keepdims=True)
        alongs = alongs + jnp.sum(scaled * unit[own, cols], axis=1, keepdims=True)
    scaled = back[own, my_cols] * query_gain[:, my_cols]
    query_in = own_rs * (scaled - sums * (1.0 / width) - unit[own, my_cols] * (alongs * (1.0 / width)))
    init_out[...] = init_sum[...].astype(F32) + query_in
    for copy in outs:
        copy.wait()


def finish(y, latents, summed, small, init_sum, fold, init_all, wq, wk, wv, query_gain, pixel_gain):
    features, width = wk.shape
    lat = init_all.shape[0]
    block = lat // 4
    vmem = pl.BlockSpec(memory_space=pltpu.VMEM)
    hbm = pl.BlockSpec(memory_space=pl.ANY)

    def f32(*shape):
        return jax.ShapeDtypeStruct(shape, F32)

    outs = pl.pallas_call(
        finish_kernel,
        out_shape=[f32(features, 2 * y.shape[2], LANES), jax.ShapeDtypeStruct(latents.shape, BF), f32(block, LANES),
                   f32(features), f32(features, LANES), f32(features, LANES)]
        + [f32(width // LANES, LANES)] * 4 + [f32(width, LANES)] * (MATS + 2),
        in_specs=[hbm] * 10 + [vmem] * 2,
        out_specs=[hbm] * 2 + [vmem] * 8 + [hbm] * (MATS + 2),
        scratch_shapes=[
            pltpu.VMEM(shape, BF)
            for shape in (summed.shape, small.shape, fold.shape, init_all.shape,
                          wq.shape, wk.shape, wv.shape, init_sum.shape)
        ]
        + [
            pltpu.VMEM((lat, width), F32),
            pltpu.VMEM((lat, width), BF),
            pltpu.VMEM((lat, width), BF),
            pltpu.VMEM((MATS + 2, width, LANES), F32),
            pltpu.VMEM((LANES, width), BF),
            pltpu.VMEM((LANES, width), BF),
            pltpu.VMEM((features, 2 * y.shape[2], LANES), F32),
            pltpu.VMEM(latents.shape, BF),
            pltpu.VMEM((lat, width), F32),
            pltpu.SemaphoreType.DMA((11,)),
            pltpu.SemaphoreType.DMA((MATS + 4,)),
        ],
        compiler_params=pltpu.CompilerParams(vmem_limit_bytes=VMEM_LIMIT),
    )(y, latents, summed, small, fold, init_all, wq, wk, wv, init_sum, query_gain[None],
      pixel_gain)
    y, latents, init_grad, pixel_gain_grad, key_grad, value_grad = outs[:6]
    return (y, latents, init_grad, outs[6:10], pixel_gain_grad, key_grad, value_grad, outs[10:])


def whole_stack(shards, z, pixel_gain, pseg, init, cots, seg, wk, wv, gains, weights):
    width = init.shape[1]
    block = init.shape[0]
    count = 2 * block
    lat = 2 * count
    share = width // shards
    half = width // 2
    bits = shards.bit_length() - 1
    orders = unit_orders(bits)
    nslots = 3
    features = wk.shape[0]
    group = z.shape[0] // features
    slots = group * LANES // 4
    small, size = [], lat
    for i in range(bits + 2):
        size = size // 2 if size > 16 else size
        small.append((size, 512))
    scratch = [
        ((nslots, width, width), BF),
        (wk.shape, BF),
        ((LANES, width), BF),
        ((2, block, width), BF),
        ((2, 2, block, FEAT_PAD), BF),
        ((2, block, FEAT_PAD), BF),
        ((2, block, FEAT_PAD), BF),
        ((count, FEAT_PAD), BF),
        ((count, FEAT_PAD), BF),
        ((2, 2, 2, block, FEAT_PAD), BF),
        ((lat, width), F32),
        ((3, count, LANES), F32),
        ((6 * count, width), BF),
        ((6, count, half), BF),
        ((2, count, width), BF),
        ((count, width), BF),
        ((2, 2, count, width), BF),
        ((2, lat, slots), BF),
        ((count, width), BF),
        ((2, count, width), BF),
        ((MATS, 2, count, width), BF),
        ((count, width), BF),
        ((FEATURE_UNIT + 1, share, LANES), BF),
        ((2, 2, 2, block, FEAT_PAD), BF),
        ((lat, FEAT_PAD), F32),
        ((16, width), F32),
        ((1, lat), F32),
        ((lat, 512), BF),
        ((2, CAT, slots), BF),
        (((MAIN + 8) * group // 2, LANES), F32),
        ((2, 8, slots), F32),
        ((group, LANES), F32),
        ((MAIN + 8, LANES), F32),
        ((FEATURE_UNIT + 1, share, LANES), BF),
        ((UNITS * 2, width, LANES), BF),
    ]
    for order in orders:
        scratch += [(shape, BF) for shape in stage_shapes(order, width)]
    scratch += [(shape, BF) for shape in small]
    stages = sum(len(order) for order in orders)
    vmem = pl.BlockSpec(memory_space=pltpu.VMEM)
    hbm = pl.BlockSpec(memory_space=pl.ANY)
    return pl.pallas_call(
        functools.partial(
            main_kernel, (shards, width, count, dict(small_stages=len(small)))
        ),
        out_shape=[
            jax.ShapeDtypeStruct((2, block, width), BF),
            jax.ShapeDtypeStruct((lat, 512), BF),
            jax.ShapeDtypeStruct((4, FEATURE_UNIT + 1, share, LANES), BF),
            jax.ShapeDtypeStruct((share, LANES), BF),
            jax.ShapeDtypeStruct((lat, FEAT_PAD), BF),
            jax.ShapeDtypeStruct((4, block, width), BF),
            jax.ShapeDtypeStruct((2, features * group // 2, LANES), F32),
            jax.ShapeDtypeStruct((2, lat, slots), BF),
        ],
        in_specs=[hbm, pl.BlockSpec(memory_space=pltpu.SMEM), vmem, vmem, hbm, vmem]
        + [hbm] * 2 + [vmem] * 4 + [hbm] * 10,
        out_specs=[vmem, vmem, hbm, vmem, vmem, hbm, hbm, hbm],
        scratch_shapes=[pltpu.VMEM(shape, kind) for shape, kind in scratch]
        + [
            pltpu.SemaphoreType.DMA((nslots + 2 + 13,)),
            pltpu.SemaphoreType.DMA((-(-z.shape[0] // width),)),
            pltpu.SemaphoreType.DMA((stages,)),
            pltpu.SemaphoreType.DMA((stages,)),
            pltpu.SemaphoreType.DMA((80,)),
            pltpu.SemaphoreType.DMA((80,)),
        ],
        compiler_params=pltpu.CompilerParams(
            collective_id=0, has_side_effects=True, vmem_limit_bytes=VMEM_LIMIT
        ),
    )(z, pixel_gain, pseg, init, cots, seg, wk, wv, *[g[None] for g in gains], *weights)


VMEM_LIMIT = 63 * 1024 * 1024


def body(
    pixels, pixel_seg, latent_seg, latent_init, cotangent,
    pixel_gain, query_gain, query_weight, key_weight, value_weight, output_weight,
    mlp_gain, up_weight, down_weight,
    self_gain, self_query, self_key, self_value, self_output,
    second_gain, second_up, second_down,
):
    seqs, pix, features = pixels.shape
    block, width = latent_init.shape
    shards = lax.axis_size("seq")
    lat = block * lax.axis_size("row")
    row = lax.axis_index("row")
    cross_scale = 1.0 / math.sqrt(width)
    tiles = pix // LANES

    z = pixels.transpose(2, 0, 1).reshape(features, seqs, tiles, LANES)
    z = z.transpose(0, 2, 1, 3).reshape(features * seqs * tiles, LANES)
    latents, small, summed, init_sum, fold, init_all, y, unused = whole_stack(
        shards, z, pixel_gain, pixel_seg, latent_init, cotangent, latent_seg, key_weight, value_weight,
        (mlp_gain, self_gain, second_gain, query_gain),
        (query_weight, output_weight, up_weight, down_weight, self_query, self_key, self_value,
         self_output, second_up, second_down),
    )
    init_all = init_all.reshape(lat, width)
    y = y.reshape(2, features, tiles, LANES)
    if width // shards == LANES:
        y, latents, init_grad, gains, pixel_gain_grad, key_grad, value_grad, mats = finish(
            y, latents, summed, small, init_sum, fold, init_all, query_weight, key_weight,
            value_weight, query_gain, pixel_gain,
        )
    else:
        y = y.transpose(1, 0, 2, 3)
    pixel_grad = y.reshape(features, tiles, seqs, LANES).transpose(2, 1, 3, 0)
    pixel_grad = pixel_grad.reshape(seqs, pix, features)
    if width // shards == LANES:
        mlp_gain_grad, self_gain_grad, second_gain_grad, query_gain_grad = [
            g.reshape(width) for g in gains
        ]
        return (
            latents, pixel_grad, init_grad, pixel_gain_grad,
            query_gain_grad, mlp_gain_grad, self_gain_grad, second_gain_grad,
            mats[MATS], key_grad, value_grad, mats[MATS + 1], mats[UP1], mats[DOWN1],
            mats[SQ], mats[SK], mats[SV], mats[SOUT], mats[UP2], mats[DOWN2],
        )

    share = width // shards
    at = lax.axis_index("seq") * share

    def columns(arr):
        return lax.dynamic_slice_in_dim(arr, at, share, arr.ndim - 1)

    score_b = small[:, :features]
    side = small[:, FEAT_PAD:]
    rests = side[:128].reshape(8, 2, 8, LANES).transpose(1, 2, 0, 3).reshape(2, 8, width)
    sums = side[128:256].reshape(8, 16, LANES).transpose(1, 0, 2).reshape(16, width).astype(F32)
    pixel_gain_grad = (
        jnp.sum(fold[:, :features].astype(F32) * score_b.astype(F32), axis=0) + sums[3, :features]
    ) / pixel_gain
    units = summed.reshape(2, 2, FEATURE_UNIT + 1, share, LANES)
    mats = units[:, :, :FEATURE_UNIT].reshape(2, 2, MATS, 2, share, LANES)
    mats = mats.transpose(2, 1, 0, 3, 5, 4).reshape(MATS, width, share).astype(F32)
    outer = units[:, :, FEATURE_UNIT].transpose(1, 0, 3, 2).reshape(2, MAIN, share)
    outer = jnp.concatenate([outer, columns(rests)[:, : features - MAIN]], axis=1)
    value_grad = outer[1].astype(F32)
    output_grad = dot_tn(value_weight, outer[0])
    query_unit, query_rs = norm_parts(init_all.astype(F32))
    query_normed = (query_unit * query_gain).astype(BF)
    my_queries = dot(query_normed, columns(query_weight)).astype(BF)
    key_grad = dot_tn(score_b, my_queries) * cross_scale
    query_total = (dot(score_b, key_weight) * cross_scale).astype(BF)
    query_grad = dot_tn(query_normed, columns(query_total))
    query_in, query_gain_grad = norm_back(
        query_unit, query_rs, query_gain, dot_nt(query_total, query_weight)
    )
    init_grad = init_sum.T.astype(F32) + lax.dynamic_slice(query_in, (row * block, at), (block, share))
    return (
        latents, pixel_grad, init_grad,
        pixel_gain_grad, query_gain_grad, sums[0], sums[1], sums[2],
        query_grad, key_grad, value_grad, output_grad, mats[UP1], mats[DOWN1],
        mats[SQ], mats[SK], mats[SV], mats[SOUT], mats[UP2], mats[DOWN2],
    )


def solution(mesh):
    placed = (
        P("seq", "row", None), P("seq", "row"), P("seq", "row"), P("row", None),
        P("seq", "row", None),
    ) + (P(),) * 17
    cols = P(None, "seq")
    return jax.shard_map(
        body,
        mesh=mesh,
        in_specs=placed,
        out_specs=(P("seq", "row", None), P("seq", "row", None), P("row", "seq"))
        + (P(),) * 5 + (cols,) * 12,
        check_vma=False,
    )
```

```python
import functools
import math

import jax
import jax.numpy as jnp
from jax import lax
from jax.experimental import pallas as pl
from jax.experimental.pallas import tpu as pltpu
from jax.sharding import PartitionSpec as P

HEADS = 8
EPSILON = 1e-05
NEGATIVE = -1e9
BF = jnp.bfloat16
F32 = jnp.float32
LANES = 128
FEAT_PAD = 384
MAIN = 256
CAT = 2 * MAIN + LANES
MESH = pl.DeviceIdType.MESH


def dot(a, b):
    return jnp.dot(a, b, preferred_element_type=F32)


def dot_tn(a, b):
    return lax.dot_general(a, b, (((0,), (0,)), ((), ())), preferred_element_type=F32)


def dot_nt(a, b):
    return lax.dot_general(a, b, (((1,), (1,)), ((), ())), preferred_element_type=F32)


def fill_rest(rest, matrix):
    rest[...] = jnp.zeros(rest.shape, rest.dtype)
    rest[: matrix.shape[0] - MAIN, :] = matrix[MAIN:, :]


def norm_parts(values):
    centre = values - jnp.mean(values, axis=-1, keepdims=True)
    rs = lax.rsqrt(jnp.mean(centre * centre, axis=-1, keepdims=True) + EPSILON)
    return centre * rs, rs


def norm_back(unit, rs, gain, upstream):
    scaled = upstream * gain
    grad = rs * (
        scaled
        - jnp.mean(scaled, axis=-1, keepdims=True)
        - unit * jnp.mean(scaled * unit, axis=-1, keepdims=True)
    )
    return grad, jnp.sum(upstream * unit, axis=0)


def gelu_parts(hidden):
    cdf = 0.5 * (1.0 + lax.erf(hidden * math.sqrt(0.5)))
    pdf = jnp.exp(-0.5 * hidden * hidden) * (1.0 / math.sqrt(2.0 * math.pi))
    return hidden * cdf, cdf + hidden * pdf


NORMED1, ACTIVE1, SELFN, MIXED, NORMED2, ACTIVE2 = range(6)
DOWN2, UP2, SOUT, SQ, SK, SV, DOWN1, UP1 = range(8)
LEFT = {
    DOWN2: ACTIVE2, UP2: NORMED2, SOUT: MIXED, SQ: SELFN, SK: SELFN, SV: SELFN,
    DOWN1: ACTIVE1, UP1: NORMED1,
}
MATS = 8
FEATURE_UNIT = 2 * MATS
UNITS = MATS + 1


class Remote:
    def __init__(self, log, src, dst, send_sem, recv_sem, device):
        self.copy = pltpu.make_async_remote_copy(
            src_ref=src, dst_ref=dst, send_sem=send_sem, recv_sem=recv_sem,
            device_id=device, device_id_type=MESH,
        )
        self.copy.start()
        self.arrived = self.sent = False
        log.append(self)

    def wait_recv(self):
        if not self.arrived:
            self.copy.wait_recv()
        self.arrived = True

    def wait_send(self):
        if not self.sent:
            self.copy.wait_send()
        self.sent = True

    def finish(self):
        self.wait_recv()
        self.wait_send()


KINDS = "FCDABCEBA"


def unit_orders(bits):
    first, second, tail = [0], list(range(1, min(bits, 2))), list(range(2, bits))
    kinds = {
        "A": ["y"] + first + second + tail,
        "B": first + second + ["y"] + tail,
        "C": second + first + ["y"] + tail,
        "D": first + ["y"] + second + tail,
        "E": second + ["y"] + first + tail,
        "F": ["y"] + second + first + tail,
    }
    return [kinds[letter] for letter in KINDS]


def stage_shapes(order, width):
    shapes, planes, size = [], 4, width
    for axis in order:
        if axis == "y":
            planes = 2
        else:
            size //= 2
        shapes.append((planes, size, LANES))
    return shapes


def main_kernel(cfg, *refs):
    shards, width, count, sizes = cfg
    bits = shards.bit_length() - 1
    share = width // shards
    half = width // 2
    block = count // 2
    lat = 2 * count
    head_width = width // HEADS
    cross_scale = 1.0 / math.sqrt(width)
    self_scale = 1.0 / math.sqrt(head_width)
    orders = unit_orders(bits)
    it = iter(refs)

    def take(n=None):
        return next(it) if n is None else [next(it) for _ in range(n)]

    (z_hbm, pixel_gain, pseg_ref, init_ref, cot_hbm, seg_ref, wk_hbm, wv_hbm) = take(8)
    gain_refs = take(4)
    w_hbm = take(10)
    (lat_ref, sm_out, gat_ref, initg_ref, fold, zall, y_ref, pspill) = take(8)
    (wslots, wkv, w_rest, zbuf, ain1, asum, ain2, amix, amix_in, amat, fbuf, rsb, acts, acts_in, slopes,
     qbuf, kv, pbuf, dmix, dkv_in, gall, gcd_in, fin, da_all, bsum, gsum, idrow,
     sm, xcat, flat, rest0, pixel_rs, gain_col, fin_in, part) = take(35)
    recv = [take(len(orders[u])) for u in range(UNITS)]
    smr = take(sizes["small_stages"])
    (wsem, psem, zsem, usend, urecv, csend, crecv) = take(7)

    j = lax.axis_index("seq")
    row = lax.axis_index("row")
    core, chip = row % 2, row // 2
    peer = {"row": row + 1 - 2 * core}
    across = {"row": row + 2 - 4 * chip}
    diagonal = {"row": 3 - row}
    bit_of = [(j // (1 << b)) % 2 for b in range(bits)]
    partner = {b: {"seq": j + (1 - 2 * bit_of[b]) * (1 << b)} for b in range(bits)}
    partner["y"] = across
    stream = fbuf.at[pl.ds(0, count)]
    upstr = fbuf.at[pl.ds(count, count)]
    dnorm = stream

    def act(k):
        return pl.ds(k * count, count)

    WQ, WO, UP, DOWN, QW, KW, VW, SO, UPB, DOWNB = range(10)
    uses = [WQ, WO, UP, DOWN, KW, VW, QW, SO, UPB, DOWNB, DOWNB, UPB, SO, QW, KW, VW, DOWN, UP, WO]
    nslots = wslots.shape[0]
    at_use = [0]

    pieces = 4

    class WeightCopy:
        def __init__(self, i):
            size = width // pieces
            self.copies = [
                pltpu.make_async_copy(
                    w_hbm[uses[i]].at[pl.ds(p * size, size)],
                    wslots.at[i % nslots, pl.ds(p * size, size)],
                    psem.at[(i % nslots) * pieces + p],
                )
                for p in range(pieces)
            ]

        def start(self):
            for copy in self.copies:
                copy.start()

        def wait(self):
            for copy in self.copies:
                copy.wait()

    def weight_copy(i):
        return WeightCopy(i)

    def weight(expect):
        i = at_use[0]
        assert uses[i] == expect
        at_use[0] += 1
        weight_copy(i).wait()
        return wslots.at[i % nslots]

    def weight_done():
        i = at_use[0] - 1 + nslots
        if i < len(uses):
            weight_copy(i).start()

    features = wk_hbm.shape[0]
    pixel_copies = []
    for i, lo in enumerate(range(0, z_hbm.shape[0], width)):
        rows = min(width, z_hbm.shape[0] - lo)
        pixel_copies.append(pltpu.make_async_copy(
            z_hbm.at[pl.ds(lo, rows)], part.at[i, pl.ds(0, rows)], zsem.at[i]
        ))
    weight_copy(0).start()
    wk_copy = pltpu.make_async_copy(wk_hbm, wkv, wsem.at[nslots])
    wk_copy.start()
    for i in range(1, nslots):
        weight_copy(i).start()
    wv_copy = pltpu.make_async_copy(wv_hbm, wkv, wsem.at[nslots + 1])
    for copy in pixel_copies:
        copy.start()

    barrier = pltpu.get_barrier_semaphore()
    partners = [peer, across, diagonal] + [partner[b] for b in range(bits)]
    for p in partners:
        pl.semaphore_signal(barrier, inc=1, device_id=p, device_id_type=MESH)
    copies = []
    slot_count = [0]

    def remote(src, dst, device):
        slot = slot_count[0]
        slot_count[0] += 1
        return Remote(copies, src, dst, csend.at[slot], crecv.at[slot], device)

    def local(src, dst, slot):
        copy = pltpu.make_async_copy(src, dst, wsem.at[nslots + 2 + slot])
        copy.start()
        return copy

    def rows_loop(body, step=64, total=None):
        def run(i, carry):
            body(pl.ds(pl.multiple_of(i * step, step), step))
            return carry
        lax.fori_loop(0, (total or count) // step, run, 0, unroll=2)

    def columns_loop(body, step=256, total=width):
        def run(i, carry):
            body(pl.ds(pl.multiple_of(i * step, step), step))
            return carry
        lax.fori_loop(0, total // step, run, 0, unroll=2)

    def layer(k, into):
        def body(rows):
            unit, rs = norm_parts(stream[rows, :])
            rsb[k, rows, :] = jnp.broadcast_to(rs, (rs.shape[0], LANES))
            place = pl.ds(pl.multiple_of(into * count + rows.start, rows.size), rows.size)
            acts[place, :] = (unit * gain_refs[k][...]).astype(BF)
        rows_loop(body)

    def layer_back(k, normed, into, start=None):
        gain = gain_refs[k][...]
        inverse = 1.0 / gain

        def body(i, total):
            rows = pl.ds(pl.multiple_of(i * 64, 64), 64)
            place = pl.ds(pl.multiple_of(normed * count + i * 64, 64), 64)
            dn = dnorm[rows, :]
            unit = acts[place, :].astype(F32) * inverse
            scaled = dn * gain
            rs = rsb[k, rows, :][:, :1]
            mean = jnp.mean(scaled, axis=-1, keepdims=True)
            along = jnp.mean(scaled * unit, axis=-1, keepdims=True)
            before = upstr[rows, :] if start is None else gall[start, 0, rows, :].astype(F32)
            after = before + rs * (scaled - mean - unit * along)
            upstr[rows, :] = after
            gall[into, 0, rows, :] = after.astype(BF)
            return total + jnp.sum(dn * unit, axis=0, keepdims=True)
        gsum[pl.ds(k, 1), :] = lax.fori_loop(
            0, count // 64, body, jnp.zeros((1, width), F32), unroll=2
        )

    act_copies, grad_copies = {}, {}

    def share_act(k):
        away = pl.ds(pl.multiple_of((1 - core) * half, half), half)
        act_copies[k] = remote(acts.at[act(k), away], acts_in.at[k], peer)

    def share_grad(m):
        grad_copies[m] = remote(gall.at[m, 0], gall.at[m, 1], peer)

    clock = [0.0]
    small = dict(lo=0, size=lat, stage=0, up=[], copy=None, due=1e9)
    axes = [(core, peer), (chip, across)] + [(bit_of[b], partner[b]) for b in range(bits)]

    def small_send():
        bit, device = axes[small["stage"]]
        size = small["size"]
        if size > 16:
            size //= 2
            away = pl.multiple_of(small["lo"] + (1 - bit) * size, 16)
            keep = pl.multiple_of(small["lo"] + bit * size, 16)
            small["up"].append((device, keep, size))
            small["lo"], small["size"] = keep, size
        else:
            away = small["lo"]
        small["copy"] = remote(sm.at[pl.ds(away, size)], smr[small["stage"]], device)
        small["due"] = clock[0] + 2.5 + size * 512 * 4 / 75e3

    def small_grow():
        device, lo, size = small["up"].pop()
        rows = pl.ds(lo, size)
        small["copy"] = remote(sm_out.at[rows], sm_out.at[rows], device)
        small["due"] = clock[0] + 2.5 + size * 512 * 4 / 75e3

    def small_step():
        copy, size = small["copy"], small["size"]
        copy.wait_recv()
        if small["stage"] < len(axes):
            copy.wait_send()
            rows = pl.ds(small["lo"], size)
            sm[rows, :] = sm[rows, :] + smr[small["stage"]][...]
            small["stage"] += 1
            if small["stage"] < len(axes):
                small_send()
                return
            sm_out[rows, :] = sm[rows, :]
        if small["up"]:
            small_grow()
        else:
            small["due"] = 1e9

    state = {}
    free = {}
    pending = []

    def region(u, planes, lo, size):
        if planes == 4:
            return part.at[pl.ds(4 * u, 4), pl.ds(lo, size)]
        return part.at[pl.ds(4 * u + 2 * chip, 2), pl.ds(lo, size)]

    def send_stage(u):
        s = state[u]
        axis = orders[u][s["stage"]]
        k = s["stage"]
        if axis == "y":
            src = part.at[pl.ds(4 * u + 2 - 2 * chip, 2), pl.ds(s["lo"], s["size"])]
            s["planes"] = 2
        else:
            size = s["size"] // 2
            keep = s["lo"] + bit_of[axis] * size
            away = s["lo"] + (1 - bit_of[axis]) * size
            src = region(u, s["planes"], pl.multiple_of(away, share), size)
            s["lo"], s["size"] = pl.multiple_of(keep, share), size
        slot = sum(len(orders[v]) for v in range(u)) + k
        s["copy"] = Remote(copies, src, recv[u][k], usend.at[slot], urecv.at[slot], partner[axis])
        took = s["size"] * s["planes"] * LANES * 2 * 2 / 80e3
        links = {"y": {"y": 1}, 0: {"x": 1}, 1: {"inner": 1}}.get(axis, {"inner": 1, "middle": 2})
        begin = max([clock[0]] + [free.get(link, 0.0) for link in links])
        for link, share_of in links.items():
            free[link] = begin + took * share_of
        s["due"] = max(free[link] for link in links) + 4.0
        pending.append(u)

    def finish_stage(u):
        s = state[u]
        k = s["stage"]
        s["copy"].wait_recv()
        last = k == len(orders[u]) - 1
        mine = pl.ds(4 * u, 4) if s["planes"] == 4 else pl.ds(4 * u + 2 * chip, 2)
        if last:
            total = part[mine, pl.ds(s["lo"], s["size"])] + recv[u][k][...]
            if u == MATS:
                fin[FEATURE_UNIT] = total[0]
                initg_ref[...] = total[1]
            else:
                fin[2 * u : 2 * u + 2] = total
            s["done"] = True
            done_units.append(u)
            gather_ready()
            return
        step = min(s["size"], 256)

        def add(i, carry):
            off = pl.multiple_of(i * step, step)
            rows = pl.ds(pl.multiple_of(s["lo"] + off, share), step)
            part[mine, rows, :] = part[mine, rows, :] + recv[u][k][:, pl.ds(off, step), :]
            return carry
        lax.fori_loop(0, s["size"] // step, add, 0)
        s["stage"] += 1
        send_stage(u)

    done_units, gathers = [], []
    groups = [[0, 1, 2], [3, 4, 5], [6, 7, 8]]

    def gather_ready():
        while len(gathers) < len(groups) and all(u in done_units for u in groups[len(gathers)]):
            g = groups[len(gathers)]
            span = pl.ds(2 * g[0], 6 if g[-1] < MATS else 5)
            from_chip = remote(fin.at[span], fin_in.at[span], across)
            remote(fin.at[span], gat_ref.at[row, span], peer)
            gathers.append((g, from_chip, local(fin.at[span], gat_ref.at[row, span], len(gathers))))

    def serve():
        at = min((state[u]["due"], u) for u in pending) if pending else (1e9, None)
        if small["due"] <= at[0]:
            clock[0] = max(clock[0], small["due"])
            small_step()
        else:
            clock[0] = max(clock[0], at[0]) + 0.3
            pending.remove(at[1])
            finish_stage(at[1])

    def next_due():
        return min([small["due"]] + [state[u]["due"] for u in pending])

    def tick(us):
        clock[0] += 1.6 * us
        while next_due() <= clock[0]:
            serve()

    def begin_unit(u):
        state[u] = dict(stage=0, planes=4, lo=0, size=width, done=False)
        send_stage(u)

    def position(u, block):
        seq_bits = [a for a in orders[u] if a != "y"]
        pos = 0
        for at, b in enumerate(seq_bits):
            pos = pos + ((block // (1 << b)) % 2) * (1 << (bits - 1 - at))
        return pos

    def store_plane(u, plane, side, value):
        if share != LANES:
            value = value.astype(F32).T.astype(BF)
        for block_at in range(shards):
            place = pl.ds(position(u, block_at) * share, share)
            if share == LANES:
                part[pl.ds(4 * u + 2 * plane + side, 1), place, :] = value[:, block_at * share : (block_at + 1) * share][None]
            else:
                part[pl.ds(4 * u + 2 * plane + side, 1), place, :] = value[block_at * share : (block_at + 1) * share][None]

    def weight_grad(m):
        left = LEFT[m]
        act_copies[left].wait_recv()
        grad_copies[m].wait_recv()

        def run(plane, carry):
            own = pl.ds(pl.multiple_of(core * half + plane * MAIN, MAIN), MAIN)
            theirs = pl.ds(pl.multiple_of(plane * MAIN, MAIN), MAIN)
            lefts = jnp.concatenate([acts[act(left), own], acts_in[left, :, theirs]], axis=0)
            total = dot_tn(lefts, gall[m].reshape(2 * count, width)).astype(BF)
            store_plane(m, plane, 0, total[:LANES])
            store_plane(m, plane, 1, total[LANES:])
            return carry
        lax.fori_loop(0, 2, run, 0)
        begin_unit(m)

    cot_rows = pl.ds(pl.multiple_of(chip * block, block), block)
    c_own = local(cot_hbm.at[chip], gall.at[DOWN2, 0, cot_rows], 3)
    zbuf[pl.ds(chip, 1)] = init_ref[...][None]
    unit, unused = norm_parts(init_ref[...].astype(F32))
    own_normed = (unit * gain_refs[3][...]).astype(BF)
    w = weight(WQ)
    queries = dot(own_normed, w[...]).astype(BF)
    weight_done()
    wk_copy.wait()
    fill_rest(w_rest, wkv)
    fold_main = dot_nt(queries, wkv[:MAIN, :]) * cross_scale
    fold_rest = dot_nt(queries, w_rest[...]) * cross_scale
    own_rows = pl.ds(pl.multiple_of(row * block, block), block)
    seg = seg_ref[...].astype(F32)
    ids = jnp.concatenate([seg, jnp.zeros((LANES - 2, block), F32)], axis=0).T
    ids = pltpu.roll(ids, 5, 1)
    fold[own_rows, :MAIN] = fold_main.astype(BF)
    fold[own_rows, MAIN:] = (fold_rest + ids).astype(BF)
    wv_copy.start()
    pl.semaphore_wait(barrier, len(partners))
    fold_copies = [remote(fold.at[own_rows], fold.at[own_rows], p) for p in (across, diagonal, peer)]
    z_copy = remote(init_ref, zbuf.at[chip], across)
    c_copy = remote(cot_hbm.at[1 - chip], gall.at[DOWN2, 0, cot_rows], across)
    group = pixel_rs.shape[0]
    blocks = group // 4
    tall = gain_col.shape[0]

    fold_in = width // group

    def pixel_row(f, lo=0, rows=group):
        at = pl.ds(pl.multiple_of((f % fold_in) * group + lo, rows), rows)
        return part[pl.ds(f // fold_in, 1), at, :][0].astype(F32)

    zero = jnp.zeros((group, LANES), F32)
    for copy in pixel_copies:
        copy.wait()
    mean = lax.fori_loop(0, features, lambda f, acc: acc + pixel_row(f), zero, unroll=9)
    mean = mean * (1.0 / features)

    def spread(f, acc):
        centre = pixel_row(f) - mean
        return acc + centre * centre
    spread_sum = lax.fori_loop(0, features, spread, zero, unroll=9)
    rs_all = lax.rsqrt(spread_sum * (1.0 / features) + EPSILON)
    pixel_rs[...] = rs_all
    gain_col[...] = jnp.ones(gain_col.shape, F32)
    flat[features * group // 2 :, :] = jnp.zeros(((tall - features) * group // 2, LANES), F32)
    for s in range(2):
        xcat[s, 2 * MAIN + 16 :, :] = jnp.zeros((LANES - 16, xcat.shape[2]), BF)
    for k in range(2):
        half_rows = slice(k * (group // 2), (k + 1) * (group // 2))
        half_mean, half_rs = mean[half_rows], rs_all[half_rows]

        def scale(f, carry, k=k, half_mean=half_mean, half_rs=half_rs):
            value = pixel_row(f, k * (group // 2), group // 2)
            rows = pl.ds(pl.multiple_of(f * (group // 2), group // 2), group // 2)
            flat[rows, :] = (value - half_mean) * (half_rs * pixel_gain[f])
            if k == 0:
                gain_col[pl.ds(f, 1), :] = jnp.full((1, LANES), pixel_gain[f], F32)
            return carry
        lax.fori_loop(0, features, scale, 0, unroll=9)
        for s in range(2):
            for jb in range(blocks):
                cols = pl.ds(jb * LANES, LANES)
                value = flat[pl.ds(2 * jb + s, tall, stride=group // 2), :]
                xcat[s, k * MAIN : (k + 1) * MAIN, cols] = value[:MAIN].astype(BF)
                if k == 0:
                    rest0[s, :, cols] = value[MAIN:]
                else:
                    both = jnp.concatenate([rest0[s, :, cols], value[MAIN:]], axis=0)
                    xcat[s, 2 * MAIN : 2 * MAIN + 16, cols] = both.astype(BF)
    for copy in fold_copies:
        copy.wait_recv()

    lane = lax.broadcasted_iota(jnp.int32, (1, LANES), 1)
    image = (2 * row).astype(F32)

    def selectors(s, rows):
        ids = fold[rows, MAIN:].astype(F32)
        ids = jnp.where(s == 0, ids[:, 5:6], ids[:, 6:7])
        return jnp.where(ids == image, 1.0, 0.0), jnp.where(ids == image + 1.0, 1.0, 0.0)

    def spread_out(source, s, rows):
        first, second = selectors(s, rows)
        main = source[:, :MAIN].astype(F32)
        rest = jnp.where(lane < 5, source[:, MAIN:].astype(F32), 0.0)
        rest = rest * first + pltpu.roll(rest, 8, 1) * second
        return jnp.concatenate([main * first, main * second, rest], axis=1).astype(BF)

    def pull_in(s, rows, zero, one, rest):
        first, second = selectors(s, rows)
        rest = jnp.where(lane < 5, rest * first + pltpu.roll(rest, LANES - 8, 1) * second, 0.0)
        return zero * first + one * second, rest

    slots = xcat.shape[2]
    core_copies = []

    def send_core(turn):
        core_copies.append(remote(amat.at[turn, :, 1 - core], ain1.at[turn], peer))

    def core_sum(turn):
        core_copies[turn].wait_recv()
        return amat[turn, :, pl.ds(core, 1)][:, 0] + ain1[turn]

    for turn in range(2):
        s = 1 - chip if turn == 0 else chip
        seq = pl.ds(s, 1)
        for i in range(4):
            rows = pl.ds(i * block, block)
            gall[2 + 2 * turn + i // 2, 0, (i % 2) * block : (i % 2 + 1) * block, :CAT] = spread_out(
                fold[rows, :], s, rows
            )
        first_ok = jnp.where(pseg_ref[seq, :slots] == 2 * row, 1.0, 0.0)
        second_ok = jnp.where(pseg_ref[seq, slots:] == 2 * row + 1, 1.0, 0.0)

        def score_cols(cols, seq=seq, turn=turn):
            queries_cat = jnp.concatenate(
                [gall[2 + 2 * turn, 0, :, :CAT], gall[3 + 2 * turn, 0, :, :CAT]], axis=0
            )
            fbuf[:, cols] = dot(queries_cat, xcat[seq, :, cols][0])
        columns_loop(score_cols, 256, slots)
        if turn == 1:
            asum[...] = core_sum(0)
            step2 = remote(asum, ain2, across)

        def soften(rows, s=s, seq=seq, first_ok=first_ok, second_ok=second_ok):
            first, unused = selectors(s, rows)
            allowed = second_ok + first * (first_ok - second_ok)
            scores = jnp.where(allowed > 0.5, fbuf[rows, :], NEGATIVE)
            weights = jnp.exp(scores - jnp.max(scores, axis=1, keepdims=True))
            prob = (weights * (1.0 / jnp.sum(weights, axis=1, keepdims=True))).astype(BF)
            pbuf[seq, rows, :] = prob[None]
        rows_loop(soften, 64, lat)
        probs = pbuf[seq][0]
        zero = dot_nt(probs, xcat[seq, :MAIN, :][0])
        one = dot_nt(probs, xcat[seq, MAIN : 2 * MAIN, :][0])
        rest = dot_nt(probs, xcat[seq, 2 * MAIN :, :][0])
        main, rest = pull_in(s, pl.ds(0, lat), zero, one, rest)
        amat[turn, :, :, :, :MAIN] = main.astype(BF).reshape(2, 2, block, MAIN)
        amat[turn, :, :, :, MAIN:] = rest.astype(BF).reshape(2, 2, block, LANES)
        send_core(turn)
    spill = local(pbuf, pspill, 4)

    for at in range(4):
        who = core if at < 2 else 1 - core
        rows = pl.ds(pl.multiple_of((2 * (at % 2) + who) * block, block), block)
        turned = fold[rows, MAIN:].astype(F32).T
        idrow[:, at * block : (at + 1) * block] = jnp.where(chip == 0, turned[5:6], turned[6:7])
    own_ids = []
    for h in range(2):
        rows = pl.ds(pl.multiple_of((2 * h + core) * block, block), block)
        ids = fold[rows, MAIN:].astype(F32)
        own_ids.append(jnp.where(chip == 0, ids[:, 5:6], ids[:, 6:7]))
    idcol = jnp.concatenate(own_ids, axis=0)
    z_copy.wait_recv()
    remote(init_ref, zall.at[row], peer)
    other_row = row + 2 - 4 * chip
    remote(zbuf.at[1 - chip], zall.at[other_row], peer)
    z_local = [local(init_ref, zall.at[row], 5), local(zbuf.at[1 - chip], zall.at[other_row], 6)]
    c_copy.wait_recv()
    c_own.wait()
    share_grad(DOWN2)
    wv_copy.wait()
    fill_rest(w_rest, wkv)
    step2.wait_recv()
    amix[...] = (core_sum(1) + ain2[...]).reshape(count, FEAT_PAD)
    amix_copy = remote(amix, amix_in, peer)

    def attended_cols(cols):
        value = dot(amix[:, :MAIN], wkv[:MAIN, cols]) + dot(amix[:, MAIN:], w_rest[:, cols])
        qbuf[:, cols] = value.astype(BF)
    columns_loop(attended_cols)
    w = weight(WO)

    def one_cols(cols):
        start = zbuf[:, :, cols].reshape(count, cols.size).astype(F32)
        stream[:, cols] = start + dot(qbuf[...], w[:, cols])
    columns_loop(one_cols)
    weight_done()

    def mlp(k, normed, active, up_id, down_id):
        layer(k, normed)
        share_act(normed)
        w_up = weight(up_id)

        def up_cols(cols):
            value, slope = gelu_parts(dot(acts[act(normed), :], w_up[:, cols]))
            acts[act(active), cols] = value.astype(BF)
            slopes[active // 4, :, cols] = slope.astype(BF)
        columns_loop(up_cols)
        weight_done()
        share_act(active)
        w_down = weight(down_id)

        def down_cols(cols):
            stream[:, cols] += dot(acts[act(active), :], w_down[:, cols])
        columns_loop(down_cols)
        weight_done()

    mlp(0, NORMED1, ACTIVE1, UP, DOWN)
    layer(1, SELFN)
    share_act(SELFN)
    kv_copies = {}
    for index, dst in ((KW, 0), (VW, 1), (QW, None)):
        w_now = weight(index)

        def project(cols, dst=dst, w_now=w_now):
            value = dot(acts[act(SELFN), :], w_now[:, cols]).astype(BF)
            if dst is None:
                qbuf[:, cols] = value
            else:
                kv[dst, 0, :, cols] = value
        columns_loop(project)
        weight_done()
        if dst is not None:
            kv_copies[dst] = remote(kv.at[dst, 0], kv.at[dst, 1], peer)
    spill.wait()
    kv_copies[0].wait_recv()
    kv_copies[1].wait_recv()

    def heads(body):
        def run(pair, carry):
            for side in range(2):
                cols = pl.ds(pl.multiple_of((2 * pair + side) * head_width, head_width), head_width)
                rows = pl.ds(pl.multiple_of((pair % 2) * count, count), count)
                body(cols, (pl.ds(pair // 2, 1), rows, pl.ds(side * lat, lat)))
            return carry
        lax.fori_loop(0, HEADS // 2, run, 0)

    def attend(cols, keep):
        keys = kv[0, :, :, cols].reshape(lat, head_width)
        values = kv[1, :, :, cols].reshape(lat, head_width)
        scores = dot_nt(qbuf[:, cols], keys) * self_scale
        scores = jnp.where(idcol == idrow[...], scores, NEGATIVE)
        weights = jnp.exp(scores - jnp.max(scores, axis=1, keepdims=True))
        prob = (weights * (1.0 / jnp.sum(weights, axis=1, keepdims=True))).astype(BF)
        pbuf[keep] = prob[None]
        acts[act(MIXED), cols] = dot(prob, values).astype(BF)
    heads(attend)
    share_act(MIXED)
    w_so = weight(SO)

    def three_cols(cols):
        stream[:, cols] += dot(acts[act(MIXED), :], w_so[:, cols])
    columns_loop(three_cols)
    weight_done()
    mlp(2, NORMED2, ACTIVE2, UPB, DOWNB)
    dmix[...] = stream[...].astype(BF)
    lat_ref[pl.ds(chip, 1)] = dmix[pl.ds(pl.multiple_of(chip * block, block), block), :][None]
    lat_copy = remote(
        dmix.at[pl.ds(pl.multiple_of((1 - chip) * block, block), block)], lat_ref.at[chip], across
    )

    weight_grad(DOWN2)
    tick(2.0)

    def mlp_back(k, normed, active, m_down, m_up, up_id, down_id, into, start=None):
        w_down = weight(down_id)

        def act_cols(cols):
            grad = dot_nt(gall[m_down, 0], w_down[cols, :]).astype(BF).astype(F32)
            gall[m_up, 0, :, cols] = (grad * slopes[active // 4, :, cols].astype(F32)).astype(BF)
        columns_loop(act_cols)
        weight_done()
        share_grad(m_up)
        tick(1.0)
        w_up = weight(up_id)

        def norm_cols(cols):
            dnorm[:, cols] = dot_nt(gall[m_up, 0], w_up[cols, :])
        columns_loop(norm_cols)
        weight_done()
        if into == 0:
            grad_copies[DOWN2].wait_send()
            grad_copies[UP2].wait_send()
        layer_back(k, normed, into, start)
        tick(1.5)

    mlp_back(2, NORMED2, ACTIVE2, DOWN2, UP2, UPB, DOWNB, SOUT, DOWN2)

    share_grad(SOUT)
    weight_grad(UP2)
    tick(1.5)
    w_so2 = weight(SO)
    lat_copy.wait_send()

    def mixed_cols(cols):
        dmix[:, cols] = dot_nt(gall[SOUT, 0], w_so2[cols, :]).astype(BF)
    columns_loop(mixed_cols)
    weight_done()

    def attend_back(cols, keep):
        keys = kv[0, :, :, cols].reshape(lat, head_width)
        values = kv[1, :, :, cols].reshape(lat, head_width)
        dm = dmix[:, cols]
        prob_b = pbuf[keep][0]
        prob = prob_b.astype(F32)
        grad = dot_nt(dm, values)
        delta = jnp.sum(prob * grad, axis=1, keepdims=True)
        score = (prob * (grad - delta)).astype(BF)
        gall[SQ, 0, :, cols] = (dot(score, keys) * self_scale).astype(BF)
        dk = (dot_tn(score, qbuf[:, cols]) * self_scale).astype(BF)
        dv = dot_tn(prob_b, dm).astype(BF)
        gall[SK, 0, :, cols] = dk[:count]
        gall[SV, 0, :, cols] = dv[:count]
        kv[0, 1, :, cols] = dk[count:]
        kv[1, 1, :, cols] = dv[count:]
    heads(attend_back)
    unspill = local(pspill, pbuf, 4)
    share_dkv = remote(kv.at[:, 1], dkv_in, peer)
    share_grad(SQ)
    tick(4.0)
    weight_grad(SOUT)
    tick(1.0)
    share_dkv.wait_recv()

    def add_kv(rows):
        for at, m in ((0, SK), (1, SV)):
            gall[m, 0, rows, :] = gall[m, 0, rows, :] + dkv_in[at, rows, :]
    rows_loop(add_kv)
    share_grad(SK)
    share_grad(SV)
    for at, (m, index) in enumerate(((SQ, QW), (SK, KW), (SV, VW))):
        w_now = weight(index)

        def normed_cols(cols, at=at, m=m, w_now=w_now):
            value = dot_nt(gall[m, 0], w_now[cols, :])
            if at == 0:
                dnorm[:, cols] = value
            else:
                dnorm[:, cols] += value
        columns_loop(normed_cols)
        weight_done()
    layer_back(1, SELFN, DOWN1)
    share_grad(DOWN1)
    tick(3.0)
    weight_grad(SQ)
    tick(1.0)
    weight_grad(SK)
    tick(1.0)
    mlp_back(0, NORMED1, ACTIVE1, DOWN1, UP1, UP, DOWN, 0)

    w_o = weight(WO)

    def attended_back(cols):
        gall[1, 0, :, cols] = dot_nt(gall[0, 0], w_o[cols, :]).astype(BF)
    columns_loop(attended_back)
    weight_done()
    share_cd = remote(gall.at[1 - core, 0], gcd_in, peer)
    folded = jnp.concatenate([dot_nt(gall[1, 0], wkv[:MAIN, :]), dot_nt(gall[1, 0], w_rest[...])], axis=1)
    along = jnp.sum(folded * amix[...].astype(F32), axis=0, keepdims=True)
    gsum[3:4, :FEAT_PAD] = along
    gsum[3:4, FEAT_PAD:] = jnp.zeros((1, width - FEAT_PAD), F32)
    da_all[pl.ds(chip, 1), :, pl.ds(core, 1)] = folded.astype(BF).reshape(1, 2, 1, block, FEAT_PAD)
    mine = da_all.at[chip, :, core]
    da_across = remote(mine, mine, across)
    da_peer = remote(mine, mine, peer)
    tick(2.0)
    weight_grad(SV)
    tick(1.0)
    da_across.wait_recv()
    other = da_all.at[1 - chip, :, core]
    da_other = remote(other, other, peer)
    weight_grad(DOWN1)
    tick(1.0)
    weight_grad(UP1)
    tick(1.0)

    share_cd.wait_recv()
    amix_copy.wait_recv()
    lefts = jnp.concatenate([amix[:, :MAIN], amix_in[:, :MAIN]], axis=0)
    grads = jnp.concatenate([gall[pl.ds(core, 1), 0][0], gcd_in[...]], axis=0)
    total = dot_tn(lefts, grads).astype(BF)
    for plane in range(2):
        store_plane(MATS, plane, 0, total[plane * LANES : (plane + 1) * LANES])
    for plane in range(2):
        store_plane(MATS, plane, 1, upstr[plane * block : (plane + 1) * block, :].astype(BF))
    begin_unit(MATS)
    gsum[4:, :] = jnp.zeros((gsum.shape[0] - 4, width), F32)
    rests = [dot_tn(amix[:, MAIN:], gall[side, 0])[:8] for side in range(2)]
    for i in range(8):
        cols = slice(i * LANES, (i + 1) * LANES)
        both = jnp.concatenate([rests[0][:, cols], rests[1][:, cols]], axis=0)
        sm[16 * i : 16 * (i + 1), FEAT_PAD:] = both.astype(BF)
        sm[128 + 16 * i : 128 + 16 * (i + 1), FEAT_PAD:] = gsum[:, cols].astype(BF)
    sm[256:, FEAT_PAD:] = jnp.zeros((lat - 256, LANES), BF)
    tick(2.0)

    da_peer.wait_recv()
    da_other.wait_recv()
    unspill.wait()

    def score_rows(s):
        return wslots.at[s, pl.ds(0, lat)]

    def da_rows(s):
        return wslots.at[s, pl.ds(lat, lat), pl.ds(0, CAT)]

    def q_rows(s):
        return wslots.at[2, pl.ds(s * lat, lat), pl.ds(0, CAT)]

    for s in range(2):
        for i in range(4):
            rows = pl.ds(i * block, block)
            wslots[s, lat + i * block : lat + (i + 1) * block, :CAT] = spread_out(
                da_all[s, i // 2, i % 2], s, rows
            )
            wslots[2, s * lat + i * block : s * lat + (i + 1) * block, :CAT] = spread_out(
                fold[rows, :], s, rows
            )

        def back_cols(cols, s=s):
            fbuf[:, cols] = dot(wslots[s, lat:, :CAT], xcat[s, :, cols])
        columns_loop(back_cols, 256, slots)

        def score_back(rows, s=s):
            prob = pbuf[s, rows, :].astype(F32)
            grad = fbuf[rows, :]
            delta = jnp.sum(prob * grad, axis=1, keepdims=True)
            wslots[s, rows, :] = (prob * (grad - delta)).astype(BF)
        rows_loop(score_back, 64, lat)
        scores = wslots[s, :lat, :]
        zero = dot_nt(scores, xcat[s, :MAIN, :])
        one = dot_nt(scores, xcat[s, MAIN : 2 * MAIN, :])
        rest = dot_nt(scores, xcat[s, 2 * MAIN :, :])
        main, rest = pull_in(s, pl.ds(0, lat), zero, one, rest)
        if s == 0:
            bsum[:, :MAIN] = main
            bsum[:, MAIN:] = rest
        else:
            sm[:, :MAIN] = (bsum[:, :MAIN] + main).astype(BF)
            sm[:, MAIN:FEAT_PAD] = (bsum[:, MAIN:] + rest).astype(BF)
        tick(4.0)

    small_send()
    for copy in act_copies.values():
        copy.wait_send()
    for s in range(2):
        for at, (lo, size) in enumerate(((0, MAIN), (MAIN, MAIN), (2 * MAIN, LANES))):
            cols = pl.ds(lo, size)
            total = dot_tn(wslots[2, s * lat : (s + 1) * lat, cols], wslots[s, :lat, :])
            total = total + dot_tn(wslots[s, lat:, cols], pbuf[s])
            acts[pl.ds(s * CAT + lo, size), :] = total.astype(BF)
            tick(2.0)

    main_gain, rest_gain = gain_col[:MAIN, :], gain_col[MAIN:, :]
    y_copy = None
    for k in range(2):
        if y_copy is not None:
            y_copy.wait()
        for s in range(2):

            def pixel_step(jb, carry, k=k, s=s):
                cols = pl.ds(pl.multiple_of(jb * LANES, LANES), LANES)
                up_main = acts[s * CAT + k * MAIN : s * CAT + (k + 1) * MAIN, cols].astype(F32)
                up_rest = acts[s * CAT + 2 * MAIN : s * CAT + 2 * MAIN + 16, cols].astype(F32)
                up_rest = up_rest[8 * k : 8 * k + 8]
                x_main = xcat[s, k * MAIN : (k + 1) * MAIN, cols].astype(F32)
                x_rest = xcat[s, 2 * MAIN : 2 * MAIN + 16, cols].astype(F32)[8 * k : 8 * k + 8]
                rs = pixel_rs[pl.ds(k * (group // 2) + 2 * jb + s, 1), :]
                scaled_main, scaled_rest = up_main * main_gain, up_rest * rest_gain

                def mean_of(a, b):
                    whole = jnp.sum(a, axis=0, keepdims=True) + jnp.sum(b, axis=0, keepdims=True)
                    return whole * (1.0 / features)
                centre = mean_of(scaled_main, scaled_rest)
                along = mean_of(up_main * x_main, up_rest * x_rest)
                unit_main, unit_rest = x_main / main_gain, x_rest / rest_gain
                out_main = rs * (scaled_main - centre - unit_main * along)
                out_rest = rs * (scaled_rest - centre - unit_rest * along)
                flat[pl.ds(2 * jb + s, tall, stride=group // 2), :] = jnp.concatenate(
                    [out_main, out_rest], axis=0
                )
                return carry
            lax.fori_loop(0, blocks, pixel_step, 0)
            tick(2.0)
        y_copy = local(flat.at[pl.ds(0, features * group // 2)], y_ref.at[k], 7 + k)
    while next_due() < 1e9:
        serve()
    for g, from_chip, own in gathers:
        from_chip.wait_recv()
        span = pl.ds(2 * g[0], 6 if g[-1] < MATS else 5)
        remote(fin_in.at[span], gat_ref.at[other_row, span], peer)
        own.wait()
        z_local.append(local(fin_in.at[span], gat_ref.at[other_row, span], 9 + g[0] // 3))
    for copy in z_local + [y_copy]:
        copy.wait()
    for copy in copies:
        copy.finish()


def finish_kernel(*refs):
    it = iter(refs)

    def take(n=None):
        return next(it) if n is None else [next(it) for _ in range(n)]

    y_in, lat_in = take(2)
    ins = take(8)
    query_gain, pixel_gain = take(2)
    y_out, lat_out, init_out, pixel_gain_out, key_out, value_out = take(6)
    gain_outs = take(4)
    mat_outs = take(MATS + 2)
    held = take(8)
    summed, small, fold, init_all, wq, wk, wv, init_sum = held
    unit, normed, total, mats, wk_rest, wv_rest, y_buf, lat_buf, back = take(9)
    sem, out_sem = take(2)
    features, width = ins[5].shape
    lat = init_all.shape[0]
    block = lat // 4
    j = lax.axis_index("seq")
    row = lax.axis_index("row")
    cross_scale = 1.0 / math.sqrt(width)

    through = [
        (pltpu.make_async_copy(y_in.at[k], y_buf.at[:, pl.ds(k * y_in.shape[2], y_in.shape[2])], sem.at[8 + k]))
        for k in range(2)
    ] + [pltpu.make_async_copy(lat_in, lat_buf, sem.at[10])]
    copies = []
    for i, (src, dst) in enumerate(zip(ins, held)):
        copies.append(pltpu.make_async_copy(src, dst, sem.at[i]))
        copies[-1].start()
        if i == 0:
            for copy in through:
                copy.start()
    outs = []

    def put(src, dst):
        copy = pltpu.make_async_copy(src, dst, out_sem.at[len(outs)])
        copy.start()
        outs.append(copy)

    copies[0].wait()
    for m in range(MATS):
        for r in range(4):
            for h in range(2):
                at = (r % 2) * (width // 2) + (r // 2) * 2 * LANES + h * LANES
                mats[m, at : at + LANES, :] = summed[r, 2 * m + h].astype(F32)
        put(mats.at[m], mat_outs[m])
    copies[3].wait()
    query_rs = []
    for r in range(4):
        rows = pl.ds(r * block, block)
        value, scale = norm_parts(init_all[rows, :].astype(F32))
        unit[rows, :] = value
        normed[rows, :] = (value * query_gain[...]).astype(BF)
        query_rs.append(scale)
    for copy in through:
        copy.wait()
    put(y_buf, y_out)
    put(lat_buf, lat_out)
    for copy in copies[1:3] + copies[4:]:
        copy.wait()
    fill_rest(wv_rest, wv)
    fill_rest(wk_rest, wk)
    my_cols = pl.ds(pl.multiple_of(j * LANES, LANES), LANES)

    for n in range(width // 256):
        cols = pl.ds(n * 256, 256)
        value = dot(small[:, :MAIN], wk[:MAIN, cols]) + dot(small[:, MAIN:FEAT_PAD], wk_rest[:, cols])
        total[:, cols] = (value * cross_scale).astype(BF)

    def put_turned(index, value):
        for n in range(width // LANES):
            mats[index, n * LANES : (n + 1) * LANES, :] = value[:, n * LANES : (n + 1) * LANES].T
        put(mats.at[index], mat_outs[index])
    put_turned(MATS, dot_tn(total[:, my_cols], normed[...]))
    outer = [
        [summed[2 * y + c, FEATURE_UNIT].astype(F32) for y in range(2)] for c in range(2)
    ]
    rests = small[pl.ds(pl.multiple_of(j * 16, 16), 16), FEAT_PAD:]
    value_out[:LANES, :] = outer[1][0]
    value_out[LANES:MAIN, :] = outer[1][1]
    value_out[MAIN:, :] = rests.astype(F32)[8 : 8 + features - MAIN]
    summed_c = jnp.concatenate(outer[0], axis=0).astype(BF)
    put_turned(MATS + 1, dot_tn(summed_c, wv[:MAIN, :]) + dot_tn(rests, wv_rest[:16, :]))
    my_queries = dot(normed[...], wq[:, my_cols]).astype(BF)
    key_turned = dot_tn(my_queries, small[:, :FEAT_PAD]) * cross_scale
    key_out[...] = jnp.concatenate(
        [key_turned[:, n * LANES : (n + 1) * LANES].T for n in range(3)], axis=0
    )[:features]
    for i in range(8):
        chunk = small[128 + 16 * i : 128 + 16 * (i + 1), FEAT_PAD:].astype(F32)
        for g in range(3):
            gain_outs[g][i : i + 1, :] = chunk[g : g + 1]
    scores = small[:, :FEAT_PAD].astype(F32)
    part = jnp.sum(fold[...].astype(F32) * scores, axis=0, keepdims=True)
    rest_sum = [small[128 + 16 * i : 128 + 16 * (i + 1), FEAT_PAD:].astype(F32)[3:4] for i in range(3)]
    whole = (part + jnp.concatenate(rest_sum, axis=1))[:, :features]
    pixel_gain_out[...] = (whole / pixel_gain[...].reshape(1, features)).reshape(features)
    own = pl.ds(pl.multiple_of(row * block, block), block)
    own_rs = query_rs[0]
    for r in range(1, 4):
        own_rs = jnp.where(row == r, query_rs[r], own_rs)
    sums = jnp.zeros((block, 1), F32)
    alongs = jnp.zeros((block, 1), F32)
    for n in range(width // 256):
        cols = pl.ds(n * 256, 256)
        back[:, cols] = dot_nt(total[...], wq[cols, :])
        row_sum = jnp.sum(back[:, cols] * unit[:, cols], axis=0, keepdims=True)
        for i in range(2):
            gain_outs[3][2 * n + i : 2 * n + i + 1, :] = row_sum[:, i * LANES : (i + 1) * LANES]
        scaled = back[own, cols] * query_gain[:, cols]
        sums = sums + jnp.sum(scaled, axis=1, keepdims=True)
        alongs = alongs + jnp.sum(scaled * unit[own, cols], axis=1, keepdims=True)
    scaled = back[own, my_cols] * query_gain[:, my_cols]
    query_in = own_rs * (scaled - sums * (1.0 / width) - unit[own, my_cols] * (alongs * (1.0 / width)))
    init_out[...] = init_sum[...].astype(F32) + query_in
    for copy in outs:
        copy.wait()


def finish(y, latents, summed, small, init_sum, fold, init_all, wq, wk, wv, query_gain, pixel_gain):
    features, width = wk.shape
    lat = init_all.shape[0]
    block = lat // 4
    vmem = pl.BlockSpec(memory_space=pltpu.VMEM)
    hbm = pl.BlockSpec(memory_space=pl.ANY)

    def f32(*shape):
        return jax.ShapeDtypeStruct(shape, F32)

    outs = pl.pallas_call(
        finish_kernel,
        out_shape=[f32(features, 2 * y.shape[2], LANES), jax.ShapeDtypeStruct(latents.shape, BF), f32(block, LANES),
                   f32(features), f32(features, LANES), f32(features, LANES)]
        + [f32(width // LANES, LANES)] * 4 + [f32(width, LANES)] * (MATS + 2),
        in_specs=[hbm] * 10 + [vmem] * 2,
        out_specs=[hbm] * 2 + [vmem] * 8 + [hbm] * (MATS + 2),
        scratch_shapes=[
            pltpu.VMEM(shape, BF)
            for shape in (summed.shape, small.shape, fold.shape, init_all.shape,
                          wq.shape, wk.shape, wv.shape, init_sum.shape)
        ]
        + [
            pltpu.VMEM((lat, width), F32),
            pltpu.VMEM((lat, width), BF),
            pltpu.VMEM((lat, width), BF),
            pltpu.VMEM((MATS + 2, width, LANES), F32),
            pltpu.VMEM((LANES, width), BF),
            pltpu.VMEM((LANES, width), BF),
            pltpu.VMEM((features, 2 * y.shape[2], LANES), F32),
            pltpu.VMEM(latents.shape, BF),
            pltpu.VMEM((lat, width), F32),
            pltpu.SemaphoreType.DMA((11,)),
            pltpu.SemaphoreType.DMA((MATS + 4,)),
        ],
        compiler_params=pltpu.CompilerParams(vmem_limit_bytes=VMEM_LIMIT),
    )(y, latents, summed, small, fold, init_all, wq, wk, wv, init_sum, query_gain[None],
      pixel_gain)
    y, latents, init_grad, pixel_gain_grad, key_grad, value_grad = outs[:6]
    return (y, latents, init_grad, outs[6:10], pixel_gain_grad, key_grad, value_grad, outs[10:])


def whole_stack(shards, z, pixel_gain, pseg, init, cots, seg, wk, wv, gains, weights):
    width = init.shape[1]
    block = init.shape[0]
    count = 2 * block
    lat = 2 * count
    share = width // shards
    half = width // 2
    bits = shards.bit_length() - 1
    orders = unit_orders(bits)
    nslots = 3
    features = wk.shape[0]
    group = z.shape[0] // features
    slots = group * LANES // 4
    small, size = [], lat
    for i in range(bits + 2):
        size = size // 2 if size > 16 else size
        small.append((size, 512))
    scratch = [
        ((nslots, width, width), BF),
        (wk.shape, BF),
        ((LANES, width), BF),
        ((2, block, width), BF),
        ((2, 2, block, FEAT_PAD), BF),
        ((2, block, FEAT_PAD), BF),
        ((2, block, FEAT_PAD), BF),
        ((count, FEAT_PAD), BF),
        ((count, FEAT_PAD), BF),
        ((2, 2, 2, block, FEAT_PAD), BF),
        ((lat, width), F32),
        ((3, count, LANES), F32),
        ((6 * count, width), BF),
        ((6, count, half), BF),
        ((2, count, width), BF),
        ((count, width), BF),
        ((2, 2, count, width), BF),
        ((2, lat, slots), BF),
        ((count, width), BF),
        ((2, count, width), BF),
        ((MATS, 2, count, width), BF),
        ((count, width), BF),
        ((FEATURE_UNIT + 1, share, LANES), BF),
        ((2, 2, 2, block, FEAT_PAD), BF),
        ((lat, FEAT_PAD), F32),
        ((16, width), F32),
        ((1, lat), F32),
        ((lat, 512), BF),
        ((2, CAT, slots), BF),
        (((MAIN + 8) * group // 2, LANES), F32),
        ((2, 8, slots), F32),
        ((group, LANES), F32),
        ((MAIN + 8, LANES), F32),
        ((FEATURE_UNIT + 1, share, LANES), BF),
        ((UNITS * 4, width, LANES), BF),
    ]
    for order in orders:
        scratch += [(shape, BF) for shape in stage_shapes(order, width)]
    scratch += [(shape, BF) for shape in small]
    stages = sum(len(order) for order in orders)
    vmem = pl.BlockSpec(memory_space=pltpu.VMEM)
    hbm = pl.BlockSpec(memory_space=pl.ANY)
    return pl.pallas_call(
        functools.partial(
            main_kernel, (shards, width, count, dict(small_stages=len(small)))
        ),
        out_shape=[
            jax.ShapeDtypeStruct((2, block, width), BF),
            jax.ShapeDtypeStruct((lat, 512), BF),
            jax.ShapeDtypeStruct((4, FEATURE_UNIT + 1, share, LANES), BF),
            jax.ShapeDtypeStruct((share, LANES), BF),
            jax.ShapeDtypeStruct((lat, FEAT_PAD), BF),
            jax.ShapeDtypeStruct((4, block, width), BF),
            jax.ShapeDtypeStruct((2, features * group // 2, LANES), F32),
            jax.ShapeDtypeStruct((2, lat, slots), BF),
        ],
        in_specs=[hbm, pl.BlockSpec(memory_space=pltpu.SMEM), vmem, vmem, hbm, vmem]
        + [hbm] * 2 + [vmem] * 4 + [hbm] * 10,
        out_specs=[vmem, vmem, hbm, vmem, vmem, hbm, hbm, hbm],
        scratch_shapes=[pltpu.VMEM(shape, kind) for shape, kind in scratch]
        + [
            pltpu.SemaphoreType.DMA((nslots + 2 + 13,)),
            pltpu.SemaphoreType.DMA((nslots * 4,)),
            pltpu.SemaphoreType.DMA((-(-z.shape[0] // width),)),
            pltpu.SemaphoreType.DMA((stages,)),
            pltpu.SemaphoreType.DMA((stages,)),
            pltpu.SemaphoreType.DMA((80,)),
            pltpu.SemaphoreType.DMA((80,)),
        ],
        compiler_params=pltpu.CompilerParams(
            collective_id=0, has_side_effects=True, vmem_limit_bytes=VMEM_LIMIT
        ),
    )(z, pixel_gain, pseg, init, cots, seg, wk, wv, *[g[None] for g in gains], *weights)


VMEM_LIMIT = 63 * 1024 * 1024


def body(
    pixels, pixel_seg, latent_seg, latent_init, cotangent,
    pixel_gain, query_gain, query_weight, key_weight, value_weight, output_weight,
    mlp_gain, up_weight, down_weight,
    self_gain, self_query, self_key, self_value, self_output,
    second_gain, second_up, second_down,
):
    seqs, pix, features = pixels.shape
    block, width = latent_init.shape
    shards = lax.axis_size("seq")
    lat = block * lax.axis_size("row")
    row = lax.axis_index("row")
    cross_scale = 1.0 / math.sqrt(width)
    tiles = pix // LANES

    z = pixels.transpose(2, 0, 1).reshape(features, seqs, tiles, LANES)
    z = z.transpose(0, 2, 1, 3).reshape(features * seqs * tiles, LANES)
    latents, small, summed, init_sum, fold, init_all, y, unused = whole_stack(
        shards, z, pixel_gain, pixel_seg, latent_init, cotangent, latent_seg, key_weight, value_weight,
        (mlp_gain, self_gain, second_gain, query_gain),
        (query_weight, output_weight, up_weight, down_weight, self_query, self_key, self_value,
         self_output, second_up, second_down),
    )
    init_all = init_all.reshape(lat, width)
    y = y.reshape(2, features, tiles, LANES)
    if width // shards == LANES:
        y, latents, init_grad, gains, pixel_gain_grad, key_grad, value_grad, mats = finish(
            y, latents, summed, small, init_sum, fold, init_all, query_weight, key_weight,
            value_weight, query_gain, pixel_gain,
        )
    else:
        y = y.transpose(1, 0, 2, 3)
    pixel_grad = y.reshape(features, tiles, seqs, LANES).transpose(2, 1, 3, 0)
    pixel_grad = pixel_grad.reshape(seqs, pix, features)
    if width // shards == LANES:
        mlp_gain_grad, self_gain_grad, second_gain_grad, query_gain_grad = [
            g.reshape(width) for g in gains
        ]
        return (
            latents, pixel_grad, init_grad, pixel_gain_grad,
            query_gain_grad, mlp_gain_grad, self_gain_grad, second_gain_grad,
            mats[MATS], key_grad, value_grad, mats[MATS + 1], mats[UP1], mats[DOWN1],
            mats[SQ], mats[SK], mats[SV], mats[SOUT], mats[UP2], mats[DOWN2],
        )

    share = width // shards
    at = lax.axis_index("seq") * share

    def columns(arr):
        return lax.dynamic_slice_in_dim(arr, at, share, arr.ndim - 1)

    score_b = small[:, :features]
    side = small[:, FEAT_PAD:]
    rests = side[:128].reshape(8, 2, 8, LANES).transpose(1, 2, 0, 3).reshape(2, 8, width)
    sums = side[128:256].reshape(8, 16, LANES).transpose(1, 0, 2).reshape(16, width).astype(F32)
    pixel_gain_grad = (
        jnp.sum(fold[:, :features].astype(F32) * score_b.astype(F32), axis=0) + sums[3, :features]
    ) / pixel_gain
    units = summed.reshape(2, 2, FEATURE_UNIT + 1, share, LANES)
    mats = units[:, :, :FEATURE_UNIT].reshape(2, 2, MATS, 2, share, LANES)
    mats = mats.transpose(2, 1, 0, 3, 5, 4).reshape(MATS, width, share).astype(F32)
    outer = units[:, :, FEATURE_UNIT].transpose(1, 0, 3, 2).reshape(2, MAIN, share)
    outer = jnp.concatenate([outer, columns(rests)[:, : features - MAIN]], axis=1)
    value_grad = outer[1].astype(F32)
    output_grad = dot_tn(value_weight, outer[0])
    query_unit, query_rs = norm_parts(init_all.astype(F32))
    query_normed = (query_unit * query_gain).astype(BF)
    my_queries = dot(query_normed, columns(query_weight)).astype(BF)
    key_grad = dot_tn(score_b, my_queries) * cross_scale
    query_total = (dot(score_b, key_weight) * cross_scale).astype(BF)
    query_grad = dot_tn(query_normed, columns(query_total))
    query_in, query_gain_grad = norm_back(
        query_unit, query_rs, query_gain, dot_nt(query_total, query_weight)
    )
    init_grad = init_sum.T.astype(F32) + lax.dynamic_slice(query_in, (row * block, at), (block, share))
    return (
        latents, pixel_grad, init_grad,
        pixel_gain_grad, query_gain_grad, sums[0], sums[1], sums[2],
        query_grad, key_grad, value_grad, output_grad, mats[UP1], mats[DOWN1],
        mats[SQ], mats[SK], mats[SV], mats[SOUT], mats[UP2], mats[DOWN2],
    )


def solution(mesh):
    placed = (
        P("seq", "row", None), P("seq", "row"), P("seq", "row"), P("row", None),
        P("seq", "row", None),
    ) + (P(),) * 17
    cols = P(None, "seq")
    return jax.shard_map(
        body,
        mesh=mesh,
        in_specs=placed,
        out_specs=(P("seq", "row", None), P("seq", "row", None), P("row", "seq"))
        + (P(),) * 5 + (cols,) * 12,
        check_vma=False,
    )
```

```python
import functools
import math

import jax
import jax.numpy as jnp
from jax import lax
from jax.experimental import pallas as pl
from jax.experimental.pallas import tpu as pltpu
from jax.sharding import PartitionSpec as P

HEADS = 8
EPSILON = 1e-05
NEGATIVE = -1e9
BF = jnp.bfloat16
F32 = jnp.float32
LANES = 128
FEAT_PAD = 384
MAIN = 256
CAT = 2 * MAIN + LANES
MESH = pl.DeviceIdType.MESH


def dot(a, b):
    return jnp.dot(a, b, preferred_element_type=F32)


def dot_tn(a, b):
    return lax.dot_general(a, b, (((0,), (0,)), ((), ())), preferred_element_type=F32)


def dot_nt(a, b):
    return lax.dot_general(a, b, (((1,), (1,)), ((), ())), preferred_element_type=F32)


def fill_rest(rest, matrix):
    rest[...] = jnp.zeros(rest.shape, rest.dtype)
    rest[: matrix.shape[0] - MAIN, :] = matrix[MAIN:, :]


def norm_parts(values):
    centre = values - jnp.mean(values, axis=-1, keepdims=True)
    rs = lax.rsqrt(jnp.mean(centre * centre, axis=-1, keepdims=True) + EPSILON)
    return centre * rs, rs


def norm_back(unit, rs, gain, upstream):
    scaled = upstream * gain
    grad = rs * (
        scaled
        - jnp.mean(scaled, axis=-1, keepdims=True)
        - unit * jnp.mean(scaled * unit, axis=-1, keepdims=True)
    )
    return grad, jnp.sum(upstream * unit, axis=0)


def gelu_parts(hidden):
    cdf = 0.5 * (1.0 + lax.erf(hidden * math.sqrt(0.5)))
    pdf = jnp.exp(-0.5 * hidden * hidden) * (1.0 / math.sqrt(2.0 * math.pi))
    return hidden * cdf, cdf + hidden * pdf


NORMED1, ACTIVE1, SELFN, MIXED, NORMED2, ACTIVE2 = range(6)
DOWN2, UP2, SOUT, SQ, SK, SV, DOWN1, UP1 = range(8)
LEFT = {
    DOWN2: ACTIVE2, UP2: NORMED2, SOUT: MIXED, SQ: SELFN, SK: SELFN, SV: SELFN,
    DOWN1: ACTIVE1, UP1: NORMED1,
}
MATS = 8
FEATURE_UNIT = 2 * MATS
UNITS = MATS + 1


class Remote:
    def __init__(self, log, src, dst, send_sem, recv_sem, device):
        self.copy = pltpu.make_async_remote_copy(
            src_ref=src, dst_ref=dst, send_sem=send_sem, recv_sem=recv_sem,
            device_id=device, device_id_type=MESH,
        )
        self.copy.start()
        self.arrived = self.sent = False
        log.append(self)

    def wait_recv(self):
        if not self.arrived:
            self.copy.wait_recv()
        self.arrived = True

    def wait_send(self):
        if not self.sent:
            self.copy.wait_send()
        self.sent = True

    def finish(self):
        self.wait_recv()
        self.wait_send()


KINDS = "FCDABCEBA"


def unit_orders(bits):
    first, second, tail = [0], list(range(1, min(bits, 2))), list(range(2, bits))
    kinds = {
        "A": ["y"] + first + second + tail,
        "B": first + second + ["y"] + tail,
        "C": second + first + ["y"] + tail,
        "D": first + ["y"] + second + tail,
        "E": second + ["y"] + first + tail,
        "F": ["y"] + second + first + tail,
    }
    return [kinds[letter] for letter in KINDS]


def stage_shapes(order, width):
    shapes, planes, size = [], 4, width
    for axis in order:
        if axis == "y":
            planes = 2
        else:
            size //= 2
        shapes.append((planes, size, LANES))
    return shapes


def main_kernel(cfg, *refs):
    shards, width, count, sizes = cfg
    bits = shards.bit_length() - 1
    share = width // shards
    half = width // 2
    block = count // 2
    lat = 2 * count
    head_width = width // HEADS
    cross_scale = 1.0 / math.sqrt(width)
    self_scale = 1.0 / math.sqrt(head_width)
    orders = unit_orders(bits)
    it = iter(refs)

    def take(n=None):
        return next(it) if n is None else [next(it) for _ in range(n)]

    (z_hbm, pixel_gain, pseg_ref, init_ref, cot_hbm, seg_ref, wk_hbm, wv_hbm) = take(8)
    gain_refs = take(4)
    w_hbm = take(10)
    (lat_ref, sm_out, gat_ref, initg_ref, fold, zall, y_ref, pspill) = take(8)
    (wslots, wkv, w_rest, zbuf, ain1, asum, ain2, amix, amix_in, amat, fbuf, rsb, acts, acts_in, slopes,
     qbuf, kv, pbuf, dmix, dkv_in, gall, gcd_in, fin, da_all, bsum, gsum, idrow,
     sm, xcat, flat, rest0, pixel_rs, gain_col, fin_in, part) = take(35)
    recv = [take(len(orders[u])) for u in range(UNITS)]
    smr = take(sizes["small_stages"])
    (wsem, psem, zsem, usend, urecv, csend, crecv, hsend, hrecv) = take(9)

    j = lax.axis_index("seq")
    row = lax.axis_index("row")
    core, chip = row % 2, row // 2
    peer = {"row": row + 1 - 2 * core}
    across = {"row": row + 2 - 4 * chip}
    diagonal = {"row": 3 - row}
    bit_of = [(j // (1 << b)) % 2 for b in range(bits)]
    partner = {b: {"seq": j + (1 - 2 * bit_of[b]) * (1 << b)} for b in range(bits)}
    partner["y"] = across
    stream = fbuf.at[pl.ds(0, count)]
    upstr = fbuf.at[pl.ds(count, count)]
    dnorm = stream

    def act(k):
        return pl.ds(k * count, count)

    WQ, WO, UP, DOWN, QW, KW, VW, SO, UPB, DOWNB = range(10)
    uses = [WQ, WO, UP, DOWN, KW, VW, QW, SO, UPB, DOWNB, DOWNB, UPB, SO, QW, KW, VW, DOWN, UP, WO]
    nslots = wslots.shape[0]
    at_use = [0]

    pieces = 4

    class WeightCopy:
        def __init__(self, i):
            size = width // pieces
            self.copies = [
                pltpu.make_async_copy(
                    w_hbm[uses[i]].at[pl.ds(p * size, size)],
                    wslots.at[i % nslots, pl.ds(p * size, size)],
                    psem.at[(i % nslots) * pieces + p],
                )
                for p in range(pieces)
            ]

        def start(self):
            for copy in self.copies:
                copy.start()

        def wait(self):
            for copy in self.copies:
                copy.wait()

    def weight_copy(i):
        return WeightCopy(i)

    def weight(expect):
        i = at_use[0]
        assert uses[i] == expect
        at_use[0] += 1
        weight_copy(i).wait()
        return wslots.at[i % nslots]

    def weight_done():
        i = at_use[0] - 1 + nslots
        if i < len(uses):
            weight_copy(i).start()

    features = wk_hbm.shape[0]
    pixel_copies = []
    for i, lo in enumerate(range(0, z_hbm.shape[0], width)):
        rows = min(width, z_hbm.shape[0] - lo)
        pixel_copies.append(pltpu.make_async_copy(
            z_hbm.at[pl.ds(lo, rows)], part.at[i, pl.ds(0, rows)], zsem.at[i]
        ))
    weight_copy(0).start()
    wk_copy = pltpu.make_async_copy(wk_hbm, wkv, wsem.at[nslots])
    wk_copy.start()
    for i in range(1, nslots):
        weight_copy(i).start()
    wv_copy = pltpu.make_async_copy(wv_hbm, wkv, wsem.at[nslots + 1])
    for copy in pixel_copies:
        copy.start()

    barrier = pltpu.get_barrier_semaphore()
    partners = [peer, across, diagonal] + [partner[b] for b in range(bits)]
    for p in partners:
        pl.semaphore_signal(barrier, inc=1, device_id=p, device_id_type=MESH)
    copies = []
    slot_count = [0]

    def remote(src, dst, device):
        slot = slot_count[0]
        slot_count[0] += 1
        return Remote(copies, src, dst, csend.at[slot], crecv.at[slot], device)

    def local(src, dst, slot):
        copy = pltpu.make_async_copy(src, dst, wsem.at[nslots + 2 + slot])
        copy.start()
        return copy

    def rows_loop(body, step=64, total=None):
        def run(i, carry):
            body(pl.ds(pl.multiple_of(i * step, step), step))
            return carry
        lax.fori_loop(0, (total or count) // step, run, 0, unroll=2)

    def columns_loop(body, step=256, total=width):
        def run(i, carry):
            body(pl.ds(pl.multiple_of(i * step, step), step))
            return carry
        lax.fori_loop(0, total // step, run, 0, unroll=2)

    def layer(k, into):
        def body(rows):
            unit, rs = norm_parts(stream[rows, :])
            rsb[k, rows, :] = jnp.broadcast_to(rs, (rs.shape[0], LANES))
            place = pl.ds(pl.multiple_of(into * count + rows.start, rows.size), rows.size)
            acts[place, :] = (unit * gain_refs[k][...]).astype(BF)
        rows_loop(body)

    def layer_back(k, normed, into, start=None):
        gain = gain_refs[k][...]
        inverse = 1.0 / gain

        def body(i, total):
            rows = pl.ds(pl.multiple_of(i * 64, 64), 64)
            place = pl.ds(pl.multiple_of(normed * count + i * 64, 64), 64)
            dn = dnorm[rows, :]
            unit = acts[place, :].astype(F32) * inverse
            scaled = dn * gain
            rs = rsb[k, rows, :][:, :1]
            mean = jnp.mean(scaled, axis=-1, keepdims=True)
            along = jnp.mean(scaled * unit, axis=-1, keepdims=True)
            before = upstr[rows, :] if start is None else gall[start, 0, rows, :].astype(F32)
            after = before + rs * (scaled - mean - unit * along)
            upstr[rows, :] = after
            gall[into, 0, rows, :] = after.astype(BF)
            return total + jnp.sum(dn * unit, axis=0, keepdims=True)
        gsum[pl.ds(k, 1), :] = lax.fori_loop(
            0, count // 64, body, jnp.zeros((1, width), F32), unroll=2
        )

    act_copies, grad_copies = {}, {}

    def share_act(k):
        away = pl.ds(pl.multiple_of((1 - core) * half, half), half)
        act_copies[k] = remote(acts.at[act(k), away], acts_in.at[k], peer)

    def share_grad(m):
        grad_copies[m] = remote(gall.at[m, 0], gall.at[m, 1], peer)

    clock = [0.0]
    small = dict(lo=0, size=lat, stage=0, up=[], copy=None, due=1e9)
    axes = [(core, peer), (chip, across)] + [(bit_of[b], partner[b]) for b in range(bits)]

    def small_send():
        bit, device = axes[small["stage"]]
        size = small["size"]
        if size > 16:
            size //= 2
            away = pl.multiple_of(small["lo"] + (1 - bit) * size, 16)
            keep = pl.multiple_of(small["lo"] + bit * size, 16)
            small["up"].append((device, keep, size))
            small["lo"], small["size"] = keep, size
        else:
            away = small["lo"]
        small["copy"] = remote(sm.at[pl.ds(away, size)], smr[small["stage"]], device)
        small["due"] = clock[0] + 2.5 + size * 512 * 4 / 75e3

    def small_grow():
        device, lo, size = small["up"].pop()
        rows = pl.ds(lo, size)
        small["copy"] = remote(sm_out.at[rows], sm_out.at[rows], device)
        small["due"] = clock[0] + 2.5 + size * 512 * 4 / 75e3

    def small_step():
        copy, size = small["copy"], small["size"]
        copy.wait_recv()
        if small["stage"] < len(axes):
            copy.wait_send()
            rows = pl.ds(small["lo"], size)
            sm[rows, :] = sm[rows, :] + smr[small["stage"]][...]
            small["stage"] += 1
            if small["stage"] < len(axes):
                small_send()
                return
            sm_out[rows, :] = sm[rows, :]
        if small["up"]:
            small_grow()
        else:
            small["due"] = 1e9

    state = {}
    free = {}
    pending = []

    def region(u, planes, lo, size):
        if planes == 4:
            return part.at[pl.ds(4 * u, 4), pl.ds(lo, size)]
        return part.at[pl.ds(4 * u + 2 * chip, 2), pl.ds(lo, size)]

    def send_stage(u):
        s = state[u]
        axis = orders[u][s["stage"]]
        k = s["stage"]
        if axis == "y":
            src = part.at[pl.ds(4 * u + 2 - 2 * chip, 2), pl.ds(s["lo"], s["size"])]
            s["planes"] = 2
        else:
            size = s["size"] // 2
            keep = s["lo"] + bit_of[axis] * size
            away = s["lo"] + (1 - bit_of[axis]) * size
            src = region(u, s["planes"], pl.multiple_of(away, share), size)
            s["lo"], s["size"] = pl.multiple_of(keep, share), size
        slot = sum(len(orders[v]) for v in range(u)) + k
        s["copy"] = Remote(copies, src, recv[u][k], usend.at[slot], urecv.at[slot], partner[axis])
        took = s["size"] * s["planes"] * LANES * 2 * 2 / 80e3
        links = {"y": {"y": 1}, 0: {"x": 1}, 1: {"inner": 1}}.get(axis, {"inner": 1, "middle": 2})
        begin = max([clock[0]] + [free.get(link, 0.0) for link in links])
        for link, share_of in links.items():
            free[link] = begin + took * share_of
        s["due"] = max(free[link] for link in links) + 4.0
        pending.append(u)

    def finish_stage(u):
        s = state[u]
        k = s["stage"]
        s["copy"].wait_recv()
        last = k == len(orders[u]) - 1
        mine = pl.ds(4 * u, 4) if s["planes"] == 4 else pl.ds(4 * u + 2 * chip, 2)
        if last:
            total = part[mine, pl.ds(s["lo"], s["size"])] + recv[u][k][...]
            if u == MATS:
                fin[FEATURE_UNIT] = total[0]
                initg_ref[...] = total[1]
            else:
                fin[2 * u : 2 * u + 2] = total
            s["done"] = True
            done_units.append(u)
            gather_ready()
            return
        step = min(s["size"], 256)

        def add(i, carry):
            off = pl.multiple_of(i * step, step)
            rows = pl.ds(pl.multiple_of(s["lo"] + off, share), step)
            part[mine, rows, :] = part[mine, rows, :] + recv[u][k][:, pl.ds(off, step), :]
            return carry
        lax.fori_loop(0, s["size"] // step, add, 0)
        s["stage"] += 1
        send_stage(u)

    done_units, gathers, forwards = [], [], []
    groups = [[0, 1, 2], [3, 4, 5], [6, 7, 8]]

    def gather_ready():
        while len(gathers) < len(groups) and all(u in done_units for u in groups[len(gathers)]):
            g = groups[len(gathers)]
            span = pl.ds(2 * g[0], 6 if g[-1] < MATS else 5)
            from_chip = remote(fin.at[span], fin_in.at[span], across)
            remote(fin.at[span], gat_ref.at[row, span], peer)
            own = local(fin.at[span], gat_ref.at[row, span], len(gathers))
            gathers.append((span, from_chip, own))
            forwards.append((clock[0] + 8.0, len(gathers) - 1))

    def forward(at):
        span, from_chip, own = gathers[at]
        from_chip.wait_recv()
        remote(fin_in.at[span], gat_ref.at[other_row, span], peer)
        own.wait()
        z_local.append(local(fin_in.at[span], gat_ref.at[other_row, span], 9 + at))

    def serve():
        at = min((state[u]["due"], u) for u in pending) if pending else (1e9, None)
        if forwards and forwards[0][0] <= min(at[0], small["due"]):
            forward(forwards.pop(0)[1])
        elif small["due"] <= at[0]:
            clock[0] = max(clock[0], small["due"])
            small_step()
        else:
            clock[0] = max(clock[0], at[0]) + 0.3
            pending.remove(at[1])
            finish_stage(at[1])

    def next_due():
        return min([small["due"]] + [f[0] for f in forwards] + [state[u]["due"] for u in pending])

    def tick(us):
        clock[0] += 1.6 * us
        while next_due() <= clock[0]:
            serve()

    def begin_unit(u):
        state[u] = dict(stage=0, planes=4, lo=0, size=width, done=False)
        send_stage(u)

    def position(u, block):
        seq_bits = [a for a in orders[u] if a != "y"]
        pos = 0
        for at, b in enumerate(seq_bits):
            pos = pos + ((block // (1 << b)) % 2) * (1 << (bits - 1 - at))
        return pos

    def store_plane(u, plane, side, value):
        if share != LANES:
            value = value.astype(F32).T.astype(BF)
        for block_at in range(shards):
            place = pl.ds(position(u, block_at) * share, share)
            if share == LANES:
                part[pl.ds(4 * u + 2 * plane + side, 1), place, :] = value[:, block_at * share : (block_at + 1) * share][None]
            else:
                part[pl.ds(4 * u + 2 * plane + side, 1), place, :] = value[block_at * share : (block_at + 1) * share][None]

    def weight_grad(m):
        left = LEFT[m]
        act_copies[left].wait_recv()
        grad_copies[m].wait_recv()

        def run(plane, carry):
            own = pl.ds(pl.multiple_of(core * half + plane * MAIN, MAIN), MAIN)
            theirs = pl.ds(pl.multiple_of(plane * MAIN, MAIN), MAIN)
            lefts = jnp.concatenate([acts[act(left), own], acts_in[left, :, theirs]], axis=0)
            total = dot_tn(lefts, gall[m].reshape(2 * count, width)).astype(BF)
            store_plane(m, plane, 0, total[:LANES])
            store_plane(m, plane, 1, total[LANES:])
            return carry
        lax.fori_loop(0, 2, run, 0)
        begin_unit(m)

    cot_rows = pl.ds(pl.multiple_of(chip * block, block), block)
    c_own = local(cot_hbm.at[chip], gall.at[DOWN2, 0, cot_rows], 3)
    zbuf[pl.ds(chip, 1)] = init_ref[...][None]
    unit, unused = norm_parts(init_ref[...].astype(F32))
    own_normed = (unit * gain_refs[3][...]).astype(BF)
    w = weight(WQ)
    queries = dot(own_normed, w[...]).astype(BF)
    weight_done()
    wk_copy.wait()
    fill_rest(w_rest, wkv)
    fold_main = dot_nt(queries, wkv[:MAIN, :]) * cross_scale
    fold_rest = dot_nt(queries, w_rest[...]) * cross_scale
    own_rows = pl.ds(pl.multiple_of(row * block, block), block)
    seg = seg_ref[...].astype(F32)
    ids = jnp.concatenate([seg, jnp.zeros((LANES - 2, block), F32)], axis=0).T
    ids = pltpu.roll(ids, 5, 1)
    fold[own_rows, :MAIN] = fold_main.astype(BF)
    fold[own_rows, MAIN:] = (fold_rest + ids).astype(BF)
    wv_copy.start()
    pl.semaphore_wait(barrier, len(partners))
    fold_copies = [remote(fold.at[own_rows], fold.at[own_rows], p) for p in (across, diagonal, peer)]
    z_copy = remote(init_ref, zbuf.at[chip], across)
    c_copy = remote(cot_hbm.at[1 - chip], gall.at[DOWN2, 0, cot_rows], across)
    group = pixel_rs.shape[0]
    blocks = group // 4
    tall = gain_col.shape[0]

    fold_in = width // group

    def pixel_row(f, lo=0, rows=group):
        at = pl.ds(pl.multiple_of((f % fold_in) * group + lo, rows), rows)
        return part[pl.ds(f // fold_in, 1), at, :][0].astype(F32)

    zero = jnp.zeros((group, LANES), F32)
    for copy in pixel_copies:
        copy.wait()
    mean = lax.fori_loop(0, features, lambda f, acc: acc + pixel_row(f), zero, unroll=9)
    mean = mean * (1.0 / features)

    def spread(f, acc):
        centre = pixel_row(f) - mean
        return acc + centre * centre
    spread_sum = lax.fori_loop(0, features, spread, zero, unroll=9)
    rs_all = lax.rsqrt(spread_sum * (1.0 / features) + EPSILON)
    pixel_rs[...] = rs_all
    gain_col[...] = jnp.ones(gain_col.shape, F32)
    flat[features * group // 2 :, :] = jnp.zeros(((tall - features) * group // 2, LANES), F32)
    for s in range(2):
        xcat[s, 2 * MAIN + 16 :, :] = jnp.zeros((LANES - 16, xcat.shape[2]), BF)
    for k in range(2):
        half_rows = slice(k * (group // 2), (k + 1) * (group // 2))
        half_mean, half_rs = mean[half_rows], rs_all[half_rows]

        def scale(f, carry, k=k, half_mean=half_mean, half_rs=half_rs):
            value = pixel_row(f, k * (group // 2), group // 2)
            rows = pl.ds(pl.multiple_of(f * (group // 2), group // 2), group // 2)
            flat[rows, :] = (value - half_mean) * (half_rs * pixel_gain[f])
            if k == 0:
                gain_col[pl.ds(f, 1), :] = jnp.full((1, LANES), pixel_gain[f], F32)
            return carry
        lax.fori_loop(0, features, scale, 0, unroll=9)
        for s in range(2):
            for jb in range(blocks):
                cols = pl.ds(jb * LANES, LANES)
                value = flat[pl.ds(2 * jb + s, tall, stride=group // 2), :]
                xcat[s, k * MAIN : (k + 1) * MAIN, cols] = value[:MAIN].astype(BF)
                if k == 0:
                    rest0[s, :, cols] = value[MAIN:]
                else:
                    both = jnp.concatenate([rest0[s, :, cols], value[MAIN:]], axis=0)
                    xcat[s, 2 * MAIN : 2 * MAIN + 16, cols] = both.astype(BF)
    for copy in fold_copies:
        copy.wait_recv()

    lane = lax.broadcasted_iota(jnp.int32, (1, LANES), 1)
    image = (2 * row).astype(F32)

    def selectors(s, rows):
        ids = fold[rows, MAIN:].astype(F32)
        ids = jnp.where(s == 0, ids[:, 5:6], ids[:, 6:7])
        return jnp.where(ids == image, 1.0, 0.0), jnp.where(ids == image + 1.0, 1.0, 0.0)

    def spread_out(source, s, rows):
        first, second = selectors(s, rows)
        main = source[:, :MAIN].astype(F32)
        rest = jnp.where(lane < 5, source[:, MAIN:].astype(F32), 0.0)
        rest = rest * first + pltpu.roll(rest, 8, 1) * second
        return jnp.concatenate([main * first, main * second, rest], axis=1).astype(BF)

    def pull_in(s, rows, zero, one, rest):
        first, second = selectors(s, rows)
        rest = jnp.where(lane < 5, rest * first + pltpu.roll(rest, LANES - 8, 1) * second, 0.0)
        return zero * first + one * second, rest

    slots = xcat.shape[2]
    core_copies = []

    def send_core(turn):
        core_copies.append(remote(amat.at[turn, :, 1 - core], ain1.at[turn], peer))

    def core_sum(turn):
        core_copies[turn].wait_recv()
        return amat[turn, :, pl.ds(core, 1)][:, 0] + ain1[turn]

    for turn in range(2):
        s = 1 - chip if turn == 0 else chip
        seq = pl.ds(s, 1)
        for i in range(4):
            rows = pl.ds(i * block, block)
            gall[2 + 2 * turn + i // 2, 0, (i % 2) * block : (i % 2 + 1) * block, :CAT] = spread_out(
                fold[rows, :], s, rows
            )
        first_ok = jnp.where(pseg_ref[seq, :slots] == 2 * row, 1.0, 0.0)
        second_ok = jnp.where(pseg_ref[seq, slots:] == 2 * row + 1, 1.0, 0.0)

        def score_cols(cols, seq=seq, turn=turn):
            queries_cat = jnp.concatenate(
                [gall[2 + 2 * turn, 0, :, :CAT], gall[3 + 2 * turn, 0, :, :CAT]], axis=0
            )
            fbuf[:, cols] = dot(queries_cat, xcat[seq, :, cols][0])
        columns_loop(score_cols, 256, slots)
        if turn == 1:
            asum[...] = core_sum(0)
            step2 = remote(asum, ain2, across)

        def soften(rows, s=s, seq=seq, first_ok=first_ok, second_ok=second_ok):
            first, unused = selectors(s, rows)
            allowed = second_ok + first * (first_ok - second_ok)
            scores = jnp.where(allowed > 0.5, fbuf[rows, :], NEGATIVE)
            weights = jnp.exp(scores - jnp.max(scores, axis=1, keepdims=True))
            prob = (weights * (1.0 / jnp.sum(weights, axis=1, keepdims=True))).astype(BF)
            pbuf[seq, rows, :] = prob[None]
        rows_loop(soften, 64, lat)
        probs = pbuf[seq][0]
        zero = dot_nt(probs, xcat[seq, :MAIN, :][0])
        one = dot_nt(probs, xcat[seq, MAIN : 2 * MAIN, :][0])
        rest = dot_nt(probs, xcat[seq, 2 * MAIN :, :][0])
        main, rest = pull_in(s, pl.ds(0, lat), zero, one, rest)
        amat[turn, :, :, :, :MAIN] = main.astype(BF).reshape(2, 2, block, MAIN)
        amat[turn, :, :, :, MAIN:] = rest.astype(BF).reshape(2, 2, block, LANES)
        send_core(turn)
    spill = local(pbuf, pspill, 4)

    for at in range(4):
        who = core if at < 2 else 1 - core
        rows = pl.ds(pl.multiple_of((2 * (at % 2) + who) * block, block), block)
        turned = fold[rows, MAIN:].astype(F32).T
        idrow[:, at * block : (at + 1) * block] = jnp.where(chip == 0, turned[5:6], turned[6:7])
    own_ids = []
    for h in range(2):
        rows = pl.ds(pl.multiple_of((2 * h + core) * block, block), block)
        ids = fold[rows, MAIN:].astype(F32)
        own_ids.append(jnp.where(chip == 0, ids[:, 5:6], ids[:, 6:7]))
    idcol = jnp.concatenate(own_ids, axis=0)
    z_copy.wait_recv()
    remote(init_ref, zall.at[row], peer)
    other_row = row + 2 - 4 * chip
    remote(zbuf.at[1 - chip], zall.at[other_row], peer)
    z_local = [local(init_ref, zall.at[row], 5), local(zbuf.at[1 - chip], zall.at[other_row], 6)]
    c_copy.wait_recv()
    c_own.wait()
    share_grad(DOWN2)
    wv_copy.wait()
    fill_rest(w_rest, wkv)
    step2.wait_recv()
    amix[...] = (core_sum(1) + ain2[...]).reshape(count, FEAT_PAD)
    amix_copy = remote(amix, amix_in, peer)

    def attended_cols(cols):
        value = dot(amix[:, :MAIN], wkv[:MAIN, cols]) + dot(amix[:, MAIN:], w_rest[:, cols])
        qbuf[:, cols] = value.astype(BF)
    columns_loop(attended_cols)
    w = weight(WO)

    def one_cols(cols):
        start = zbuf[:, :, cols].reshape(count, cols.size).astype(F32)
        stream[:, cols] = start + dot(qbuf[...], w[:, cols])
    columns_loop(one_cols)
    weight_done()

    def mlp(k, normed, active, up_id, down_id):
        layer(k, normed)
        share_act(normed)
        w_up = weight(up_id)

        def up_cols(cols):
            value, slope = gelu_parts(dot(acts[act(normed), :], w_up[:, cols]))
            acts[act(active), cols] = value.astype(BF)
            slopes[active // 4, :, cols] = slope.astype(BF)
        columns_loop(up_cols)
        weight_done()
        share_act(active)
        w_down = weight(down_id)

        def down_cols(cols):
            stream[:, cols] += dot(acts[act(active), :], w_down[:, cols])
        columns_loop(down_cols)
        weight_done()

    mlp(0, NORMED1, ACTIVE1, UP, DOWN)
    layer(1, SELFN)
    share_act(SELFN)
    chunks = HEADS // 2

    def chunk_copy(src, dst, at, slot):
        cols = pl.ds(pl.multiple_of(at * 2 * head_width, 2 * head_width), 2 * head_width)
        return pltpu.make_async_remote_copy(
            src_ref=src.at[:, cols], dst_ref=dst.at[:, cols], send_sem=hsend.at[slot + at],
            recv_sem=hrecv.at[slot + at], device_id=peer, device_id_type=MESH,
        )

    def kv_chunk(dst, at):
        return chunk_copy(kv.at[dst, 0], kv.at[dst, 1], at, dst * chunks)

    def dkv_chunk(dst, at):
        return chunk_copy(kv.at[dst, 1], dkv_in.at[dst], at, (2 + dst) * chunks)

    for index, dst in ((KW, 0), (VW, 1), (QW, None)):
        w_now = weight(index)

        def project(cols, dst=dst, w_now=w_now):
            value = dot(acts[act(SELFN), :], w_now[:, cols]).astype(BF)
            if dst is None:
                qbuf[:, cols] = value
            else:
                kv[dst, 0, :, cols] = value
                kv_chunk(dst, cols.start // (2 * head_width)).start()
        columns_loop(project, 2 * head_width)
        weight_done()
    spill.wait()

    def heads(body, before, after):
        def run(pair, carry):
            before(pair)
            for side in range(2):
                cols = pl.ds(pl.multiple_of((2 * pair + side) * head_width, head_width), head_width)
                rows = pl.ds(pl.multiple_of((pair % 2) * count, count), count)
                body(cols, (pl.ds(pair // 2, 1), rows, pl.ds(side * lat, lat)))
            after(pair)
            return carry
        lax.fori_loop(0, HEADS // 2, run, 0)

    def attend(cols, keep):
        keys = kv[0, :, :, cols].reshape(lat, head_width)
        values = kv[1, :, :, cols].reshape(lat, head_width)
        scores = dot_nt(qbuf[:, cols], keys) * self_scale
        scores = jnp.where(idcol == idrow[...], scores, NEGATIVE)
        weights = jnp.exp(scores - jnp.max(scores, axis=1, keepdims=True))
        prob = (weights * (1.0 / jnp.sum(weights, axis=1, keepdims=True))).astype(BF)
        pbuf[keep] = prob[None]
        acts[act(MIXED), cols] = dot(prob, values).astype(BF)

    def kv_arrived(pair):
        kv_chunk(0, pair).wait_recv()
        kv_chunk(1, pair).wait_recv()

    heads(attend, kv_arrived, lambda pair: None)
    share_act(MIXED)
    w_so = weight(SO)

    def three_cols(cols):
        stream[:, cols] += dot(acts[act(MIXED), :], w_so[:, cols])
    columns_loop(three_cols)
    weight_done()
    mlp(2, NORMED2, ACTIVE2, UPB, DOWNB)
    dmix[...] = stream[...].astype(BF)
    lat_ref[pl.ds(chip, 1)] = dmix[pl.ds(pl.multiple_of(chip * block, block), block), :][None]
    lat_copy = remote(
        dmix.at[pl.ds(pl.multiple_of((1 - chip) * block, block), block)], lat_ref.at[chip], across
    )

    weight_grad(DOWN2)
    tick(2.0)

    def mlp_back(k, normed, active, m_down, m_up, up_id, down_id, into, start=None):
        w_down = weight(down_id)

        def act_cols(cols):
            grad = dot_nt(gall[m_down, 0], w_down[cols, :]).astype(BF).astype(F32)
            gall[m_up, 0, :, cols] = (grad * slopes[active // 4, :, cols].astype(F32)).astype(BF)
        columns_loop(act_cols)
        weight_done()
        share_grad(m_up)
        tick(1.0)
        w_up = weight(up_id)

        def norm_cols(cols):
            dnorm[:, cols] = dot_nt(gall[m_up, 0], w_up[cols, :])
        columns_loop(norm_cols)
        weight_done()
        if into == 0:
            grad_copies[DOWN2].wait_send()
            grad_copies[UP2].wait_send()
        layer_back(k, normed, into, start)
        tick(1.5)

    mlp_back(2, NORMED2, ACTIVE2, DOWN2, UP2, UPB, DOWNB, SOUT, DOWN2)

    share_grad(SOUT)
    weight_grad(UP2)
    tick(1.5)
    w_so2 = weight(SO)
    lat_copy.wait_send()

    def mixed_cols(cols):
        dmix[:, cols] = dot_nt(gall[SOUT, 0], w_so2[cols, :]).astype(BF)
    columns_loop(mixed_cols)
    weight_done()

    def attend_back(cols, keep):
        keys = kv[0, :, :, cols].reshape(lat, head_width)
        values = kv[1, :, :, cols].reshape(lat, head_width)
        dm = dmix[:, cols]
        prob_b = pbuf[keep][0]
        prob = prob_b.astype(F32)
        grad = dot_nt(dm, values)
        delta = jnp.sum(prob * grad, axis=1, keepdims=True)
        score = (prob * (grad - delta)).astype(BF)
        gall[SQ, 0, :, cols] = (dot(score, keys) * self_scale).astype(BF)
        dk = (dot_tn(score, qbuf[:, cols]) * self_scale).astype(BF)
        dv = dot_tn(prob_b, dm).astype(BF)
        gall[SK, 0, :, cols] = dk[:count]
        gall[SV, 0, :, cols] = dv[:count]
        kv[0, 1, :, cols] = dk[count:]
        kv[1, 1, :, cols] = dv[count:]

    def dkv_leave(pair):
        dkv_chunk(0, pair).start()
        dkv_chunk(1, pair).start()

    heads(attend_back, lambda pair: None, dkv_leave)
    unspill = local(pspill, pbuf, 4)
    share_grad(SQ)
    tick(4.0)
    weight_grad(SOUT)
    tick(1.0)
    for at in range(chunks):
        dkv_chunk(0, at).wait_recv()
        dkv_chunk(1, at).wait_recv()

    def add_kv(rows):
        for at, m in ((0, SK), (1, SV)):
            gall[m, 0, rows, :] = gall[m, 0, rows, :] + dkv_in[at, rows, :]
    rows_loop(add_kv)
    share_grad(SK)
    share_grad(SV)
    for at, (m, index) in enumerate(((SQ, QW), (SK, KW), (SV, VW))):
        w_now = weight(index)

        def normed_cols(cols, at=at, m=m, w_now=w_now):
            value = dot_nt(gall[m, 0], w_now[cols, :])
            if at == 0:
                dnorm[:, cols] = value
            else:
                dnorm[:, cols] += value
        columns_loop(normed_cols)
        weight_done()
    layer_back(1, SELFN, DOWN1)
    share_grad(DOWN1)
    tick(3.0)
    weight_grad(SQ)
    tick(1.0)
    weight_grad(SK)
    tick(1.0)
    mlp_back(0, NORMED1, ACTIVE1, DOWN1, UP1, UP, DOWN, 0)

    w_o = weight(WO)

    def attended_back(cols):
        gall[1, 0, :, cols] = dot_nt(gall[0, 0], w_o[cols, :]).astype(BF)
    columns_loop(attended_back)
    weight_done()
    share_cd = remote(gall.at[1 - core, 0], gcd_in, peer)
    folded = jnp.concatenate([dot_nt(gall[1, 0], wkv[:MAIN, :]), dot_nt(gall[1, 0], w_rest[...])], axis=1)
    along = jnp.sum(folded * amix[...].astype(F32), axis=0, keepdims=True)
    gsum[3:4, :FEAT_PAD] = along
    gsum[3:4, FEAT_PAD:] = jnp.zeros((1, width - FEAT_PAD), F32)
    da_all[pl.ds(chip, 1), :, pl.ds(core, 1)] = folded.astype(BF).reshape(1, 2, 1, block, FEAT_PAD)
    mine = da_all.at[chip, :, core]
    da_across = remote(mine, mine, across)
    da_peer = remote(mine, mine, peer)
    tick(2.0)
    weight_grad(SV)
    tick(1.0)
    da_across.wait_recv()
    other = da_all.at[1 - chip, :, core]
    da_other = remote(other, other, peer)
    weight_grad(DOWN1)
    tick(1.0)
    weight_grad(UP1)
    tick(1.0)

    share_cd.wait_recv()
    amix_copy.wait_recv()
    lefts = jnp.concatenate([amix[:, :MAIN], amix_in[:, :MAIN]], axis=0)
    grads = jnp.concatenate([gall[pl.ds(core, 1), 0][0], gcd_in[...]], axis=0)
    total = dot_tn(lefts, grads).astype(BF)
    for plane in range(2):
        store_plane(MATS, plane, 0, total[plane * LANES : (plane + 1) * LANES])
    for plane in range(2):
        store_plane(MATS, plane, 1, upstr[plane * block : (plane + 1) * block, :].astype(BF))
    begin_unit(MATS)
    gsum[4:, :] = jnp.zeros((gsum.shape[0] - 4, width), F32)
    rests = [dot_tn(amix[:, MAIN:], gall[side, 0])[:8] for side in range(2)]
    for i in range(8):
        cols = slice(i * LANES, (i + 1) * LANES)
        both = jnp.concatenate([rests[0][:, cols], rests[1][:, cols]], axis=0)
        sm[16 * i : 16 * (i + 1), FEAT_PAD:] = both.astype(BF)
        sm[128 + 16 * i : 128 + 16 * (i + 1), FEAT_PAD:] = gsum[:, cols].astype(BF)
    sm[256:, FEAT_PAD:] = jnp.zeros((lat - 256, LANES), BF)
    tick(2.0)

    da_peer.wait_recv()
    da_other.wait_recv()
    unspill.wait()

    def score_rows(s):
        return wslots.at[s, pl.ds(0, lat)]

    def da_rows(s):
        return wslots.at[s, pl.ds(lat, lat), pl.ds(0, CAT)]

    def q_rows(s):
        return wslots.at[2, pl.ds(s * lat, lat), pl.ds(0, CAT)]

    for s in range(2):
        for i in range(4):
            rows = pl.ds(i * block, block)
            wslots[s, lat + i * block : lat + (i + 1) * block, :CAT] = spread_out(
                da_all[s, i // 2, i % 2], s, rows
            )
            wslots[2, s * lat + i * block : s * lat + (i + 1) * block, :CAT] = spread_out(
                fold[rows, :], s, rows
            )

        def back_cols(cols, s=s):
            fbuf[:, cols] = dot(wslots[s, lat:, :CAT], xcat[s, :, cols])
        columns_loop(back_cols, 256, slots)

        def score_back(rows, s=s):
            prob = pbuf[s, rows, :].astype(F32)
            grad = fbuf[rows, :]
            delta = jnp.sum(prob * grad, axis=1, keepdims=True)
            wslots[s, rows, :] = (prob * (grad - delta)).astype(BF)
        rows_loop(score_back, 64, lat)
        scores = wslots[s, :lat, :]
        zero = dot_nt(scores, xcat[s, :MAIN, :])
        one = dot_nt(scores, xcat[s, MAIN : 2 * MAIN, :])
        rest = dot_nt(scores, xcat[s, 2 * MAIN :, :])
        main, rest = pull_in(s, pl.ds(0, lat), zero, one, rest)
        if s == 0:
            bsum[:, :MAIN] = main
            bsum[:, MAIN:] = rest
        else:
            sm[:, :MAIN] = (bsum[:, :MAIN] + main).astype(BF)
            sm[:, MAIN:FEAT_PAD] = (bsum[:, MAIN:] + rest).astype(BF)
        tick(4.0)

    small_send()
    for copy in act_copies.values():
        copy.wait_send()
    for s in range(2):
        for at, (lo, size) in enumerate(((0, MAIN), (MAIN, MAIN), (2 * MAIN, LANES))):
            cols = pl.ds(lo, size)
            total = dot_tn(wslots[2, s * lat : (s + 1) * lat, cols], wslots[s, :lat, :])
            total = total + dot_tn(wslots[s, lat:, cols], pbuf[s])
            acts[pl.ds(s * CAT + lo, size), :] = total.astype(BF)
            tick(2.0)

    main_gain, rest_gain = gain_col[:MAIN, :], gain_col[MAIN:, :]
    y_copy = None
    for k in range(2):
        if y_copy is not None:
            y_copy.wait()
        for s in range(2):

            def pixel_step(jb, carry, k=k, s=s):
                cols = pl.ds(pl.multiple_of(jb * LANES, LANES), LANES)
                up_main = acts[s * CAT + k * MAIN : s * CAT + (k + 1) * MAIN, cols].astype(F32)
                up_rest = acts[s * CAT + 2 * MAIN : s * CAT + 2 * MAIN + 16, cols].astype(F32)
                up_rest = up_rest[8 * k : 8 * k + 8]
                x_main = xcat[s, k * MAIN : (k + 1) * MAIN, cols].astype(F32)
                x_rest = xcat[s, 2 * MAIN : 2 * MAIN + 16, cols].astype(F32)[8 * k : 8 * k + 8]
                rs = pixel_rs[pl.ds(k * (group // 2) + 2 * jb + s, 1), :]
                scaled_main, scaled_rest = up_main * main_gain, up_rest * rest_gain

                def mean_of(a, b):
                    whole = jnp.sum(a, axis=0, keepdims=True) + jnp.sum(b, axis=0, keepdims=True)
                    return whole * (1.0 / features)
                centre = mean_of(scaled_main, scaled_rest)
                along = mean_of(up_main * x_main, up_rest * x_rest)
                unit_main, unit_rest = x_main / main_gain, x_rest / rest_gain
                out_main = rs * (scaled_main - centre - unit_main * along)
                out_rest = rs * (scaled_rest - centre - unit_rest * along)
                flat[pl.ds(2 * jb + s, tall, stride=group // 2), :] = jnp.concatenate(
                    [out_main, out_rest], axis=0
                )
                return carry
            lax.fori_loop(0, blocks, pixel_step, 0)
            tick(2.0)
        y_copy = local(flat.at[pl.ds(0, features * group // 2)], y_ref.at[k], 7 + k)
    while next_due() < 1e9:
        serve()
    for copy in z_local + [y_copy]:
        copy.wait()
    for at in range(chunks):
        for dst in range(2):
            kv_chunk(dst, at).wait_send()
            dkv_chunk(dst, at).wait_send()
    for copy in copies:
        copy.finish()


def finish_kernel(*refs):
    it = iter(refs)

    def take(n=None):
        return next(it) if n is None else [next(it) for _ in range(n)]

    y_in, lat_in = take(2)
    ins = take(8)
    query_gain, pixel_gain = take(2)
    y_out, lat_out, init_out, pixel_gain_out, key_out, value_out = take(6)
    gain_outs = take(4)
    mat_outs = take(MATS + 2)
    held = take(8)
    summed, small, fold, init_all, wq, wk, wv, init_sum = held
    unit, normed, total, mats, wk_rest, wv_rest, y_buf, lat_buf, back = take(9)
    sem, out_sem = take(2)
    features, width = ins[5].shape
    lat = init_all.shape[0]
    block = lat // 4
    j = lax.axis_index("seq")
    row = lax.axis_index("row")
    cross_scale = 1.0 / math.sqrt(width)

    through = [
        (pltpu.make_async_copy(y_in.at[k], y_buf.at[:, pl.ds(k * y_in.shape[2], y_in.shape[2])], sem.at[8 + k]))
        for k in range(2)
    ] + [pltpu.make_async_copy(lat_in, lat_buf, sem.at[10])]
    copies = []
    for i, (src, dst) in enumerate(zip(ins, held)):
        copies.append(pltpu.make_async_copy(src, dst, sem.at[i]))
        copies[-1].start()
        if i == 0:
            for copy in through:
                copy.start()
    outs = []

    def put(src, dst):
        copy = pltpu.make_async_copy(src, dst, out_sem.at[len(outs)])
        copy.start()
        outs.append(copy)

    copies[0].wait()
    for m in range(MATS):
        for r in range(4):
            for h in range(2):
                at = (r % 2) * (width // 2) + (r // 2) * 2 * LANES + h * LANES
                mats[m, at : at + LANES, :] = summed[r, 2 * m + h].astype(F32)
        put(mats.at[m], mat_outs[m])
    copies[3].wait()
    query_rs = []
    for r in range(4):
        rows = pl.ds(r * block, block)
        value, scale = norm_parts(init_all[rows, :].astype(F32))
        unit[rows, :] = value
        normed[rows, :] = (value * query_gain[...]).astype(BF)
        query_rs.append(scale)
    for copy in through:
        copy.wait()
    put(y_buf, y_out)
    put(lat_buf, lat_out)
    for copy in copies[1:3] + copies[4:]:
        copy.wait()
    fill_rest(wv_rest, wv)
    fill_rest(wk_rest, wk)
    my_cols = pl.ds(pl.multiple_of(j * LANES, LANES), LANES)

    for n in range(width // 256):
        cols = pl.ds(n * 256, 256)
        value = dot(small[:, :MAIN], wk[:MAIN, cols]) + dot(small[:, MAIN:FEAT_PAD], wk_rest[:, cols])
        total[:, cols] = (value * cross_scale).astype(BF)

    def put_turned(index, value):
        for n in range(width // LANES):
            mats[index, n * LANES : (n + 1) * LANES, :] = value[:, n * LANES : (n + 1) * LANES].T
        put(mats.at[index], mat_outs[index])
    put_turned(MATS, dot_tn(total[:, my_cols], normed[...]))
    outer = [
        [summed[2 * y + c, FEATURE_UNIT].astype(F32) for y in range(2)] for c in range(2)
    ]
    rests = small[pl.ds(pl.multiple_of(j * 16, 16), 16), FEAT_PAD:]
    value_out[:LANES, :] = outer[1][0]
    value_out[LANES:MAIN, :] = outer[1][1]
    value_out[MAIN:, :] = rests.astype(F32)[8 : 8 + features - MAIN]
    summed_c = jnp.concatenate(outer[0], axis=0).astype(BF)
    put_turned(MATS + 1, dot_tn(summed_c, wv[:MAIN, :]) + dot_tn(rests, wv_rest[:16, :]))
    my_queries = dot(normed[...], wq[:, my_cols]).astype(BF)
    key_turned = dot_tn(my_queries, small[:, :FEAT_PAD]) * cross_scale
    key_out[...] = jnp.concatenate(
        [key_turned[:, n * LANES : (n + 1) * LANES].T for n in range(3)], axis=0
    )[:features]
    for i in range(8):
        chunk = small[128 + 16 * i : 128 + 16 * (i + 1), FEAT_PAD:].astype(F32)
        for g in range(3):
            gain_outs[g][i : i + 1, :] = chunk[g : g + 1]
    scores = small[:, :FEAT_PAD].astype(F32)
    part = jnp.sum(fold[...].astype(F32) * scores, axis=0, keepdims=True)
    rest_sum = [small[128 + 16 * i : 128 + 16 * (i + 1), FEAT_PAD:].astype(F32)[3:4] for i in range(3)]
    whole = (part + jnp.concatenate(rest_sum, axis=1))[:, :features]
    pixel_gain_out[...] = (whole / pixel_gain[...].reshape(1, features)).reshape(features)
    own = pl.ds(pl.multiple_of(row * block, block), block)
    own_rs = query_rs[0]
    for r in range(1, 4):
        own_rs = jnp.where(row == r, query_rs[r], own_rs)
    sums = jnp.zeros((block, 1), F32)
    alongs = jnp.zeros((block, 1), F32)
    for n in range(width // 256):
        cols = pl.ds(n * 256, 256)
        back[:, cols] = dot_nt(total[...], wq[cols, :])
        row_sum = jnp.sum(back[:, cols] * unit[:, cols], axis=0, keepdims=True)
        for i in range(2):
            gain_outs[3][2 * n + i : 2 * n + i + 1, :] = row_sum[:, i * LANES : (i + 1) * LANES]
        scaled = back[own, cols] * query_gain[:, cols]
        sums = sums + jnp.sum(scaled, axis=1, keepdims=True)
        alongs = alongs + jnp.sum(scaled * unit[own, cols], axis=1, keepdims=True)
    scaled = back[own, my_cols] * query_gain[:, my_cols]
    query_in = own_rs * (scaled - sums * (1.0 / width) - unit[own, my_cols] * (alongs * (1.0 / width)))
    init_out[...] = init_sum[...].astype(F32) + query_in
    for copy in outs:
        copy.wait()


def finish(y, latents, summed, small, init_sum, fold, init_all, wq, wk, wv, query_gain, pixel_gain):
    features, width = wk.shape
    lat = init_all.shape[0]
    block = lat // 4
    vmem = pl.BlockSpec(memory_space=pltpu.VMEM)
    hbm = pl.BlockSpec(memory_space=pl.ANY)

    def f32(*shape):
        return jax.ShapeDtypeStruct(shape, F32)

    outs = pl.pallas_call(
        finish_kernel,
        out_shape=[f32(features, 2 * y.shape[2], LANES), jax.ShapeDtypeStruct(latents.shape, BF), f32(block, LANES),
                   f32(features), f32(features, LANES), f32(features, LANES)]
        + [f32(width // LANES, LANES)] * 4 + [f32(width, LANES)] * (MATS + 2),
        in_specs=[hbm] * 10 + [vmem] * 2,
        out_specs=[hbm] * 2 + [vmem] * 8 + [hbm] * (MATS + 2),
        scratch_shapes=[
            pltpu.VMEM(shape, BF)
            for shape in (summed.shape, small.shape, fold.shape, init_all.shape,
                          wq.shape, wk.shape, wv.shape, init_sum.shape)
        ]
        + [
            pltpu.VMEM((lat, width), F32),
            pltpu.VMEM((lat, width), BF),
            pltpu.VMEM((lat, width), BF),
            pltpu.VMEM((MATS + 2, width, LANES), F32),
            pltpu.VMEM((LANES, width), BF),
            pltpu.VMEM((LANES, width), BF),
            pltpu.VMEM((features, 2 * y.shape[2], LANES), F32),
            pltpu.VMEM(latents.shape, BF),
            pltpu.VMEM((lat, width), F32),
            pltpu.SemaphoreType.DMA((11,)),
            pltpu.SemaphoreType.DMA((MATS + 4,)),
        ],
        compiler_params=pltpu.CompilerParams(vmem_limit_bytes=VMEM_LIMIT),
    )(y, latents, summed, small, fold, init_all, wq, wk, wv, init_sum, query_gain[None],
      pixel_gain)
    y, latents, init_grad, pixel_gain_grad, key_grad, value_grad = outs[:6]
    return (y, latents, init_grad, outs[6:10], pixel_gain_grad, key_grad, value_grad, outs[10:])


def whole_stack(shards, z, pixel_gain, pseg, init, cots, seg, wk, wv, gains, weights):
    width = init.shape[1]
    block = init.shape[0]
    count = 2 * block
    lat = 2 * count
    share = width // shards
    half = width // 2
    bits = shards.bit_length() - 1
    orders = unit_orders(bits)
    nslots = 3
    features = wk.shape[0]
    group = z.shape[0] // features
    slots = group * LANES // 4
    small, size = [], lat
    for i in range(bits + 2):
        size = size // 2 if size > 16 else size
        small.append((size, 512))
    scratch = [
        ((nslots, width, width), BF),
        (wk.shape, BF),
        ((LANES, width), BF),
        ((2, block, width), BF),
        ((2, 2, block, FEAT_PAD), BF),
        ((2, block, FEAT_PAD), BF),
        ((2, block, FEAT_PAD), BF),
        ((count, FEAT_PAD), BF),
        ((count, FEAT_PAD), BF),
        ((2, 2, 2, block, FEAT_PAD), BF),
        ((lat, width), F32),
        ((3, count, LANES), F32),
        ((6 * count, width), BF),
        ((6, count, half), BF),
        ((2, count, width), BF),
        ((count, width), BF),
        ((2, 2, count, width), BF),
        ((2, lat, slots), BF),
        ((count, width), BF),
        ((2, count, width), BF),
        ((MATS, 2, count, width), BF),
        ((count, width), BF),
        ((FEATURE_UNIT + 1, share, LANES), BF),
        ((2, 2, 2, block, FEAT_PAD), BF),
        ((lat, FEAT_PAD), F32),
        ((16, width), F32),
        ((1, lat), F32),
        ((lat, 512), BF),
        ((2, CAT, slots), BF),
        (((MAIN + 8) * group // 2, LANES), F32),
        ((2, 8, slots), F32),
        ((group, LANES), F32),
        ((MAIN + 8, LANES), F32),
        ((FEATURE_UNIT + 1, share, LANES), BF),
        ((UNITS * 4, width, LANES), BF),
    ]
    for order in orders:
        scratch += [(shape, BF) for shape in stage_shapes(order, width)]
    scratch += [(shape, BF) for shape in small]
    stages = sum(len(order) for order in orders)
    vmem = pl.BlockSpec(memory_space=pltpu.VMEM)
    hbm = pl.BlockSpec(memory_space=pl.ANY)
    return pl.pallas_call(
        functools.partial(
            main_kernel, (shards, width, count, dict(small_stages=len(small)))
        ),
        out_shape=[
            jax.ShapeDtypeStruct((2, block, width), BF),
            jax.ShapeDtypeStruct((lat, 512), BF),
            jax.ShapeDtypeStruct((4, FEATURE_UNIT + 1, share, LANES), BF),
            jax.ShapeDtypeStruct((share, LANES), BF),
            jax.ShapeDtypeStruct((lat, FEAT_PAD), BF),
            jax.ShapeDtypeStruct((4, block, width), BF),
            jax.ShapeDtypeStruct((2, features * group // 2, LANES), F32),
            jax.ShapeDtypeStruct((2, lat, slots), BF),
        ],
        in_specs=[hbm, pl.BlockSpec(memory_space=pltpu.SMEM), vmem, vmem, hbm, vmem]
        + [hbm] * 2 + [vmem] * 4 + [hbm] * 10,
        out_specs=[vmem, vmem, hbm, vmem, vmem, hbm, hbm, hbm],
        scratch_shapes=[pltpu.VMEM(shape, kind) for shape, kind in scratch]
        + [
            pltpu.SemaphoreType.DMA((nslots + 2 + 13,)),
            pltpu.SemaphoreType.DMA((nslots * 4,)),
            pltpu.SemaphoreType.DMA((-(-z.shape[0] // width),)),
            pltpu.SemaphoreType.DMA((stages,)),
            pltpu.SemaphoreType.DMA((stages,)),
            pltpu.SemaphoreType.DMA((80,)),
            pltpu.SemaphoreType.DMA((80,)),
            pltpu.SemaphoreType.DMA((16,)),
            pltpu.SemaphoreType.DMA((16,)),
        ],
        compiler_params=pltpu.CompilerParams(
            collective_id=0, has_side_effects=True, vmem_limit_bytes=VMEM_LIMIT
        ),
    )(z, pixel_gain, pseg, init, cots, seg, wk, wv, *[g[None] for g in gains], *weights)


VMEM_LIMIT = 63 * 1024 * 1024


def body(
    pixels, pixel_seg, latent_seg, latent_init, cotangent,
    pixel_gain, query_gain, query_weight, key_weight, value_weight, output_weight,
    mlp_gain, up_weight, down_weight,
    self_gain, self_query, self_key, self_value, self_output,
    second_gain, second_up, second_down,
):
    seqs, pix, features = pixels.shape
    block, width = latent_init.shape
    shards = lax.axis_size("seq")
    lat = block * lax.axis_size("row")
    row = lax.axis_index("row")
    cross_scale = 1.0 / math.sqrt(width)
    tiles = pix // LANES

    z = pixels.transpose(2, 0, 1).reshape(features, seqs, tiles, LANES)
    z = z.transpose(0, 2, 1, 3).reshape(features * seqs * tiles, LANES)
    latents, small, summed, init_sum, fold, init_all, y, unused = whole_stack(
        shards, z, pixel_gain, pixel_seg, latent_init, cotangent, latent_seg, key_weight, value_weight,
        (mlp_gain, self_gain, second_gain, query_gain),
        (query_weight, output_weight, up_weight, down_weight, self_query, self_key, self_value,
         self_output, second_up, second_down),
    )
    init_all = init_all.reshape(lat, width)
    y = y.reshape(2, features, tiles, LANES)
    if width // shards == LANES:
        y, latents, init_grad, gains, pixel_gain_grad, key_grad, value_grad, mats = finish(
            y, latents, summed, small, init_sum, fold, init_all, query_weight, key_weight,
            value_weight, query_gain, pixel_gain,
        )
    else:
        y = y.transpose(1, 0, 2, 3)
    pixel_grad = y.reshape(features, tiles, seqs, LANES).transpose(2, 1, 3, 0)
    pixel_grad = pixel_grad.reshape(seqs, pix, features)
    if width // shards == LANES:
        mlp_gain_grad, self_gain_grad, second_gain_grad, query_gain_grad = [
            g.reshape(width) for g in gains
        ]
        return (
            latents, pixel_grad, init_grad, pixel_gain_grad,
            query_gain_grad, mlp_gain_grad, self_gain_grad, second_gain_grad,
            mats[MATS], key_grad, value_grad, mats[MATS + 1], mats[UP1], mats[DOWN1],
            mats[SQ], mats[SK], mats[SV], mats[SOUT], mats[UP2], mats[DOWN2],
        )

    share = width // shards
    at = lax.axis_index("seq") * share

    def columns(arr):
        return lax.dynamic_slice_in_dim(arr, at, share, arr.ndim - 1)

    score_b = small[:, :features]
    side = small[:, FEAT_PAD:]
    rests = side[:128].reshape(8, 2, 8, LANES).transpose(1, 2, 0, 3).reshape(2, 8, width)
    sums = side[128:256].reshape(8, 16, LANES).transpose(1, 0, 2).reshape(16, width).astype(F32)
    pixel_gain_grad = (
        jnp.sum(fold[:, :features].astype(F32) * score_b.astype(F32), axis=0) + sums[3, :features]
    ) / pixel_gain
    units = summed.reshape(2, 2, FEATURE_UNIT + 1, share, LANES)
    mats = units[:, :, :FEATURE_UNIT].reshape(2, 2, MATS, 2, share, LANES)
    mats = mats.transpose(2, 1, 0, 3, 5, 4).reshape(MATS, width, share).astype(F32)
    outer = units[:, :, FEATURE_UNIT].transpose(1, 0, 3, 2).reshape(2, MAIN, share)
    outer = jnp.concatenate([outer, columns(rests)[:, : features - MAIN]], axis=1)
    value_grad = outer[1].astype(F32)
    output_grad = dot_tn(value_weight, outer[0])
    query_unit, query_rs = norm_parts(init_all.astype(F32))
    query_normed = (query_unit * query_gain).astype(BF)
    my_queries = dot(query_normed, columns(query_weight)).astype(BF)
    key_grad = dot_tn(score_b, my_queries) * cross_scale
    query_total = (dot(score_b, key_weight) * cross_scale).astype(BF)
    query_grad = dot_tn(query_normed, columns(query_total))
    query_in, query_gain_grad = norm_back(
        query_unit, query_rs, query_gain, dot_nt(query_total, query_weight)
    )
    init_grad = init_sum.T.astype(F32) + lax.dynamic_slice(query_in, (row * block, at), (block, share))
    return (
        latents, pixel_grad, init_grad,
        pixel_gain_grad, query_gain_grad, sums[0], sums[1], sums[2],
        query_grad, key_grad, value_grad, output_grad, mats[UP1], mats[DOWN1],
        mats[SQ], mats[SK], mats[SV], mats[SOUT], mats[UP2], mats[DOWN2],
    )


def solution(mesh):
    placed = (
        P("seq", "row", None), P("seq", "row"), P("seq", "row"), P("row", None),
        P("seq", "row", None),
    ) + (P(),) * 17
    cols = P(None, "seq")
    return jax.shard_map(
        body,
        mesh=mesh,
        in_specs=placed,
        out_specs=(P("seq", "row", None), P("seq", "row", None), P("row", "seq"))
        + (P(),) * 5 + (cols,) * 12,
        check_vma=False,
    )
```

```python
import functools
import math

import jax
import jax.numpy as jnp
from jax import lax
from jax.experimental import pallas as pl
from jax.experimental.pallas import tpu as pltpu
from jax.sharding import PartitionSpec as P

HEADS = 8
EPSILON = 1e-05
NEGATIVE = -1e9
BF = jnp.bfloat16
F32 = jnp.float32
LANES = 128
FEAT_PAD = 384
MAIN = 256
CAT = 2 * MAIN + LANES
MESH = pl.DeviceIdType.MESH


def dot(a, b):
    return jnp.dot(a, b, preferred_element_type=F32)


def dot_tn(a, b):
    return lax.dot_general(a, b, (((0,), (0,)), ((), ())), preferred_element_type=F32)


def dot_nt(a, b):
    return lax.dot_general(a, b, (((1,), (1,)), ((), ())), preferred_element_type=F32)


def fill_rest(rest, matrix):
    rest[...] = jnp.zeros(rest.shape, rest.dtype)
    rest[: matrix.shape[0] - MAIN, :] = matrix[MAIN:, :]


def norm_parts(values):
    centre = values - jnp.mean(values, axis=-1, keepdims=True)
    rs = lax.rsqrt(jnp.mean(centre * centre, axis=-1, keepdims=True) + EPSILON)
    return centre * rs, rs


def norm_back(unit, rs, gain, upstream):
    scaled = upstream * gain
    grad = rs * (
        scaled
        - jnp.mean(scaled, axis=-1, keepdims=True)
        - unit * jnp.mean(scaled * unit, axis=-1, keepdims=True)
    )
    return grad, jnp.sum(upstream * unit, axis=0)


def gelu_parts(hidden):
    cdf = 0.5 * (1.0 + lax.erf(hidden * math.sqrt(0.5)))
    pdf = jnp.exp(-0.5 * hidden * hidden) * (1.0 / math.sqrt(2.0 * math.pi))
    return hidden * cdf, cdf + hidden * pdf


NORMED1, ACTIVE1, SELFN, MIXED, NORMED2, ACTIVE2 = range(6)
DOWN2, UP2, SOUT, SQ, SK, SV, DOWN1, UP1 = range(8)
LEFT = {
    DOWN2: ACTIVE2, UP2: NORMED2, SOUT: MIXED, SQ: SELFN, SK: SELFN, SV: SELFN,
    DOWN1: ACTIVE1, UP1: NORMED1,
}
MATS = 8
FEATURE_UNIT = 2 * MATS
UNITS = MATS + 1


class Remote:
    def __init__(self, log, src, dst, send_sem, recv_sem, device):
        self.copy = pltpu.make_async_remote_copy(
            src_ref=src, dst_ref=dst, send_sem=send_sem, recv_sem=recv_sem,
            device_id=device, device_id_type=MESH,
        )
        self.copy.start()
        self.arrived = self.sent = False
        log.append(self)

    def wait_recv(self):
        if not self.arrived:
            self.copy.wait_recv()
        self.arrived = True

    def wait_send(self):
        if not self.sent:
            self.copy.wait_send()
        self.sent = True

    def finish(self):
        self.wait_recv()
        self.wait_send()


KINDS = "FCDABCEBA"


def unit_orders(bits):
    first, second, tail = [0], list(range(1, min(bits, 2))), list(range(2, bits))
    kinds = {
        "A": ["y"] + first + second + tail,
        "B": first + second + ["y"] + tail,
        "C": second + first + ["y"] + tail,
        "D": first + ["y"] + second + tail,
        "E": second + ["y"] + first + tail,
        "F": ["y"] + second + first + tail,
    }
    return [kinds[letter] for letter in KINDS]


def stage_shapes(order, width):
    shapes, planes, size = [], 4, width
    for axis in order:
        if axis == "y":
            planes = 2
        else:
            size //= 2
        shapes.append((planes, size, LANES))
    return shapes


def main_kernel(cfg, *refs):
    shards, width, count, sizes = cfg
    bits = shards.bit_length() - 1
    share = width // shards
    half = width // 2
    block = count // 2
    lat = 2 * count
    head_width = width // HEADS
    cross_scale = 1.0 / math.sqrt(width)
    self_scale = 1.0 / math.sqrt(head_width)
    orders = unit_orders(bits)
    it = iter(refs)

    def take(n=None):
        return next(it) if n is None else [next(it) for _ in range(n)]

    (z_hbm, pixel_gain, pseg_ref, init_ref, cot_hbm, seg_ref, wk_hbm, wv_hbm) = take(8)
    gain_refs = take(4)
    w_hbm = take(10)
    (lat_ref, sm_out, gat_ref, initg_ref, fold, zall, y_ref, pspill) = take(8)
    (wslots, wkv, w_rest, zbuf, ain1, asum, ain2, amix, amix_in, amat, fbuf, rsb, acts, acts_in, slopes,
     qbuf, kv, pbuf, dmix, dkv_in, gall, gcd_in, fin, da_all, bsum, gsum, idrow,
     sm, xcat, flat, rest0, pixel_rs, gain_col, inverse, fin_in, part) = take(36)
    recv = [take(len(orders[u])) for u in range(UNITS)]
    smr = take(sizes["small_stages"])
    (wsem, psem, zsem, usend, urecv, csend, crecv) = take(7)

    j = lax.axis_index("seq")
    row = lax.axis_index("row")
    core, chip = row % 2, row // 2
    peer = {"row": row + 1 - 2 * core}
    across = {"row": row + 2 - 4 * chip}
    diagonal = {"row": 3 - row}
    bit_of = [(j // (1 << b)) % 2 for b in range(bits)]
    partner = {b: {"seq": j + (1 - 2 * bit_of[b]) * (1 << b)} for b in range(bits)}
    partner["y"] = across
    stream = fbuf.at[pl.ds(0, count)]
    upstr = fbuf.at[pl.ds(count, count)]
    dnorm = stream

    def act(k):
        return pl.ds(k * count, count)

    WQ, WO, UP, DOWN, QW, KW, VW, SO, UPB, DOWNB = range(10)
    uses = [WQ, WO, UP, DOWN, KW, VW, QW, SO, UPB, DOWNB, DOWNB, UPB, SO, QW, KW, VW, DOWN, UP, WO]
    nslots = wslots.shape[0]
    at_use = [0]

    pieces = 4

    class WeightCopy:
        def __init__(self, i):
            size = width // pieces
            self.copies = [
                pltpu.make_async_copy(
                    w_hbm[uses[i]].at[pl.ds(p * size, size)],
                    wslots.at[i % nslots, pl.ds(p * size, size)],
                    psem.at[(i % nslots) * pieces + p],
                )
                for p in range(pieces)
            ]

        def start(self):
            for copy in self.copies:
                copy.start()

        def wait(self):
            for copy in self.copies:
                copy.wait()

    def weight_copy(i):
        return WeightCopy(i)

    def weight(expect):
        i = at_use[0]
        assert uses[i] == expect
        at_use[0] += 1
        weight_copy(i).wait()
        return wslots.at[i % nslots]

    def weight_done():
        i = at_use[0] - 1 + nslots
        if i < len(uses):
            weight_copy(i).start()

    features = wk_hbm.shape[0]
    pixel_copies = []
    for i, lo in enumerate(range(0, z_hbm.shape[0], width)):
        rows = min(width, z_hbm.shape[0] - lo)
        pixel_copies.append(pltpu.make_async_copy(
            z_hbm.at[pl.ds(lo, rows)], part.at[i, pl.ds(0, rows)], zsem.at[i]
        ))
    weight_copy(0).start()
    wk_copy = pltpu.make_async_copy(wk_hbm, wkv, wsem.at[nslots])
    wk_copy.start()
    for i in range(1, nslots):
        weight_copy(i).start()
    wv_copy = pltpu.make_async_copy(wv_hbm, wkv, wsem.at[nslots + 1])
    for copy in pixel_copies:
        copy.start()

    barrier = pltpu.get_barrier_semaphore()
    partners = [peer, across, diagonal] + [partner[b] for b in range(bits)]
    for p in partners:
        pl.semaphore_signal(barrier, inc=1, device_id=p, device_id_type=MESH)
    copies = []
    slot_count = [0]

    def remote(src, dst, device):
        slot = slot_count[0]
        slot_count[0] += 1
        return Remote(copies, src, dst, csend.at[slot], crecv.at[slot], device)

    def local(src, dst, slot):
        copy = pltpu.make_async_copy(src, dst, wsem.at[nslots + 2 + slot])
        copy.start()
        return copy

    def rows_loop(body, step=64, total=None):
        def run(i, carry):
            body(pl.ds(pl.multiple_of(i * step, step), step))
            return carry
        lax.fori_loop(0, (total or count) // step, run, 0, unroll=2)

    def columns_loop(body, step=512, total=width):
        def run(i, carry):
            body(pl.ds(pl.multiple_of(i * step, step), step))
            return carry
        lax.fori_loop(0, total // step, run, 0)

    def layer(k, into):
        def body(rows):
            unit, rs = norm_parts(stream[rows, :])
            rsb[k, rows, :] = jnp.broadcast_to(rs, (rs.shape[0], LANES))
            place = pl.ds(pl.multiple_of(into * count + rows.start, rows.size), rows.size)
            acts[place, :] = (unit * gain_refs[k][...]).astype(BF)
        rows_loop(body)

    def layer_back(k, normed, into, start=None):
        gain = gain_refs[k][...]
        inverse = 1.0 / gain

        def body(i, total):
            rows = pl.ds(pl.multiple_of(i * 64, 64), 64)
            place = pl.ds(pl.multiple_of(normed * count + i * 64, 64), 64)
            dn = dnorm[rows, :]
            unit = acts[place, :].astype(F32) * inverse
            scaled = dn * gain
            rs = rsb[k, rows, :][:, :1]
            mean = jnp.mean(scaled, axis=-1, keepdims=True)
            along = jnp.mean(scaled * unit, axis=-1, keepdims=True)
            before = upstr[rows, :] if start is None else gall[start, 0, rows, :].astype(F32)
            after = before + rs * (scaled - mean - unit * along)
            upstr[rows, :] = after
            gall[into, 0, rows, :] = after.astype(BF)
            return total + jnp.sum(dn * unit, axis=0, keepdims=True)
        gsum[pl.ds(k, 1), :] = lax.fori_loop(
            0, count // 64, body, jnp.zeros((1, width), F32), unroll=2
        )

    act_copies, grad_copies = {}, {}

    def share_act(k):
        away = pl.ds(pl.multiple_of((1 - core) * half, half), half)
        act_copies[k] = remote(acts.at[act(k), away], acts_in.at[k], peer)

    def share_grad(m):
        grad_copies[m] = remote(gall.at[m, 0], gall.at[m, 1], peer)

    clock = [0.0]
    small = dict(lo=0, size=lat, stage=0, up=[], copy=None, due=1e9)
    axes = [(core, peer), (chip, across)] + [(bit_of[b], partner[b]) for b in range(bits)]

    def small_send():
        bit, device = axes[small["stage"]]
        size = small["size"]
        if size > 16:
            size //= 2
            away = pl.multiple_of(small["lo"] + (1 - bit) * size, 16)
            keep = pl.multiple_of(small["lo"] + bit * size, 16)
            small["up"].append((device, keep, size))
            small["lo"], small["size"] = keep, size
        else:
            away = small["lo"]
        small["copy"] = remote(sm.at[pl.ds(away, size)], smr[small["stage"]], device)
        small["due"] = clock[0] + 2.5 + size * 512 * 4 / 75e3

    def small_grow():
        device, lo, size = small["up"].pop()
        rows = pl.ds(lo, size)
        small["copy"] = remote(sm_out.at[rows], sm_out.at[rows], device)
        small["due"] = clock[0] + 2.5 + size * 512 * 4 / 75e3

    def small_step():
        copy, size = small["copy"], small["size"]
        copy.wait_recv()
        if small["stage"] < len(axes):
            copy.wait_send()
            rows = pl.ds(small["lo"], size)
            sm[rows, :] = sm[rows, :] + smr[small["stage"]][...]
            small["stage"] += 1
            if small["stage"] < len(axes):
                small_send()
                return
            sm_out[rows, :] = sm[rows, :]
        if small["up"]:
            small_grow()
        else:
            small["due"] = 1e9

    state = {}
    free = {}
    pending = []

    def region(u, planes, lo, size):
        if planes == 4:
            return part.at[pl.ds(4 * u, 4), pl.ds(lo, size)]
        return part.at[pl.ds(4 * u + 2 * chip, 2), pl.ds(lo, size)]

    def send_stage(u):
        s = state[u]
        axis = orders[u][s["stage"]]
        k = s["stage"]
        if axis == "y":
            src = part.at[pl.ds(4 * u + 2 - 2 * chip, 2), pl.ds(s["lo"], s["size"])]
            s["planes"] = 2
        else:
            size = s["size"] // 2
            keep = s["lo"] + bit_of[axis] * size
            away = s["lo"] + (1 - bit_of[axis]) * size
            src = region(u, s["planes"], pl.multiple_of(away, share), size)
            s["lo"], s["size"] = pl.multiple_of(keep, share), size
        slot = sum(len(orders[v]) for v in range(u)) + k
        s["copy"] = Remote(copies, src, recv[u][k], usend.at[slot], urecv.at[slot], partner[axis])
        took = s["size"] * s["planes"] * LANES * 2 * 2 / 80e3
        links = {"y": {"y": 1}, 0: {"x": 1}, 1: {"inner": 1}}.get(axis, {"inner": 1, "middle": 2})
        begin = max([clock[0]] + [free.get(link, 0.0) for link in links])
        for link, share_of in links.items():
            free[link] = begin + took * share_of
        s["due"] = max(free[link] for link in links) + 4.0
        pending.append(u)

    def finish_stage(u):
        s = state[u]
        k = s["stage"]
        s["copy"].wait_recv()
        last = k == len(orders[u]) - 1
        mine = pl.ds(4 * u, 4) if s["planes"] == 4 else pl.ds(4 * u + 2 * chip, 2)
        if last:
            total = part[mine, pl.ds(s["lo"], s["size"])] + recv[u][k][...]
            if u == MATS:
                fin[FEATURE_UNIT] = total[0]
                initg_ref[...] = total[1]
            else:
                fin[2 * u : 2 * u + 2] = total
            s["done"] = True
            done_units.append(u)
            gather_ready()
            return
        step = min(s["size"], 256)

        def add(i, carry):
            off = pl.multiple_of(i * step, step)
            rows = pl.ds(pl.multiple_of(s["lo"] + off, share), step)
            part[mine, rows, :] = part[mine, rows, :] + recv[u][k][:, pl.ds(off, step), :]
            return carry
        lax.fori_loop(0, s["size"] // step, add, 0)
        s["stage"] += 1
        send_stage(u)

    done_units, gathers = [], []
    groups = [[0, 1, 2], [3, 4, 5], [6, 7, 8]]

    def gather_ready():
        while len(gathers) < len(groups) and all(u in done_units for u in groups[len(gathers)]):
            g = groups[len(gathers)]
            span = pl.ds(2 * g[0], 6 if g[-1] < MATS else 5)
            from_chip = remote(fin.at[span], fin_in.at[span], across)
            remote(fin.at[span], gat_ref.at[row, span], peer)
            gathers.append((g, from_chip, local(fin.at[span], gat_ref.at[row, span], len(gathers))))

    def serve():
        at = min((state[u]["due"], u) for u in pending) if pending else (1e9, None)
        if small["due"] <= at[0]:
            clock[0] = max(clock[0], small["due"])
            small_step()
        else:
            clock[0] = max(clock[0], at[0]) + 0.3
            pending.remove(at[1])
            finish_stage(at[1])

    def next_due():
        return min([small["due"]] + [state[u]["due"] for u in pending])

    def tick(us):
        clock[0] += 1.6 * us
        while next_due() <= clock[0]:
            serve()

    def begin_unit(u):
        state[u] = dict(stage=0, planes=4, lo=0, size=width, done=False)
        send_stage(u)

    def position(u, block):
        seq_bits = [a for a in orders[u] if a != "y"]
        pos = 0
        for at, b in enumerate(seq_bits):
            pos = pos + ((block // (1 << b)) % 2) * (1 << (bits - 1 - at))
        return pos

    def store_plane(u, plane, side, value):
        if share != LANES:
            value = value.astype(F32).T.astype(BF)
        for block_at in range(shards):
            place = pl.ds(position(u, block_at) * share, share)
            if share == LANES:
                part[pl.ds(4 * u + 2 * plane + side, 1), place, :] = value[:, block_at * share : (block_at + 1) * share][None]
            else:
                part[pl.ds(4 * u + 2 * plane + side, 1), place, :] = value[block_at * share : (block_at + 1) * share][None]

    def weight_grad(m):
        left = LEFT[m]
        act_copies[left].wait_recv()
        grad_copies[m].wait_recv()

        def run(plane, carry):
            own = pl.ds(pl.multiple_of(core * half + plane * MAIN, MAIN), MAIN)
            theirs = pl.ds(pl.multiple_of(plane * MAIN, MAIN), MAIN)
            lefts = jnp.concatenate([acts[act(left), own], acts_in[left, :, theirs]], axis=0)
            total = dot_tn(lefts, gall[m].reshape(2 * count, width)).astype(BF)
            store_plane(m, plane, 0, total[:LANES])
            store_plane(m, plane, 1, total[LANES:])
            return carry
        lax.fori_loop(0, 2, run, 0)
        begin_unit(m)

    cot_rows = pl.ds(pl.multiple_of(chip * block, block), block)
    c_own = local(cot_hbm.at[chip], gall.at[DOWN2, 0, cot_rows], 3)
    zbuf[pl.ds(chip, 1)] = init_ref[...][None]
    unit, unused = norm_parts(init_ref[...].astype(F32))
    own_normed = (unit * gain_refs[3][...]).astype(BF)
    w = weight(WQ)
    queries = dot(own_normed, w[...]).astype(BF)
    weight_done()
    wk_copy.wait()
    fill_rest(w_rest, wkv)
    fold_main = dot_nt(queries, wkv[:MAIN, :]) * cross_scale
    fold_rest = dot_nt(queries, w_rest[...]) * cross_scale
    own_rows = pl.ds(pl.multiple_of(row * block, block), block)
    seg = seg_ref[...].astype(F32)
    ids = jnp.concatenate([seg, jnp.zeros((LANES - 2, block), F32)], axis=0).T
    ids = pltpu.roll(ids, 5, 1)
    fold[own_rows, :MAIN] = fold_main.astype(BF)
    fold[own_rows, MAIN:] = (fold_rest + ids).astype(BF)
    wv_copy.start()
    pl.semaphore_wait(barrier, len(partners))
    fold_copies = [remote(fold.at[own_rows], fold.at[own_rows], p) for p in (across, diagonal, peer)]
    z_copy = remote(init_ref, zbuf.at[chip], across)
    c_copy = remote(cot_hbm.at[1 - chip], gall.at[DOWN2, 0, cot_rows], across)
    group = pixel_rs.shape[0]
    blocks = group // 4
    tall = gain_col.shape[0]

    fold_in = width // group

    def pixel_row(f, lo=0, rows=group):
        at = pl.ds(pl.multiple_of((f % fold_in) * group + lo, rows), rows)
        return part[pl.ds(f // fold_in, 1), at, :][0].astype(F32)

    zero = jnp.zeros((group, LANES), F32)
    for copy in pixel_copies:
        copy.wait()
    mean = lax.fori_loop(0, features, lambda f, acc: acc + pixel_row(f), zero, unroll=9)
    mean = mean * (1.0 / features)

    def spread(f, acc):
        centre = pixel_row(f) - mean
        return acc + centre * centre
    spread_sum = lax.fori_loop(0, features, spread, zero, unroll=9)
    rs_all = lax.rsqrt(spread_sum * (1.0 / features) + EPSILON)
    pixel_rs[...] = rs_all
    gain_col[...] = jnp.ones(gain_col.shape, F32)
    flat[features * group // 2 :, :] = jnp.zeros(((tall - features) * group // 2, LANES), F32)
    for s in range(2):
        xcat[s, 2 * MAIN + 16 :, :] = jnp.zeros((LANES - 16, xcat.shape[2]), BF)
    for k in range(2):
        half_rows = slice(k * (group // 2), (k + 1) * (group // 2))
        half_mean, half_rs = mean[half_rows], rs_all[half_rows]

        def scale(f, carry, k=k, half_mean=half_mean, half_rs=half_rs):
            value = pixel_row(f, k * (group // 2), group // 2)
            rows = pl.ds(pl.multiple_of(f * (group // 2), group // 2), group // 2)
            flat[rows, :] = (value - half_mean) * (half_rs * pixel_gain[f])
            if k == 0:
                gain_col[pl.ds(f, 1), :] = jnp.full((1, LANES), pixel_gain[f], F32)
            return carry
        lax.fori_loop(0, features, scale, 0, unroll=9)
        for s in range(2):
            for jb in range(blocks):
                cols = pl.ds(jb * LANES, LANES)
                value = flat[pl.ds(2 * jb + s, tall, stride=group // 2), :]
                xcat[s, k * MAIN : (k + 1) * MAIN, cols] = value[:MAIN].astype(BF)
                if k == 0:
                    rest0[s, :, cols] = value[MAIN:]
                else:
                    both = jnp.concatenate([rest0[s, :, cols], value[MAIN:]], axis=0)
                    xcat[s, 2 * MAIN : 2 * MAIN + 16, cols] = both.astype(BF)
    for copy in fold_copies:
        copy.wait_recv()

    lane = lax.broadcasted_iota(jnp.int32, (1, LANES), 1)
    image = (2 * row).astype(F32)

    def selectors(s, rows):
        ids = fold[rows, MAIN:].astype(F32)
        ids = jnp.where(s == 0, ids[:, 5:6], ids[:, 6:7])
        return jnp.where(ids == image, 1.0, 0.0), jnp.where(ids == image + 1.0, 1.0, 0.0)

    def spread_out(source, s, rows):
        first, second = selectors(s, rows)
        main = source[:, :MAIN].astype(F32)
        rest = jnp.where(lane < 5, source[:, MAIN:].astype(F32), 0.0)
        rest = rest * first + pltpu.roll(rest, 8, 1) * second
        return jnp.concatenate([main * first, main * second, rest], axis=1).astype(BF)

    def pull_in(s, rows, zero, one, rest):
        first, second = selectors(s, rows)
        rest = jnp.where(lane < 5, rest * first + pltpu.roll(rest, LANES - 8, 1) * second, 0.0)
        return zero * first + one * second, rest

    slots = xcat.shape[2]
    core_copies = []

    def send_core(turn):
        core_copies.append(remote(amat.at[turn, :, 1 - core], ain1.at[turn], peer))

    def core_sum(turn):
        core_copies[turn].wait_recv()
        return amat[turn, :, pl.ds(core, 1)][:, 0] + ain1[turn]

    for turn in range(2):
        s = 1 - chip if turn == 0 else chip
        seq = pl.ds(s, 1)
        for i in range(4):
            rows = pl.ds(i * block, block)
            gall[2 + 2 * turn + i // 2, 0, (i % 2) * block : (i % 2 + 1) * block, :CAT] = spread_out(
                fold[rows, :], s, rows
            )
        first_ok = jnp.where(pseg_ref[seq, :slots] == 2 * row, 1.0, 0.0)
        second_ok = jnp.where(pseg_ref[seq, slots:] == 2 * row + 1, 1.0, 0.0)

        def score_cols(cols, seq=seq, turn=turn):
            queries_cat = jnp.concatenate(
                [gall[2 + 2 * turn, 0, :, :CAT], gall[3 + 2 * turn, 0, :, :CAT]], axis=0
            )
            fbuf[:, cols] = dot(queries_cat, xcat[seq, :, cols][0])
        columns_loop(score_cols, 512, slots)
        if turn == 1:
            asum[...] = core_sum(0)
            step2 = remote(asum, ain2, across)

        def soften(rows, s=s, seq=seq, first_ok=first_ok, second_ok=second_ok):
            first, unused = selectors(s, rows)
            allowed = second_ok + first * (first_ok - second_ok)
            scores = jnp.where(allowed > 0.5, fbuf[rows, :], NEGATIVE)
            weights = jnp.exp(scores - jnp.max(scores, axis=1, keepdims=True))
            prob = (weights * (1.0 / jnp.sum(weights, axis=1, keepdims=True))).astype(BF)
            pbuf[seq, rows, :] = prob[None]
        rows_loop(soften, 64, lat)
        probs = pbuf[seq][0]
        zero = dot_nt(probs, xcat[seq, :MAIN, :][0])
        one = dot_nt(probs, xcat[seq, MAIN : 2 * MAIN, :][0])
        rest = dot_nt(probs, xcat[seq, 2 * MAIN :, :][0])
        main, rest = pull_in(s, pl.ds(0, lat), zero, one, rest)
        amat[turn, :, :, :, :MAIN] = main.astype(BF).reshape(2, 2, block, MAIN)
        amat[turn, :, :, :, MAIN:] = rest.astype(BF).reshape(2, 2, block, LANES)
        send_core(turn)
    spill = local(pbuf, pspill, 4)

    for at in range(4):
        who = core if at < 2 else 1 - core
        rows = pl.ds(pl.multiple_of((2 * (at % 2) + who) * block, block), block)
        turned = fold[rows, MAIN:].astype(F32).T
        idrow[:, at * block : (at + 1) * block] = jnp.where(chip == 0, turned[5:6], turned[6:7])
    own_ids = []
    for h in range(2):
        rows = pl.ds(pl.multiple_of((2 * h + core) * block, block), block)
        ids = fold[rows, MAIN:].astype(F32)
        own_ids.append(jnp.where(chip == 0, ids[:, 5:6], ids[:, 6:7]))
    idcol = jnp.concatenate(own_ids, axis=0)
    z_copy.wait_recv()
    remote(init_ref, zall.at[row], peer)
    other_row = row + 2 - 4 * chip
    remote(zbuf.at[1 - chip], zall.at[other_row], peer)
    z_local = [local(init_ref, zall.at[row], 5), local(zbuf.at[1 - chip], zall.at[other_row], 6)]
    c_copy.wait_recv()
    c_own.wait()
    share_grad(DOWN2)
    wv_copy.wait()
    fill_rest(w_rest, wkv)
    step2.wait_recv()
    amix[...] = (core_sum(1) + ain2[...]).reshape(count, FEAT_PAD)
    amix_copy = remote(amix, amix_in, peer)

    def attended_cols(cols):
        value = dot(amix[:, :MAIN], wkv[:MAIN, cols]) + dot(amix[:, MAIN:], w_rest[:, cols])
        qbuf[:, cols] = value.astype(BF)
    columns_loop(attended_cols)
    w = weight(WO)

    def one_cols(cols):
        start = zbuf[:, :, cols].reshape(count, cols.size).astype(F32)
        stream[:, cols] = start + dot(qbuf[...], w[:, cols])
    columns_loop(one_cols)
    weight_done()

    def mlp(k, normed, active, up_id, down_id):
        layer(k, normed)
        share_act(normed)
        w_up = weight(up_id)

        def up_cols(cols):
            value, slope = gelu_parts(dot(acts[act(normed), :], w_up[:, cols]))
            acts[act(active), cols] = value.astype(BF)
            slopes[active // 4, :, cols] = slope.astype(BF)
        columns_loop(up_cols)
        weight_done()
        share_act(active)
        w_down = weight(down_id)

        def down_cols(cols):
            stream[:, cols] += dot(acts[act(active), :], w_down[:, cols])
        columns_loop(down_cols)
        weight_done()

    mlp(0, NORMED1, ACTIVE1, UP, DOWN)
    layer(1, SELFN)
    share_act(SELFN)
    kv_copies = {}
    for index, dst in ((KW, 0), (VW, 1), (QW, None)):
        w_now = weight(index)

        def project(cols, dst=dst, w_now=w_now):
            value = dot(acts[act(SELFN), :], w_now[:, cols]).astype(BF)
            if dst is None:
                qbuf[:, cols] = value
            else:
                kv[dst, 0, :, cols] = value
        columns_loop(project)
        weight_done()
        if dst is not None:
            kv_copies[dst] = remote(kv.at[dst, 0], kv.at[dst, 1], peer)
    spill.wait()
    kv_copies[0].wait_recv()
    kv_copies[1].wait_recv()

    def heads(body):
        def run(pair, carry):
            for side in range(2):
                cols = pl.ds(pl.multiple_of((2 * pair + side) * head_width, head_width), head_width)
                rows = pl.ds(pl.multiple_of((pair % 2) * count, count), count)
                body(cols, (pl.ds(pair // 2, 1), rows, pl.ds(side * lat, lat)))
            return carry
        lax.fori_loop(0, HEADS // 2, run, 0, unroll=2)

    def attend(cols, keep):
        keys = kv[0, :, :, cols].reshape(lat, head_width)
        values = kv[1, :, :, cols].reshape(lat, head_width)
        scores = dot_nt(qbuf[:, cols], keys) * self_scale
        scores = jnp.where(idcol == idrow[...], scores, NEGATIVE)
        weights = jnp.exp(scores - jnp.max(scores, axis=1, keepdims=True))
        prob = (weights * (1.0 / jnp.sum(weights, axis=1, keepdims=True))).astype(BF)
        pbuf[keep] = prob[None]
        acts[act(MIXED), cols] = dot(prob, values).astype(BF)
    heads(attend)
    share_act(MIXED)
    w_so = weight(SO)

    def three_cols(cols):
        stream[:, cols] += dot(acts[act(MIXED), :], w_so[:, cols])
    columns_loop(three_cols)
    weight_done()
    mlp(2, NORMED2, ACTIVE2, UPB, DOWNB)
    dmix[...] = stream[...].astype(BF)
    lat_ref[pl.ds(chip, 1)] = dmix[pl.ds(pl.multiple_of(chip * block, block), block), :][None]
    lat_copy = remote(
        dmix.at[pl.ds(pl.multiple_of((1 - chip) * block, block), block)], lat_ref.at[chip], across
    )

    weight_grad(DOWN2)
    tick(2.0)

    def mlp_back(k, normed, active, m_down, m_up, up_id, down_id, into, start=None):
        w_down = weight(down_id)

        def act_cols(cols):
            grad = dot_nt(gall[m_down, 0], w_down[cols, :]).astype(BF).astype(F32)
            gall[m_up, 0, :, cols] = (grad * slopes[active // 4, :, cols].astype(F32)).astype(BF)
        columns_loop(act_cols)
        weight_done()
        share_grad(m_up)
        tick(1.0)
        w_up = weight(up_id)

        def norm_cols(cols):
            dnorm[:, cols] = dot_nt(gall[m_up, 0], w_up[cols, :])
        columns_loop(norm_cols)
        weight_done()
        if into == 0:
            grad_copies[DOWN2].wait_send()
            grad_copies[UP2].wait_send()
        layer_back(k, normed, into, start)
        tick(1.5)

    mlp_back(2, NORMED2, ACTIVE2, DOWN2, UP2, UPB, DOWNB, SOUT, DOWN2)

    share_grad(SOUT)
    weight_grad(UP2)
    tick(1.5)
    w_so2 = weight(SO)
    lat_copy.wait_send()

    def mixed_cols(cols):
        dmix[:, cols] = dot_nt(gall[SOUT, 0], w_so2[cols, :]).astype(BF)
    columns_loop(mixed_cols)
    weight_done()

    def attend_back(cols, keep):
        keys = kv[0, :, :, cols].reshape(lat, head_width)
        values = kv[1, :, :, cols].reshape(lat, head_width)
        dm = dmix[:, cols]
        prob_b = pbuf[keep][0]
        prob = prob_b.astype(F32)
        grad = dot_nt(dm, values)
        delta = jnp.sum(prob * grad, axis=1, keepdims=True)
        score = (prob * (grad - delta)).astype(BF)
        gall[SQ, 0, :, cols] = (dot(score, keys) * self_scale).astype(BF)
        dk = (dot_tn(score, qbuf[:, cols]) * self_scale).astype(BF)
        dv = dot_tn(prob_b, dm).astype(BF)
        gall[SK, 0, :, cols] = dk[:count]
        gall[SV, 0, :, cols] = dv[:count]
        kv[0, 1, :, cols] = dk[count:]
        kv[1, 1, :, cols] = dv[count:]
    heads(attend_back)
    unspill = local(pspill, pbuf, 4)
    share_dkv = remote(kv.at[:, 1], dkv_in, peer)
    share_grad(SQ)
    tick(4.0)
    weight_grad(SOUT)
    tick(1.0)
    share_dkv.wait_recv()

    def add_kv(rows):
        for at, m in ((0, SK), (1, SV)):
            gall[m, 0, rows, :] = gall[m, 0, rows, :] + dkv_in[at, rows, :]
    rows_loop(add_kv)
    share_grad(SK)
    share_grad(SV)
    for at, (m, index) in enumerate(((SQ, QW), (SK, KW), (SV, VW))):
        w_now = weight(index)

        def normed_cols(cols, at=at, m=m, w_now=w_now):
            value = dot_nt(gall[m, 0], w_now[cols, :])
            if at == 0:
                dnorm[:, cols] = value
            else:
                dnorm[:, cols] += value
        columns_loop(normed_cols)
        weight_done()
    layer_back(1, SELFN, DOWN1)
    share_grad(DOWN1)
    tick(3.0)
    weight_grad(SQ)
    tick(1.0)
    weight_grad(SK)
    tick(1.0)
    mlp_back(0, NORMED1, ACTIVE1, DOWN1, UP1, UP, DOWN, 0)

    w_o = weight(WO)

    def attended_back(cols):
        gall[1, 0, :, cols] = dot_nt(gall[0, 0], w_o[cols, :]).astype(BF)
    columns_loop(attended_back)
    weight_done()
    share_cd = remote(gall.at[1 - core, 0], gcd_in, peer)
    folded = jnp.concatenate([dot_nt(gall[1, 0], wkv[:MAIN, :]), dot_nt(gall[1, 0], w_rest[...])], axis=1)
    along = jnp.sum(folded * amix[...].astype(F32), axis=0, keepdims=True)
    gsum[3:4, :FEAT_PAD] = along
    gsum[3:4, FEAT_PAD:] = jnp.zeros((1, width - FEAT_PAD), F32)
    da_all[pl.ds(chip, 1), :, pl.ds(core, 1)] = folded.astype(BF).reshape(1, 2, 1, block, FEAT_PAD)
    mine = da_all.at[chip, :, core]
    da_across = remote(mine, mine, across)
    da_peer = remote(mine, mine, peer)
    tick(2.0)
    weight_grad(SV)
    tick(1.0)
    da_across.wait_recv()
    other = da_all.at[1 - chip, :, core]
    da_other = remote(other, other, peer)
    weight_grad(DOWN1)
    tick(1.0)
    weight_grad(UP1)
    tick(1.0)

    share_cd.wait_recv()
    amix_copy.wait_recv()
    lefts = jnp.concatenate([amix[:, :MAIN], amix_in[:, :MAIN]], axis=0)
    grads = jnp.concatenate([gall[pl.ds(core, 1), 0][0], gcd_in[...]], axis=0)
    total = dot_tn(lefts, grads).astype(BF)
    for plane in range(2):
        store_plane(MATS, plane, 0, total[plane * LANES : (plane + 1) * LANES])
    for plane in range(2):
        store_plane(MATS, plane, 1, upstr[plane * block : (plane + 1) * block, :].astype(BF))
    begin_unit(MATS)
    gsum[4:, :] = jnp.zeros((gsum.shape[0] - 4, width), F32)
    rests = [dot_tn(amix[:, MAIN:], gall[side, 0])[:8] for side in range(2)]
    for i in range(8):
        cols = slice(i * LANES, (i + 1) * LANES)
        both = jnp.concatenate([rests[0][:, cols], rests[1][:, cols]], axis=0)
        sm[16 * i : 16 * (i + 1), FEAT_PAD:] = both.astype(BF)
        sm[128 + 16 * i : 128 + 16 * (i + 1), FEAT_PAD:] = gsum[:, cols].astype(BF)
    sm[256:, FEAT_PAD:] = jnp.zeros((lat - 256, LANES), BF)
    tick(2.0)

    da_peer.wait_recv()
    da_other.wait_recv()
    unspill.wait()

    def score_rows(s):
        return wslots.at[s, pl.ds(0, lat)]

    def da_rows(s):
        return wslots.at[s, pl.ds(lat, lat), pl.ds(0, CAT)]

    def q_rows(s):
        return wslots.at[2, pl.ds(s * lat, lat), pl.ds(0, CAT)]

    for s in range(2):
        for i in range(4):
            rows = pl.ds(i * block, block)
            wslots[s, lat + i * block : lat + (i + 1) * block, :CAT] = spread_out(
                da_all[s, i // 2, i % 2], s, rows
            )
            wslots[2, s * lat + i * block : s * lat + (i + 1) * block, :CAT] = spread_out(
                fold[rows, :], s, rows
            )

        def back_cols(cols, s=s):
            fbuf[:, cols] = dot(wslots[s, lat:, :CAT], xcat[s, :, cols])
        columns_loop(back_cols, 512, slots)

        def score_back(rows, s=s):
            prob = pbuf[s, rows, :].astype(F32)
            grad = fbuf[rows, :]
            delta = jnp.sum(prob * grad, axis=1, keepdims=True)
            wslots[s, rows, :] = (prob * (grad - delta)).astype(BF)
        rows_loop(score_back, 64, lat)
        scores = wslots[s, :lat, :]
        zero = dot_nt(scores, xcat[s, :MAIN, :])
        one = dot_nt(scores, xcat[s, MAIN : 2 * MAIN, :])
        rest = dot_nt(scores, xcat[s, 2 * MAIN :, :])
        main, rest = pull_in(s, pl.ds(0, lat), zero, one, rest)
        if s == 0:
            bsum[:, :MAIN] = main
            bsum[:, MAIN:] = rest
        else:
            sm[:, :MAIN] = (bsum[:, :MAIN] + main).astype(BF)
            sm[:, MAIN:FEAT_PAD] = (bsum[:, MAIN:] + rest).astype(BF)
        tick(4.0)

    small_send()
    for copy in act_copies.values():
        copy.wait_send()
    for s in range(2):
        for at, (lo, size) in enumerate(((0, MAIN), (MAIN, MAIN), (2 * MAIN, LANES))):
            cols = pl.ds(lo, size)
            total = dot_tn(wslots[2, s * lat : (s + 1) * lat, cols], wslots[s, :lat, :])
            total = total + dot_tn(wslots[s, lat:, cols], pbuf[s])
            acts[pl.ds(s * CAT + lo, size), :] = total.astype(BF)
            tick(2.0)

    main_gain, rest_gain = gain_col[:MAIN, :], gain_col[MAIN:, :]
    inverse[...] = 1.0 / gain_col[...]
    y_copy = None
    for k in range(2):
        if y_copy is not None:
            y_copy.wait()
        for s in range(2):

            def pixel_step(jb, carry, k=k, s=s):
                cols = pl.ds(pl.multiple_of(jb * LANES, LANES), LANES)
                up_main = acts[s * CAT + k * MAIN : s * CAT + (k + 1) * MAIN, cols].astype(F32)
                up_rest = acts[s * CAT + 2 * MAIN : s * CAT + 2 * MAIN + 16, cols].astype(F32)
                up_rest = up_rest[8 * k : 8 * k + 8]
                x_main = xcat[s, k * MAIN : (k + 1) * MAIN, cols].astype(F32)
                x_rest = xcat[s, 2 * MAIN : 2 * MAIN + 16, cols].astype(F32)[8 * k : 8 * k + 8]
                rs = pixel_rs[pl.ds(k * (group // 2) + 2 * jb + s, 1), :]
                scaled_main, scaled_rest = up_main * main_gain, up_rest * rest_gain

                def mean_of(a, b):
                    whole = jnp.sum(a, axis=0, keepdims=True) + jnp.sum(b, axis=0, keepdims=True)
                    return whole * (1.0 / features)
                centre = mean_of(scaled_main, scaled_rest)
                along = mean_of(up_main * x_main, up_rest * x_rest)
                unit_main, unit_rest = x_main * inverse[:MAIN, :], x_rest * inverse[MAIN:, :]
                out_main = rs * (scaled_main - centre - unit_main * along)
                out_rest = rs * (scaled_rest - centre - unit_rest * along)
                flat[pl.ds(2 * jb + s, tall, stride=group // 2), :] = jnp.concatenate(
                    [out_main, out_rest], axis=0
                )
                return carry
            lax.fori_loop(0, blocks, pixel_step, 0)
            tick(2.0)
        y_copy = local(flat.at[pl.ds(0, features * group // 2)], y_ref.at[k], 7 + k)
    while next_due() < 1e9:
        serve()
    for g, from_chip, own in gathers:
        from_chip.wait_recv()
        span = pl.ds(2 * g[0], 6 if g[-1] < MATS else 5)
        remote(fin_in.at[span], gat_ref.at[other_row, span], peer)
        own.wait()
        z_local.append(local(fin_in.at[span], gat_ref.at[other_row, span], 9 + g[0] // 3))
    for copy in z_local + [y_copy]:
        copy.wait()
    for copy in copies:
        copy.finish()


def finish_kernel(*refs):
    it = iter(refs)

    def take(n=None):
        return next(it) if n is None else [next(it) for _ in range(n)]

    y_in, lat_in = take(2)
    ins = take(8)
    query_gain, pixel_gain = take(2)
    y_out, lat_out, init_out, pixel_gain_out, key_out, value_out = take(6)
    gain_outs = take(4)
    mat_outs = take(MATS + 2)
    held = take(8)
    summed, small, fold, init_all, wq, wk, wv, init_sum = held
    unit, normed, total, mats, wk_rest, wv_rest, y_buf, lat_buf, back = take(9)
    sem, out_sem = take(2)
    features, width = ins[5].shape
    lat = init_all.shape[0]
    block = lat // 4
    j = lax.axis_index("seq")
    row = lax.axis_index("row")
    cross_scale = 1.0 / math.sqrt(width)

    through = [
        (pltpu.make_async_copy(y_in.at[k], y_buf.at[:, pl.ds(k * y_in.shape[2], y_in.shape[2])], sem.at[8 + k]))
        for k in range(2)
    ] + [pltpu.make_async_copy(lat_in, lat_buf, sem.at[10])]
    copies = []
    for i, (src, dst) in enumerate(zip(ins, held)):
        copies.append(pltpu.make_async_copy(src, dst, sem.at[i]))
        copies[-1].start()
        if i == 0:
            for copy in through:
                copy.start()
    outs = []

    def put(src, dst):
        copy = pltpu.make_async_copy(src, dst, out_sem.at[len(outs)])
        copy.start()
        outs.append(copy)

    copies[0].wait()
    for m in range(MATS):
        for r in range(4):
            for h in range(2):
                at = (r % 2) * (width // 2) + (r // 2) * 2 * LANES + h * LANES
                mats[m, at : at + LANES, :] = summed[r, 2 * m + h].astype(F32)
        put(mats.at[m], mat_outs[m])
    copies[3].wait()
    query_rs = []
    for r in range(4):
        rows = pl.ds(r * block, block)
        value, scale = norm_parts(init_all[rows, :].astype(F32))
        unit[rows, :] = value
        normed[rows, :] = (value * query_gain[...]).astype(BF)
        query_rs.append(scale)
    for copy in through:
        copy.wait()
    put(y_buf, y_out)
    put(lat_buf, lat_out)
    for copy in copies[1:3] + copies[4:]:
        copy.wait()
    fill_rest(wv_rest, wv)
    fill_rest(wk_rest, wk)
    my_cols = pl.ds(pl.multiple_of(j * LANES, LANES), LANES)

    for n in range(width // 256):
        cols = pl.ds(n * 256, 256)
        value = dot(small[:, :MAIN], wk[:MAIN, cols]) + dot(small[:, MAIN:FEAT_PAD], wk_rest[:, cols])
        total[:, cols] = (value * cross_scale).astype(BF)

    def put_turned(index, value):
        for n in range(width // LANES):
            mats[index, n * LANES : (n + 1) * LANES, :] = value[:, n * LANES : (n + 1) * LANES].T
        put(mats.at[index], mat_outs[index])
    put_turned(MATS, dot_tn(total[:, my_cols], normed[...]))
    outer = [
        [summed[2 * y + c, FEATURE_UNIT].astype(F32) for y in range(2)] for c in range(2)
    ]
    rests = small[pl.ds(pl.multiple_of(j * 16, 16), 16), FEAT_PAD:]
    value_out[:LANES, :] = outer[1][0]
    value_out[LANES:MAIN, :] = outer[1][1]
    value_out[MAIN:, :] = rests.astype(F32)[8 : 8 + features - MAIN]
    summed_c = jnp.concatenate(outer[0], axis=0).astype(BF)
    put_turned(MATS + 1, dot_tn(summed_c, wv[:MAIN, :]) + dot_tn(rests, wv_rest[:16, :]))
    my_queries = dot(normed[...], wq[:, my_cols]).astype(BF)
    key_turned = dot_tn(my_queries, small[:, :FEAT_PAD]) * cross_scale
    key_out[...] = jnp.concatenate(
        [key_turned[:, n * LANES : (n + 1) * LANES].T for n in range(3)], axis=0
    )[:features]
    for i in range(8):
        chunk = small[128 + 16 * i : 128 + 16 * (i + 1), FEAT_PAD:].astype(F32)
        for g in range(3):
            gain_outs[g][i : i + 1, :] = chunk[g : g + 1]
    scores = small[:, :FEAT_PAD].astype(F32)
    part = jnp.sum(fold[...].astype(F32) * scores, axis=0, keepdims=True)
    rest_sum = [small[128 + 16 * i : 128 + 16 * (i + 1), FEAT_PAD:].astype(F32)[3:4] for i in range(3)]
    whole = (part + jnp.concatenate(rest_sum, axis=1))[:, :features]
    pixel_gain_out[...] = (whole / pixel_gain[...].reshape(1, features)).reshape(features)
    own = pl.ds(pl.multiple_of(row * block, block), block)
    own_rs = query_rs[0]
    for r in range(1, 4):
        own_rs = jnp.where(row == r, query_rs[r], own_rs)
    sums = jnp.zeros((block, 1), F32)
    alongs = jnp.zeros((block, 1), F32)
    for n in range(width // 256):
        cols = pl.ds(n * 256, 256)
        back[:, cols] = dot_nt(total[...], wq[cols, :])
        row_sum = jnp.sum(back[:, cols] * unit[:, cols], axis=0, keepdims=True)
        for i in range(2):
            gain_outs[3][2 * n + i : 2 * n + i + 1, :] = row_sum[:, i * LANES : (i + 1) * LANES]
        scaled = back[own, cols] * query_gain[:, cols]
        sums = sums + jnp.sum(scaled, axis=1, keepdims=True)
        alongs = alongs + jnp.sum(scaled * unit[own, cols], axis=1, keepdims=True)
    scaled = back[own, my_cols] * query_gain[:, my_cols]
    query_in = own_rs * (scaled - sums * (1.0 / width) - unit[own, my_cols] * (alongs * (1.0 / width)))
    init_out[...] = init_sum[...].astype(F32) + query_in
    for copy in outs:
        copy.wait()


def finish(y, latents, summed, small, init_sum, fold, init_all, wq, wk, wv, query_gain, pixel_gain):
    features, width = wk.shape
    lat = init_all.shape[0]
    block = lat // 4
    vmem = pl.BlockSpec(memory_space=pltpu.VMEM)
    hbm = pl.BlockSpec(memory_space=pl.ANY)

    def f32(*shape):
        return jax.ShapeDtypeStruct(shape, F32)

    outs = pl.pallas_call(
        finish_kernel,
        out_shape=[f32(features, 2 * y.shape[2], LANES), jax.ShapeDtypeStruct(latents.shape, BF), f32(block, LANES),
                   f32(features), f32(features, LANES), f32(features, LANES)]
        + [f32(width // LANES, LANES)] * 4 + [f32(width, LANES)] * (MATS + 2),
        in_specs=[hbm] * 10 + [vmem] * 2,
        out_specs=[hbm] * 2 + [vmem] * 8 + [hbm] * (MATS + 2),
        scratch_shapes=[
            pltpu.VMEM(shape, BF)
            for shape in (summed.shape, small.shape, fold.shape, init_all.shape,
                          wq.shape, wk.shape, wv.shape, init_sum.shape)
        ]
        + [
            pltpu.VMEM((lat, width), F32),
            pltpu.VMEM((lat, width), BF),
            pltpu.VMEM((lat, width), BF),
            pltpu.VMEM((MATS + 2, width, LANES), F32),
            pltpu.VMEM((LANES, width), BF),
            pltpu.VMEM((LANES, width), BF),
            pltpu.VMEM((features, 2 * y.shape[2], LANES), F32),
            pltpu.VMEM(latents.shape, BF),
            pltpu.VMEM((lat, width), F32),
            pltpu.SemaphoreType.DMA((11,)),
            pltpu.SemaphoreType.DMA((MATS + 4,)),
        ],
        compiler_params=pltpu.CompilerParams(vmem_limit_bytes=VMEM_LIMIT),
    )(y, latents, summed, small, fold, init_all, wq, wk, wv, init_sum, query_gain[None],
      pixel_gain)
    y, latents, init_grad, pixel_gain_grad, key_grad, value_grad = outs[:6]
    return (y, latents, init_grad, outs[6:10], pixel_gain_grad, key_grad, value_grad, outs[10:])


def whole_stack(shards, z, pixel_gain, pseg, init, cots, seg, wk, wv, gains, weights):
    width = init.shape[1]
    block = init.shape[0]
    count = 2 * block
    lat = 2 * count
    share = width // shards
    half = width // 2
    bits = shards.bit_length() - 1
    orders = unit_orders(bits)
    nslots = 3
    features = wk.shape[0]
    group = z.shape[0] // features
    slots = group * LANES // 4
    small, size = [], lat
    for i in range(bits + 2):
        size = size // 2 if size > 16 else size
        small.append((size, 512))
    scratch = [
        ((nslots, width, width), BF),
        (wk.shape, BF),
        ((LANES, width), BF),
        ((2, block, width), BF),
        ((2, 2, block, FEAT_PAD), BF),
        ((2, block, FEAT_PAD), BF),
        ((2, block, FEAT_PAD), BF),
        ((count, FEAT_PAD), BF),
        ((count, FEAT_PAD), BF),
        ((2, 2, 2, block, FEAT_PAD), BF),
        ((lat, width), F32),
        ((3, count, LANES), F32),
        ((6 * count, width), BF),
        ((6, count, half), BF),
        ((2, count, width), BF),
        ((count, width), BF),
        ((2, 2, count, width), BF),
        ((2, lat, slots), BF),
        ((count, width), BF),
        ((2, count, width), BF),
        ((MATS, 2, count, width), BF),
        ((count, width), BF),
        ((FEATURE_UNIT + 1, share, LANES), BF),
        ((2, 2, 2, block, FEAT_PAD), BF),
        ((lat, FEAT_PAD), F32),
        ((16, width), F32),
        ((1, lat), F32),
        ((lat, 512), BF),
        ((2, CAT, slots), BF),
        (((MAIN + 8) * group // 2, LANES), F32),
        ((2, 8, slots), F32),
        ((group, LANES), F32),
        ((MAIN + 8, LANES), F32),
        ((MAIN + 8, LANES), F32),
        ((FEATURE_UNIT + 1, share, LANES), BF),
        ((UNITS * 4, width, LANES), BF),
    ]
    for order in orders:
        scratch += [(shape, BF) for shape in stage_shapes(order, width)]
    scratch += [(shape, BF) for shape in small]
    stages = sum(len(order) for order in orders)
    vmem = pl.BlockSpec(memory_space=pltpu.VMEM)
    hbm = pl.BlockSpec(memory_space=pl.ANY)
    return pl.pallas_call(
        functools.partial(
            main_kernel, (shards, width, count, dict(small_stages=len(small)))
        ),
        out_shape=[
            jax.ShapeDtypeStruct((2, block, width), BF),
            jax.ShapeDtypeStruct((lat, 512), BF),
            jax.ShapeDtypeStruct((4, FEATURE_UNIT + 1, share, LANES), BF),
            jax.ShapeDtypeStruct((share, LANES), BF),
            jax.ShapeDtypeStruct((lat, FEAT_PAD), BF),
            jax.ShapeDtypeStruct((4, block, width), BF),
            jax.ShapeDtypeStruct((2, features * group // 2, LANES), F32),
            jax.ShapeDtypeStruct((2, lat, slots), BF),
        ],
        in_specs=[hbm, pl.BlockSpec(memory_space=pltpu.SMEM), vmem, vmem, hbm, vmem]
        + [hbm] * 2 + [vmem] * 4 + [hbm] * 10,
        out_specs=[vmem, vmem, hbm, vmem, vmem, hbm, hbm, hbm],
        scratch_shapes=[pltpu.VMEM(shape, kind) for shape, kind in scratch]
        + [
            pltpu.SemaphoreType.DMA((nslots + 2 + 13,)),
            pltpu.SemaphoreType.DMA((nslots * 4,)),
            pltpu.SemaphoreType.DMA((-(-z.shape[0] // width),)),
            pltpu.SemaphoreType.DMA((stages,)),
            pltpu.SemaphoreType.DMA((stages,)),
            pltpu.SemaphoreType.DMA((80,)),
            pltpu.SemaphoreType.DMA((80,)),
        ],
        compiler_params=pltpu.CompilerParams(
            collective_id=0, has_side_effects=True, vmem_limit_bytes=VMEM_LIMIT
        ),
    )(z, pixel_gain, pseg, init, cots, seg, wk, wv, *[g[None] for g in gains], *weights)


VMEM_LIMIT = 63 * 1024 * 1024


def body(
    pixels, pixel_seg, latent_seg, latent_init, cotangent,
    pixel_gain, query_gain, query_weight, key_weight, value_weight, output_weight,
    mlp_gain, up_weight, down_weight,
    self_gain, self_query, self_key, self_value, self_output,
    second_gain, second_up, second_down,
):
    seqs, pix, features = pixels.shape
    block, width = latent_init.shape
    shards = lax.axis_size("seq")
    lat = block * lax.axis_size("row")
    row = lax.axis_index("row")
    cross_scale = 1.0 / math.sqrt(width)
    tiles = pix // LANES

    z = pixels.transpose(2, 0, 1).reshape(features, seqs, tiles, LANES)
    z = z.transpose(0, 2, 1, 3).reshape(features * seqs * tiles, LANES)
    latents, small, summed, init_sum, fold, init_all, y, unused = whole_stack(
        shards, z, pixel_gain, pixel_seg, latent_init, cotangent, latent_seg, key_weight, value_weight,
        (mlp_gain, self_gain, second_gain, query_gain),
        (query_weight, output_weight, up_weight, down_weight, self_query, self_key, self_value,
         self_output, second_up, second_down),
    )
    init_all = init_all.reshape(lat, width)
    y = y.reshape(2, features, tiles, LANES)
    if width // shards == LANES:
        y, latents, init_grad, gains, pixel_gain_grad, key_grad, value_grad, mats = finish(
            y, latents, summed, small, init_sum, fold, init_all, query_weight, key_weight,
            value_weight, query_gain, pixel_gain,
        )
    else:
        y = y.transpose(1, 0, 2, 3)
    pixel_grad = y.reshape(features, tiles, seqs, LANES).transpose(2, 1, 3, 0)
    pixel_grad = pixel_grad.reshape(seqs, pix, features)
    if width // shards == LANES:
        mlp_gain_grad, self_gain_grad, second_gain_grad, query_gain_grad = [
            g.reshape(width) for g in gains
        ]
        return (
            latents, pixel_grad, init_grad, pixel_gain_grad,
            query_gain_grad, mlp_gain_grad, self_gain_grad, second_gain_grad,
            mats[MATS], key_grad, value_grad, mats[MATS + 1], mats[UP1], mats[DOWN1],
            mats[SQ], mats[SK], mats[SV], mats[SOUT], mats[UP2], mats[DOWN2],
        )

    share = width // shards
    at = lax.axis_index("seq") * share

    def columns(arr):
        return lax.dynamic_slice_in_dim(arr, at, share, arr.ndim - 1)

    score_b = small[:, :features]
    side = small[:, FEAT_PAD:]
    rests = side[:128].reshape(8, 2, 8, LANES).transpose(1, 2, 0, 3).reshape(2, 8, width)
    sums = side[128:256].reshape(8, 16, LANES).transpose(1, 0, 2).reshape(16, width).astype(F32)
    pixel_gain_grad = (
        jnp.sum(fold[:, :features].astype(F32) * score_b.astype(F32), axis=0) + sums[3, :features]
    ) / pixel_gain
    units = summed.reshape(2, 2, FEATURE_UNIT + 1, share, LANES)
    mats = units[:, :, :FEATURE_UNIT].reshape(2, 2, MATS, 2, share, LANES)
    mats = mats.transpose(2, 1, 0, 3, 5, 4).reshape(MATS, width, share).astype(F32)
    outer = units[:, :, FEATURE_UNIT].transpose(1, 0, 3, 2).reshape(2, MAIN, share)
    outer = jnp.concatenate([outer, columns(rests)[:, : features - MAIN]], axis=1)
    value_grad = outer[1].astype(F32)
    output_grad = dot_tn(value_weight, outer[0])
    query_unit, query_rs = norm_parts(init_all.astype(F32))
    query_normed = (query_unit * query_gain).astype(BF)
    my_queries = dot(query_normed, columns(query_weight)).astype(BF)
    key_grad = dot_tn(score_b, my_queries) * cross_scale
    query_total = (dot(score_b, key_weight) * cross_scale).astype(BF)
    query_grad = dot_tn(query_normed, columns(query_total))
    query_in, query_gain_grad = norm_back(
        query_unit, query_rs, query_gain, dot_nt(query_total, query_weight)
    )
    init_grad = init_sum.T.astype(F32) + lax.dynamic_slice(query_in, (row * block, at), (block, share))
    return (
        latents, pixel_grad, init_grad,
        pixel_gain_grad, query_gain_grad, sums[0], sums[1], sums[2],
        query_grad, key_grad, value_grad, output_grad, mats[UP1], mats[DOWN1],
        mats[SQ], mats[SK], mats[SV], mats[SOUT], mats[UP2], mats[DOWN2],
    )


def solution(mesh):
    placed = (
        P("seq", "row", None), P("seq", "row"), P("seq", "row"), P("row", None),
        P("seq", "row", None),
    ) + (P(),) * 17
    cols = P(None, "seq")
    return jax.shard_map(
        body,
        mesh=mesh,
        in_specs=placed,
        out_specs=(P("seq", "row", None), P("seq", "row", None), P("row", "seq"))
        + (P(),) * 5 + (cols,) * 12,
        check_vma=False,
    )
```

```python
import functools
import math

import jax
import jax.numpy as jnp
from jax import lax
from jax.experimental import pallas as pl
from jax.experimental.pallas import tpu as pltpu
from jax.sharding import PartitionSpec as P

HEADS = 8
EPSILON = 1e-05
NEGATIVE = -1e9
BF = jnp.bfloat16
F32 = jnp.float32
LANES = 128
FEAT_PAD = 384
MAIN = 256
CAT = 2 * MAIN + LANES
MESH = pl.DeviceIdType.MESH


def dot(a, b):
    return jnp.dot(a, b, preferred_element_type=F32)


def dot_tn(a, b):
    return lax.dot_general(a, b, (((0,), (0,)), ((), ())), preferred_element_type=F32)


def dot_nt(a, b):
    return lax.dot_general(a, b, (((1,), (1,)), ((), ())), preferred_element_type=F32)


def fill_rest(rest, matrix):
    rest[...] = jnp.zeros(rest.shape, rest.dtype)
    rest[: matrix.shape[0] - MAIN, :] = matrix[MAIN:, :]


def norm_parts(values):
    centre = values - jnp.mean(values, axis=-1, keepdims=True)
    rs = lax.rsqrt(jnp.mean(centre * centre, axis=-1, keepdims=True) + EPSILON)
    return centre * rs, rs


def norm_back(unit, rs, gain, upstream):
    scaled = upstream * gain
    grad = rs * (
        scaled
        - jnp.mean(scaled, axis=-1, keepdims=True)
        - unit * jnp.mean(scaled * unit, axis=-1, keepdims=True)
    )
    return grad, jnp.sum(upstream * unit, axis=0)


def gelu_parts(hidden):
    cdf = 0.5 * (1.0 + lax.erf(hidden * math.sqrt(0.5)))
    pdf = jnp.exp(-0.5 * hidden * hidden) * (1.0 / math.sqrt(2.0 * math.pi))
    return hidden * cdf, cdf + hidden * pdf


NORMED1, ACTIVE1, SELFN, MIXED, NORMED2, ACTIVE2 = range(6)
DOWN2, UP2, SOUT, SQ, SK, SV, DOWN1, UP1 = range(8)
LEFT = {
    DOWN2: ACTIVE2, UP2: NORMED2, SOUT: MIXED, SQ: SELFN, SK: SELFN, SV: SELFN,
    DOWN1: ACTIVE1, UP1: NORMED1,
}
MATS = 8
FEATURE_UNIT = 2 * MATS
UNITS = MATS + 1


class Remote:
    def __init__(self, log, src, dst, send_sem, recv_sem, device):
        self.copy = pltpu.make_async_remote_copy(
            src_ref=src, dst_ref=dst, send_sem=send_sem, recv_sem=recv_sem,
            device_id=device, device_id_type=MESH,
        )
        self.copy.start()
        self.arrived = self.sent = False
        log.append(self)

    def wait_recv(self):
        if not self.arrived:
            self.copy.wait_recv()
        self.arrived = True

    def wait_send(self):
        if not self.sent:
            self.copy.wait_send()
        self.sent = True

    def finish(self):
        self.wait_recv()
        self.wait_send()


KINDS = "FCDABCEBA"


def unit_orders(bits):
    first, second, tail = [0], list(range(1, min(bits, 2))), list(range(2, bits))
    kinds = {
        "A": ["y"] + first + second + tail,
        "B": first + second + ["y"] + tail,
        "C": second + first + ["y"] + tail,
        "D": first + ["y"] + second + tail,
        "E": second + ["y"] + first + tail,
        "F": ["y"] + second + first + tail,
    }
    return [kinds[letter] for letter in KINDS]


def stage_shapes(order, width):
    shapes, planes, size = [], 4, width
    for axis in order:
        if axis == "y":
            planes = 2
        else:
            size //= 2
        shapes.append((planes, size, LANES))
    return shapes


def main_kernel(cfg, *refs):
    shards, width, count, sizes = cfg
    bits = shards.bit_length() - 1
    share = width // shards
    half = width // 2
    block = count // 2
    lat = 2 * count
    head_width = width // HEADS
    cross_scale = 1.0 / math.sqrt(width)
    self_scale = 1.0 / math.sqrt(head_width)
    orders = unit_orders(bits)
    it = iter(refs)

    def take(n=None):
        return next(it) if n is None else [next(it) for _ in range(n)]

    (z_hbm, pixel_gain, pseg_ref, init_ref, cot_hbm, seg_ref, wk_hbm, wv_hbm) = take(8)
    gain_refs = take(4)
    w_hbm = take(10)
    (lat_ref, sm_out, gat_ref, initg_ref, fold, zall, y_ref, pspill) = take(8)
    (wslots, wkv, w_rest, zbuf, ain1, asum, ain2, amix, amix_in, amat, fbuf, rsb, acts, acts_in, slopes,
     qbuf, kv, pbuf, dmix, dkv_in, gall, gcd_in, fin, da_all, bsum, gsum, idrow,
     sm, xcat, flat, rest0, pixel_rs, gain_col, inverse, fin_in, part) = take(36)
    recv = [take(len(orders[u])) for u in range(UNITS)]
    smr = take(sizes["small_stages"])
    (wsem, psem, zsem, usend, urecv, csend, crecv) = take(7)

    j = lax.axis_index("seq")
    row = lax.axis_index("row")
    core, chip = row % 2, row // 2
    peer = {"row": row + 1 - 2 * core}
    across = {"row": row + 2 - 4 * chip}
    diagonal = {"row": 3 - row}
    bit_of = [(j // (1 << b)) % 2 for b in range(bits)]
    partner = {b: {"seq": j + (1 - 2 * bit_of[b]) * (1 << b)} for b in range(bits)}
    partner["y"] = across
    stream = fbuf.at[pl.ds(0, count)]
    upstr = fbuf.at[pl.ds(count, count)]
    dnorm = stream

    def act(k):
        return pl.ds(k * count, count)

    WQ, WO, UP, DOWN, QW, KW, VW, SO, UPB, DOWNB = range(10)
    uses = [WQ, WO, UP, DOWN, KW, VW, QW, SO, UPB, DOWNB, DOWNB, UPB, SO, QW, KW, VW, DOWN, UP, WO]
    nslots = wslots.shape[0]
    at_use = [0]

    pieces = 4

    class WeightCopy:
        def __init__(self, i):
            size = width // pieces
            self.copies = [
                pltpu.make_async_copy(
                    w_hbm[uses[i]].at[pl.ds(p * size, size)],
                    wslots.at[i % nslots, pl.ds(p * size, size)],
                    psem.at[(i % nslots) * pieces + p],
                )
                for p in range(pieces)
            ]

        def start(self):
            for copy in self.copies:
                copy.start()

        def wait(self):
            for copy in self.copies:
                copy.wait()

    def weight_copy(i):
        return WeightCopy(i)

    def weight(expect):
        i = at_use[0]
        assert uses[i] == expect
        at_use[0] += 1
        weight_copy(i).wait()
        return wslots.at[i % nslots]

    def weight_done():
        i = at_use[0] - 1 + nslots
        if i < len(uses):
            weight_copy(i).start()

    features = wk_hbm.shape[0]
    pixel_copies = []
    for i, lo in enumerate(range(0, z_hbm.shape[0], width)):
        rows = min(width, z_hbm.shape[0] - lo)
        pixel_copies.append(pltpu.make_async_copy(
            z_hbm.at[pl.ds(lo, rows)], part.at[i, pl.ds(0, rows)], zsem.at[i]
        ))
    weight_copy(0).start()
    wk_copy = pltpu.make_async_copy(wk_hbm, wkv, wsem.at[nslots])
    wk_copy.start()
    for i in range(1, nslots):
        weight_copy(i).start()
    wv_copy = pltpu.make_async_copy(wv_hbm, wkv, wsem.at[nslots + 1])
    for copy in pixel_copies:
        copy.start()

    barrier = pltpu.get_barrier_semaphore()
    partners = [peer, across, diagonal] + [partner[b] for b in range(bits)]
    for p in partners:
        pl.semaphore_signal(barrier, inc=1, device_id=p, device_id_type=MESH)
    copies = []
    slot_count = [0]

    def remote(src, dst, device):
        slot = slot_count[0]
        slot_count[0] += 1
        return Remote(copies, src, dst, csend.at[slot], crecv.at[slot], device)

    def local(src, dst, slot):
        copy = pltpu.make_async_copy(src, dst, wsem.at[nslots + 2 + slot])
        copy.start()
        return copy

    def rows_loop(body, step=64, total=None):
        def run(i, carry):
            body(pl.ds(pl.multiple_of(i * step, step), step))
            return carry
        lax.fori_loop(0, (total or count) // step, run, 0, unroll=2)

    def columns_loop(body, step=512, total=width):
        def run(i, carry):
            body(pl.ds(pl.multiple_of(i * step, step), step))
            return carry
        lax.fori_loop(0, total // step, run, 0)

    def layer(k, into):
        def body(rows):
            unit, rs = norm_parts(stream[rows, :])
            rsb[k, rows, :] = jnp.broadcast_to(rs, (rs.shape[0], LANES))
            place = pl.ds(pl.multiple_of(into * count + rows.start, rows.size), rows.size)
            acts[place, :] = (unit * gain_refs[k][...]).astype(BF)
        rows_loop(body)

    def layer_back(k, normed, into, start=None):
        gain = gain_refs[k][...]
        inverse = 1.0 / gain

        def body(i, total):
            rows = pl.ds(pl.multiple_of(i * 64, 64), 64)
            place = pl.ds(pl.multiple_of(normed * count + i * 64, 64), 64)
            dn = dnorm[rows, :]
            unit = acts[place, :].astype(F32) * inverse
            scaled = dn * gain
            rs = rsb[k, rows, :][:, :1]
            mean = jnp.mean(scaled, axis=-1, keepdims=True)
            along = jnp.mean(scaled * unit, axis=-1, keepdims=True)
            before = upstr[rows, :] if start is None else gall[start, 0, rows, :].astype(F32)
            after = before + rs * (scaled - mean - unit * along)
            upstr[rows, :] = after
            gall[into, 0, rows, :] = after.astype(BF)
            return total + jnp.sum(dn * unit, axis=0, keepdims=True)
        gsum[pl.ds(k, 1), :] = lax.fori_loop(
            0, count // 64, body, jnp.zeros((1, width), F32), unroll=2
        )

    act_copies, grad_copies = {}, {}

    def share_act(k):
        away = pl.ds(pl.multiple_of((1 - core) * half, half), half)
        act_copies[k] = remote(acts.at[act(k), away], acts_in.at[k], peer)

    def share_grad(m):
        grad_copies[m] = remote(gall.at[m, 0], gall.at[m, 1], peer)

    clock = [0.0]
    small = dict(lo=0, size=lat, stage=0, up=[], copy=None, due=1e9)
    axes = [(core, peer), (chip, across)] + [(bit_of[b], partner[b]) for b in range(bits)]

    def small_send():
        bit, device = axes[small["stage"]]
        size = small["size"]
        if size > 16:
            size //= 2
            away = pl.multiple_of(small["lo"] + (1 - bit) * size, 16)
            keep = pl.multiple_of(small["lo"] + bit * size, 16)
            small["up"].append((device, keep, size))
            small["lo"], small["size"] = keep, size
        else:
            away = small["lo"]
        small["copy"] = remote(sm.at[pl.ds(away, size)], smr[small["stage"]], device)
        small["due"] = clock[0] + 2.5 + size * 512 * 4 / 75e3

    def small_grow():
        device, lo, size = small["up"].pop()
        rows = pl.ds(lo, size)
        small["copy"] = remote(sm_out.at[rows], sm_out.at[rows], device)
        small["due"] = clock[0] + 2.5 + size * 512 * 4 / 75e3

    def small_step():
        copy, size = small["copy"], small["size"]
        copy.wait_recv()
        if small["stage"] < len(axes):
            copy.wait_send()
            rows = pl.ds(small["lo"], size)
            sm[rows, :] = sm[rows, :] + smr[small["stage"]][...]
            small["stage"] += 1
            if small["stage"] < len(axes):
                small_send()
                return
            sm_out[rows, :] = sm[rows, :]
        if small["up"]:
            small_grow()
        else:
            small["due"] = 1e9

    state = {}
    free = {}
    pending = []

    def region(u, planes, lo, size):
        if planes == 4:
            return part.at[pl.ds(4 * u, 4), pl.ds(lo, size)]
        return part.at[pl.ds(4 * u + 2 * chip, 2), pl.ds(lo, size)]

    def send_stage(u):
        s = state[u]
        axis = orders[u][s["stage"]]
        k = s["stage"]
        if axis == "y":
            src = part.at[pl.ds(4 * u + 2 - 2 * chip, 2), pl.ds(s["lo"], s["size"])]
            s["planes"] = 2
        else:
            size = s["size"] // 2
            keep = s["lo"] + bit_of[axis] * size
            away = s["lo"] + (1 - bit_of[axis]) * size
            src = region(u, s["planes"], pl.multiple_of(away, share), size)
            s["lo"], s["size"] = pl.multiple_of(keep, share), size
        slot = sum(len(orders[v]) for v in range(u)) + k
        s["copy"] = Remote(copies, src, recv[u][k], usend.at[slot], urecv.at[slot], partner[axis])
        took = s["size"] * s["planes"] * LANES * 2 * 2 / 80e3
        links = {"y": {"y": 1}, 0: {"x": 1}, 1: {"inner": 1}}.get(axis, {"inner": 1, "middle": 2})
        begin = max([clock[0]] + [free.get(link, 0.0) for link in links])
        for link, share_of in links.items():
            free[link] = begin + took * share_of
        s["due"] = max(free[link] for link in links) + 4.0
        pending.append(u)

    def finish_stage(u):
        s = state[u]
        k = s["stage"]
        s["copy"].wait_recv()
        last = k == len(orders[u]) - 1
        mine = pl.ds(4 * u, 4) if s["planes"] == 4 else pl.ds(4 * u + 2 * chip, 2)
        if last:
            total = part[mine, pl.ds(s["lo"], s["size"])] + recv[u][k][...]
            if u == MATS:
                fin[FEATURE_UNIT] = total[0]
                initg_ref[...] = total[1]
            else:
                fin[2 * u : 2 * u + 2] = total
            s["done"] = True
            done_units.append(u)
            gather_ready()
            return
        step = min(s["size"], 256)

        def add(i, carry):
            off = pl.multiple_of(i * step, step)
            rows = pl.ds(pl.multiple_of(s["lo"] + off, share), step)
            part[mine, rows, :] = part[mine, rows, :] + recv[u][k][:, pl.ds(off, step), :]
            return carry
        lax.fori_loop(0, s["size"] // step, add, 0)
        s["stage"] += 1
        send_stage(u)

    done_units, gathers = [], []
    groups = [[0, 1, 2], [3, 4, 5], [6, 7, 8]]

    def gather_ready():
        while len(gathers) < len(groups) and all(u in done_units for u in groups[len(gathers)]):
            g = groups[len(gathers)]
            span = pl.ds(2 * g[0], 6 if g[-1] < MATS else 5)
            from_chip = remote(fin.at[span], fin_in.at[span], across)
            remote(fin.at[span], gat_ref.at[row, span], peer)
            gathers.append((g, from_chip, local(fin.at[span], gat_ref.at[row, span], len(gathers))))

    def serve():
        at = min((state[u]["due"], u) for u in pending) if pending else (1e9, None)
        if small["due"] <= at[0]:
            clock[0] = max(clock[0], small["due"])
            small_step()
        else:
            clock[0] = max(clock[0], at[0]) + 0.3
            pending.remove(at[1])
            finish_stage(at[1])

    def next_due():
        return min([small["due"]] + [state[u]["due"] for u in pending])

    def tick(us):
        clock[0] += 1.6 * us
        while next_due() <= clock[0]:
            serve()

    def begin_unit(u):
        state[u] = dict(stage=0, planes=4, lo=0, size=width, done=False)
        send_stage(u)

    def position(u, block):
        seq_bits = [a for a in orders[u] if a != "y"]
        pos = 0
        for at, b in enumerate(seq_bits):
            pos = pos + ((block // (1 << b)) % 2) * (1 << (bits - 1 - at))
        return pos

    def store_plane(u, plane, side, value):
        if share != LANES:
            value = value.astype(F32).T.astype(BF)
        for block_at in range(shards):
            place = pl.ds(position(u, block_at) * share, share)
            if share == LANES:
                part[pl.ds(4 * u + 2 * plane + side, 1), place, :] = value[:, block_at * share : (block_at + 1) * share][None]
            else:
                part[pl.ds(4 * u + 2 * plane + side, 1), place, :] = value[block_at * share : (block_at + 1) * share][None]

    def weight_grad(m):
        left = LEFT[m]
        act_copies[left].wait_recv()
        grad_copies[m].wait_recv()

        def run(plane, carry):
            own = pl.ds(pl.multiple_of(core * half + plane * MAIN, MAIN), MAIN)
            theirs = pl.ds(pl.multiple_of(plane * MAIN, MAIN), MAIN)
            lefts = jnp.concatenate([acts[act(left), own], acts_in[left, :, theirs]], axis=0)
            total = dot_tn(lefts, gall[m].reshape(2 * count, width)).astype(BF)
            store_plane(m, plane, 0, total[:LANES])
            store_plane(m, plane, 1, total[LANES:])
            return carry
        lax.fori_loop(0, 2, run, 0)
        begin_unit(m)

    cot_rows = pl.ds(pl.multiple_of(chip * block, block), block)
    c_own = local(cot_hbm.at[chip], gall.at[DOWN2, 0, cot_rows], 3)
    zbuf[pl.ds(chip, 1)] = init_ref[...][None]
    unit, unused = norm_parts(init_ref[...].astype(F32))
    own_normed = (unit * gain_refs[3][...]).astype(BF)
    w = weight(WQ)
    queries = dot(own_normed, w[...]).astype(BF)
    weight_done()
    wk_copy.wait()
    fill_rest(w_rest, wkv)
    fold_main = dot_nt(queries, wkv[:MAIN, :]) * cross_scale
    fold_rest = dot_nt(queries, w_rest[...]) * cross_scale
    own_rows = pl.ds(pl.multiple_of(row * block, block), block)
    seg = seg_ref[...].astype(F32)
    ids = jnp.concatenate([seg, jnp.zeros((LANES - 2, block), F32)], axis=0).T
    ids = pltpu.roll(ids, 5, 1)
    fold[own_rows, :MAIN] = fold_main.astype(BF)
    fold[own_rows, MAIN:] = (fold_rest + ids).astype(BF)
    wv_copy.start()
    pl.semaphore_wait(barrier, len(partners))
    fold_copies = [remote(fold.at[own_rows], fold.at[own_rows], p) for p in (across, diagonal, peer)]
    z_copy = remote(init_ref, zbuf.at[chip], across)
    c_copy = remote(cot_hbm.at[1 - chip], gall.at[DOWN2, 0, cot_rows], across)
    group = pixel_rs.shape[0]
    blocks = group // 4
    tall = gain_col.shape[0]

    fold_in = width // group

    def pixel_row(f, lo=0, rows=group):
        at = pl.ds(pl.multiple_of((f % fold_in) * group + lo, rows), rows)
        return part[pl.ds(f // fold_in, 1), at, :][0].astype(F32)

    zero = jnp.zeros((group, LANES), F32)
    for copy in pixel_copies:
        copy.wait()
    mean = lax.fori_loop(0, features, lambda f, acc: acc + pixel_row(f), zero, unroll=9)
    mean = mean * (1.0 / features)

    def spread(f, acc):
        centre = pixel_row(f) - mean
        return acc + centre * centre
    spread_sum = lax.fori_loop(0, features, spread, zero, unroll=9)
    rs_all = lax.rsqrt(spread_sum * (1.0 / features) + EPSILON)
    pixel_rs[...] = rs_all
    gain_col[...] = jnp.ones(gain_col.shape, F32)
    flat[features * group // 2 :, :] = jnp.zeros(((tall - features) * group // 2, LANES), F32)
    for s in range(2):
        xcat[s, 2 * MAIN + 16 :, :] = jnp.zeros((LANES - 16, xcat.shape[2]), BF)
    for k in range(2):
        half_rows = slice(k * (group // 2), (k + 1) * (group // 2))
        half_mean, half_rs = mean[half_rows], rs_all[half_rows]

        def scale(f, carry, k=k, half_mean=half_mean, half_rs=half_rs):
            value = pixel_row(f, k * (group // 2), group // 2)
            rows = pl.ds(pl.multiple_of(f * (group // 2), group // 2), group // 2)
            flat[rows, :] = (value - half_mean) * (half_rs * pixel_gain[f])
            if k == 0:
                gain_col[pl.ds(f, 1), :] = jnp.full((1, LANES), pixel_gain[f], F32)
            return carry
        lax.fori_loop(0, features, scale, 0, unroll=9)
        for s in range(2):
            for jb in range(blocks):
                cols = pl.ds(jb * LANES, LANES)
                value = flat[pl.ds(2 * jb + s, tall, stride=group // 2), :]
                xcat[s, k * MAIN : (k + 1) * MAIN, cols] = value[:MAIN].astype(BF)
                if k == 0:
                    rest0[s, :, cols] = value[MAIN:]
                else:
                    both = jnp.concatenate([rest0[s, :, cols], value[MAIN:]], axis=0)
                    xcat[s, 2 * MAIN : 2 * MAIN + 16, cols] = both.astype(BF)
    for copy in fold_copies:
        copy.wait_recv()

    lane = lax.broadcasted_iota(jnp.int32, (1, LANES), 1)
    image = (2 * row).astype(F32)

    def selectors(s, rows):
        ids = fold[rows, MAIN:].astype(F32)
        ids = jnp.where(s == 0, ids[:, 5:6], ids[:, 6:7])
        return jnp.where(ids == image, 1.0, 0.0), jnp.where(ids == image + 1.0, 1.0, 0.0)

    def spread_out(source, s, rows):
        first, second = selectors(s, rows)
        main = source[:, :MAIN].astype(F32)
        rest = jnp.where(lane < 5, source[:, MAIN:].astype(F32), 0.0)
        rest = rest * first + pltpu.roll(rest, 8, 1) * second
        return jnp.concatenate([main * first, main * second, rest], axis=1).astype(BF)

    def pull_in(s, rows, zero, one, rest):
        first, second = selectors(s, rows)
        rest = jnp.where(lane < 5, rest * first + pltpu.roll(rest, LANES - 8, 1) * second, 0.0)
        return zero * first + one * second, rest

    slots = xcat.shape[2]
    core_copies = []

    def send_core(turn):
        core_copies.append(remote(amat.at[turn, :, 1 - core], ain1.at[turn], peer))

    def core_sum(turn):
        core_copies[turn].wait_recv()
        return amat[turn, :, pl.ds(core, 1)][:, 0] + ain1[turn]

    for turn in range(2):
        s = 1 - chip if turn == 0 else chip
        seq = pl.ds(s, 1)
        for i in range(4):
            rows = pl.ds(i * block, block)
            gall[2 + 2 * turn + i // 2, 0, (i % 2) * block : (i % 2 + 1) * block, :CAT] = spread_out(
                fold[rows, :], s, rows
            )
        first_ok = jnp.where(pseg_ref[seq, :slots] == 2 * row, 1.0, 0.0)
        second_ok = jnp.where(pseg_ref[seq, slots:] == 2 * row + 1, 1.0, 0.0)

        def score_cols(cols, seq=seq, turn=turn):
            queries_cat = jnp.concatenate(
                [gall[2 + 2 * turn, 0, :, :CAT], gall[3 + 2 * turn, 0, :, :CAT]], axis=0
            )
            fbuf[:, cols] = dot(queries_cat, xcat[seq, :, cols][0])
        columns_loop(score_cols, 512, slots)
        if turn == 1:
            asum[...] = core_sum(0)
            step2 = remote(asum, ain2, across)

        def soften(rows, s=s, seq=seq, first_ok=first_ok, second_ok=second_ok):
            first, unused = selectors(s, rows)
            allowed = second_ok + first * (first_ok - second_ok)
            scores = jnp.where(allowed > 0.5, fbuf[rows, :], NEGATIVE)
            weights = jnp.exp(scores - jnp.max(scores, axis=1, keepdims=True))
            prob = (weights * (1.0 / jnp.sum(weights, axis=1, keepdims=True))).astype(BF)
            pbuf[seq, rows, :] = prob[None]
        rows_loop(soften, 64, lat)
        probs = pbuf[seq][0]
        zero = dot_nt(probs, xcat[seq, :MAIN, :][0])
        one = dot_nt(probs, xcat[seq, MAIN : 2 * MAIN, :][0])
        rest = dot_nt(probs, xcat[seq, 2 * MAIN :, :][0])
        main, rest = pull_in(s, pl.ds(0, lat), zero, one, rest)
        amat[turn, :, :, :, :MAIN] = main.astype(BF).reshape(2, 2, block, MAIN)
        amat[turn, :, :, :, MAIN:] = rest.astype(BF).reshape(2, 2, block, LANES)
        send_core(turn)
    spill = local(pbuf, pspill, 4)

    for at in range(4):
        who = core if at < 2 else 1 - core
        rows = pl.ds(pl.multiple_of((2 * (at % 2) + who) * block, block), block)
        turned = fold[rows, MAIN:].astype(F32).T
        idrow[:, at * block : (at + 1) * block] = jnp.where(chip == 0, turned[5:6], turned[6:7])
    own_ids = []
    for h in range(2):
        rows = pl.ds(pl.multiple_of((2 * h + core) * block, block), block)
        ids = fold[rows, MAIN:].astype(F32)
        own_ids.append(jnp.where(chip == 0, ids[:, 5:6], ids[:, 6:7]))
    idcol = jnp.concatenate(own_ids, axis=0)
    z_copy.wait_recv()
    remote(init_ref, zall.at[row], peer)
    other_row = row + 2 - 4 * chip
    remote(zbuf.at[1 - chip], zall.at[other_row], peer)
    z_local = [local(init_ref, zall.at[row], 5), local(zbuf.at[1 - chip], zall.at[other_row], 6)]
    c_copy.wait_recv()
    c_own.wait()
    share_grad(DOWN2)
    wv_copy.wait()
    fill_rest(w_rest, wkv)
    step2.wait_recv()
    amix[...] = (core_sum(1) + ain2[...]).reshape(count, FEAT_PAD)
    amix_copy = remote(amix, amix_in, peer)

    def attended_cols(cols):
        value = dot(amix[:, :MAIN], wkv[:MAIN, cols]) + dot(amix[:, MAIN:], w_rest[:, cols])
        qbuf[:, cols] = value.astype(BF)
    columns_loop(attended_cols)
    w = weight(WO)

    def one_cols(cols):
        start = zbuf[:, :, cols].reshape(count, cols.size).astype(F32)
        stream[:, cols] = start + dot(qbuf[...], w[:, cols])
    columns_loop(one_cols)
    weight_done()

    def mlp(k, normed, active, up_id, down_id):
        layer(k, normed)
        share_act(normed)
        w_up = weight(up_id)

        def up_cols(cols):
            value, slope = gelu_parts(dot(acts[act(normed), :], w_up[:, cols]))
            acts[act(active), cols] = value.astype(BF)
            slopes[active // 4, :, cols] = slope.astype(BF)
        columns_loop(up_cols)
        weight_done()
        share_act(active)
        w_down = weight(down_id)

        def down_cols(cols):
            stream[:, cols] += dot(acts[act(active), :], w_down[:, cols])
        columns_loop(down_cols)
        weight_done()

    mlp(0, NORMED1, ACTIVE1, UP, DOWN)
    layer(1, SELFN)
    share_act(SELFN)
    kv_copies = {}
    for index, dst in ((KW, 0), (VW, 1), (QW, None)):
        w_now = weight(index)

        def project(cols, dst=dst, w_now=w_now):
            value = dot(acts[act(SELFN), :], w_now[:, cols]).astype(BF)
            if dst is None:
                qbuf[:, cols] = value
            else:
                kv[dst, 0, :, cols] = value
        columns_loop(project)
        weight_done()
        if dst is not None:
            kv_copies[dst] = remote(kv.at[dst, 0], kv.at[dst, 1], peer)
    spill.wait()
    kv_copies[0].wait_recv()
    kv_copies[1].wait_recv()

    def heads(body):
        def run(pair, carry):
            for side in range(2):
                cols = pl.ds(pl.multiple_of((2 * pair + side) * head_width, head_width), head_width)
                rows = pl.ds(pl.multiple_of((pair % 2) * count, count), count)
                body(cols, (pl.ds(pair // 2, 1), rows, pl.ds(side * lat, lat)))
            return carry
        lax.fori_loop(0, HEADS // 2, run, 0, unroll=2)

    def attend(cols, keep):
        keys = kv[0, :, :, cols].reshape(lat, head_width)
        values = kv[1, :, :, cols].reshape(lat, head_width)
        scores = dot_nt(qbuf[:, cols], keys) * self_scale
        scores = jnp.where(idcol == idrow[...], scores, NEGATIVE)
        weights = jnp.exp(scores - jnp.max(scores, axis=1, keepdims=True))
        prob = (weights * (1.0 / jnp.sum(weights, axis=1, keepdims=True))).astype(BF)
        pbuf[keep] = prob[None]
        acts[act(MIXED), cols] = dot(prob, values).astype(BF)
    heads(attend)
    share_act(MIXED)
    w_so = weight(SO)

    def three_cols(cols):
        stream[:, cols] += dot(acts[act(MIXED), :], w_so[:, cols])
    columns_loop(three_cols)
    weight_done()
    mlp(2, NORMED2, ACTIVE2, UPB, DOWNB)
    dmix[...] = stream[...].astype(BF)
    lat_ref[pl.ds(chip, 1)] = dmix[pl.ds(pl.multiple_of(chip * block, block), block), :][None]
    lat_copy = remote(
        dmix.at[pl.ds(pl.multiple_of((1 - chip) * block, block), block)], lat_ref.at[chip], across
    )

    weight_grad(DOWN2)
    tick(2.0)

    def mlp_back(k, normed, active, m_down, m_up, up_id, down_id, into, start=None):
        w_down = weight(down_id)

        def act_cols(cols):
            grad = dot_nt(gall[m_down, 0], w_down[cols, :]).astype(BF).astype(F32)
            gall[m_up, 0, :, cols] = (grad * slopes[active // 4, :, cols].astype(F32)).astype(BF)
        columns_loop(act_cols)
        weight_done()
        share_grad(m_up)
        tick(1.0)
        w_up = weight(up_id)

        def norm_cols(cols):
            dnorm[:, cols] = dot_nt(gall[m_up, 0], w_up[cols, :])
        columns_loop(norm_cols)
        weight_done()
        if into == 0:
            grad_copies[DOWN2].wait_send()
            grad_copies[UP2].wait_send()
        layer_back(k, normed, into, start)
        tick(1.5)

    mlp_back(2, NORMED2, ACTIVE2, DOWN2, UP2, UPB, DOWNB, SOUT, DOWN2)

    share_grad(SOUT)
    weight_grad(UP2)
    tick(1.5)
    w_so2 = weight(SO)
    lat_copy.wait_send()

    def mixed_cols(cols):
        dmix[:, cols] = dot_nt(gall[SOUT, 0], w_so2[cols, :]).astype(BF)
    columns_loop(mixed_cols)
    weight_done()

    def attend_back(cols, keep):
        keys = kv[0, :, :, cols].reshape(lat, head_width)
        values = kv[1, :, :, cols].reshape(lat, head_width)
        dm = dmix[:, cols]
        prob_b = pbuf[keep][0]
        prob = prob_b.astype(F32)
        grad = dot_nt(dm, values)
        delta = jnp.sum(prob * grad, axis=1, keepdims=True)
        score = (prob * (grad - delta)).astype(BF)
        gall[SQ, 0, :, cols] = (dot(score, keys) * self_scale).astype(BF)
        dk = (dot_tn(score, qbuf[:, cols]) * self_scale).astype(BF)
        dv = dot_tn(prob_b, dm).astype(BF)
        gall[SK, 0, :, cols] = dk[:count]
        gall[SV, 0, :, cols] = dv[:count]
        kv[0, 1, :, cols] = dk[count:]
        kv[1, 1, :, cols] = dv[count:]
    heads(attend_back)
    unspill = local(pspill, pbuf, 4)
    share_dkv = remote(kv.at[:, 1], dkv_in, peer)
    share_grad(SQ)
    tick(4.0)
    weight_grad(SOUT)
    tick(1.0)
    share_dkv.wait_recv()

    def add_kv(rows):
        for at, m in ((0, SK), (1, SV)):
            gall[m, 0, rows, :] = gall[m, 0, rows, :] + dkv_in[at, rows, :]
    rows_loop(add_kv)
    share_grad(SK)
    share_grad(SV)
    for at, (m, index) in enumerate(((SQ, QW), (SK, KW), (SV, VW))):
        w_now = weight(index)

        def normed_cols(cols, at=at, m=m, w_now=w_now):
            value = dot_nt(gall[m, 0], w_now[cols, :])
            if at == 0:
                dnorm[:, cols] = value
            else:
                dnorm[:, cols] += value
        columns_loop(normed_cols)
        weight_done()
    layer_back(1, SELFN, DOWN1)
    share_grad(DOWN1)
    tick(3.0)
    weight_grad(SQ)
    tick(1.0)
    weight_grad(SK)
    tick(1.0)
    mlp_back(0, NORMED1, ACTIVE1, DOWN1, UP1, UP, DOWN, 0)

    w_o = weight(WO)

    def attended_back(cols):
        gall[1, 0, :, cols] = dot_nt(gall[0, 0], w_o[cols, :]).astype(BF)
    columns_loop(attended_back)
    weight_done()
    share_cd = remote(gall.at[1 - core, 0], gcd_in, peer)
    folded = jnp.concatenate([dot_nt(gall[1, 0], wkv[:MAIN, :]), dot_nt(gall[1, 0], w_rest[...])], axis=1)
    along = jnp.sum(folded * amix[...].astype(F32), axis=0, keepdims=True)
    gsum[3:4, :FEAT_PAD] = along
    gsum[3:4, FEAT_PAD:] = jnp.zeros((1, width - FEAT_PAD), F32)
    da_all[pl.ds(chip, 1), :, pl.ds(core, 1)] = folded.astype(BF).reshape(1, 2, 1, block, FEAT_PAD)
    mine = da_all.at[chip, :, core]
    da_across = remote(mine, mine, across)
    da_peer = remote(mine, mine, peer)
    tick(2.0)
    weight_grad(SV)
    tick(1.0)
    da_across.wait_recv()
    other = da_all.at[1 - chip, :, core]
    da_other = remote(other, other, peer)
    weight_grad(DOWN1)
    tick(1.0)
    weight_grad(UP1)
    tick(1.0)

    share_cd.wait_recv()
    amix_copy.wait_recv()
    lefts = jnp.concatenate([amix[:, :MAIN], amix_in[:, :MAIN]], axis=0)
    grads = jnp.concatenate([gall[pl.ds(core, 1), 0][0], gcd_in[...]], axis=0)
    total = dot_tn(lefts, grads).astype(BF)
    for plane in range(2):
        store_plane(MATS, plane, 0, total[plane * LANES : (plane + 1) * LANES])
    for plane in range(2):
        store_plane(MATS, plane, 1, upstr[plane * block : (plane + 1) * block, :].astype(BF))
    begin_unit(MATS)
    gsum[4:, :] = jnp.zeros((gsum.shape[0] - 4, width), F32)
    rests = [dot_tn(amix[:, MAIN:], gall[side, 0])[:8] for side in range(2)]
    for i in range(8):
        cols = slice(i * LANES, (i + 1) * LANES)
        both = jnp.concatenate([rests[0][:, cols], rests[1][:, cols]], axis=0)
        sm[16 * i : 16 * (i + 1), FEAT_PAD:] = both.astype(BF)
        sm[128 + 16 * i : 128 + 16 * (i + 1), FEAT_PAD:] = gsum[:, cols].astype(BF)
    sm[256:, FEAT_PAD:] = jnp.zeros((lat - 256, LANES), BF)
    tick(2.0)

    da_peer.wait_recv()
    da_other.wait_recv()
    unspill.wait()

    def score_rows(s):
        return wslots.at[s, pl.ds(0, lat)]

    def da_rows(s):
        return wslots.at[s, pl.ds(lat, lat), pl.ds(0, CAT)]

    def q_rows(s):
        return wslots.at[2, pl.ds(s * lat, lat), pl.ds(0, CAT)]

    for s in range(2):
        for i in range(4):
            rows = pl.ds(i * block, block)
            wslots[s, lat + i * block : lat + (i + 1) * block, :CAT] = spread_out(
                da_all[s, i // 2, i % 2], s, rows
            )
            wslots[2, s * lat + i * block : s * lat + (i + 1) * block, :CAT] = spread_out(
                fold[rows, :], s, rows
            )

        def back_cols(cols, s=s):
            fbuf[:, cols] = dot(wslots[s, lat:, :CAT], xcat[s, :, cols])
        columns_loop(back_cols, 512, slots)

        def score_back(rows, s=s):
            prob = pbuf[s, rows, :].astype(F32)
            grad = fbuf[rows, :]
            delta = jnp.sum(prob * grad, axis=1, keepdims=True)
            wslots[s, rows, :] = (prob * (grad - delta)).astype(BF)
        rows_loop(score_back, 64, lat)
        scores = wslots[s, :lat, :]
        zero = dot_nt(scores, xcat[s, :MAIN, :])
        one = dot_nt(scores, xcat[s, MAIN : 2 * MAIN, :])
        rest = dot_nt(scores, xcat[s, 2 * MAIN :, :])
        main, rest = pull_in(s, pl.ds(0, lat), zero, one, rest)
        if s == 0:
            bsum[:, :MAIN] = main
            bsum[:, MAIN:] = rest
        else:
            sm[:, :MAIN] = (bsum[:, :MAIN] + main).astype(BF)
            sm[:, MAIN:FEAT_PAD] = (bsum[:, MAIN:] + rest).astype(BF)
        tick(4.0)

    small_send()
    for copy in act_copies.values():
        copy.wait_send()
    for s in range(2):
        for at, (lo, size) in enumerate(((0, MAIN), (MAIN, MAIN), (2 * MAIN, LANES))):
            cols = pl.ds(lo, size)
            total = dot_tn(wslots[2, s * lat : (s + 1) * lat, cols], wslots[s, :lat, :])
            total = total + dot_tn(wslots[s, lat:, cols], pbuf[s])
            acts[pl.ds(s * CAT + lo, size), :] = total.astype(BF)
            tick(2.0)

    main_gain, rest_gain = gain_col[:MAIN, :], gain_col[MAIN:, :]
    inverse[...] = 1.0 / gain_col[...]
    y_copy = None
    for k in range(2):
        if y_copy is not None:
            y_copy.wait()
        for s in range(2):

            def pixel_step(jb, carry, k=k, s=s):
                cols = pl.ds(pl.multiple_of(jb * LANES, LANES), LANES)
                up_main = acts[s * CAT + k * MAIN : s * CAT + (k + 1) * MAIN, cols].astype(F32)
                up_rest = acts[s * CAT + 2 * MAIN : s * CAT + 2 * MAIN + 16, cols].astype(F32)
                up_rest = up_rest[8 * k : 8 * k + 8]
                x_main = xcat[s, k * MAIN : (k + 1) * MAIN, cols].astype(F32)
                x_rest = xcat[s, 2 * MAIN : 2 * MAIN + 16, cols].astype(F32)[8 * k : 8 * k + 8]
                rs = pixel_rs[pl.ds(k * (group // 2) + 2 * jb + s, 1), :]
                scaled_main, scaled_rest = up_main * main_gain, up_rest * rest_gain

                def mean_of(a, b):
                    whole = jnp.sum(a, axis=0, keepdims=True) + jnp.sum(b, axis=0, keepdims=True)
                    return whole * (1.0 / features)
                centre = mean_of(scaled_main, scaled_rest)
                along = mean_of(up_main * x_main, up_rest * x_rest)
                unit_main, unit_rest = x_main * inverse[:MAIN, :], x_rest * inverse[MAIN:, :]
                out_main = rs * (scaled_main - centre - unit_main * along)
                out_rest = rs * (scaled_rest - centre - unit_rest * along)
                flat[pl.ds(2 * jb + s, tall, stride=group // 2), :] = jnp.concatenate(
                    [out_main, out_rest], axis=0
                )
                return carry
            lax.fori_loop(0, blocks, pixel_step, 0)
            tick(2.0)
        y_copy = local(flat.at[pl.ds(0, features * group // 2)], y_ref.at[k], 7 + k)
    while next_due() < 1e9:
        serve()
    for g, from_chip, own in gathers:
        from_chip.wait_recv()
        span = pl.ds(2 * g[0], 6 if g[-1] < MATS else 5)
        remote(fin_in.at[span], gat_ref.at[other_row, span], peer)
        own.wait()
        z_local.append(local(fin_in.at[span], gat_ref.at[other_row, span], 9 + g[0] // 3))
    for copy in z_local + [y_copy]:
        copy.wait()
    for copy in copies:
        copy.finish()


def finish_kernel(*refs):
    it = iter(refs)

    def take(n=None):
        return next(it) if n is None else [next(it) for _ in range(n)]

    y_in, lat_in = take(2)
    ins = take(8)
    query_gain, pixel_gain = take(2)
    y_out, lat_out, init_out, pixel_gain_out, key_out, value_out = take(6)
    gain_outs = take(4)
    mat_outs = take(MATS + 2)
    held = take(8)
    summed, small, fold, init_all, wq, wk, wv, init_sum = held
    unit, normed, total, mats, wk_rest, wv_rest, y_buf, lat_buf, back = take(9)
    sem, out_sem = take(2)
    features, width = ins[5].shape
    lat = init_all.shape[0]
    block = lat // 4
    j = lax.axis_index("seq")
    row = lax.axis_index("row")
    cross_scale = 1.0 / math.sqrt(width)

    through = [
        (pltpu.make_async_copy(y_in.at[k], y_buf.at[:, pl.ds(k * y_in.shape[2], y_in.shape[2])], sem.at[8 + k]))
        for k in range(2)
    ] + [pltpu.make_async_copy(lat_in, lat_buf, sem.at[10])]
    copies = [
        pltpu.make_async_copy(src, dst, sem.at[i]) for i, (src, dst) in enumerate(zip(ins, held))
    ]
    for copy in [copies[3], copies[0]] + through + [copies[i] for i in (1, 5, 4, 6, 2, 7)]:
        copy.start()
    outs = []

    def put(src, dst):
        copy = pltpu.make_async_copy(src, dst, out_sem.at[len(outs)])
        copy.start()
        outs.append(copy)

    copies[3].wait()
    query_rs = []
    for r in range(4):
        rows = pl.ds(r * block, block)
        value, scale = norm_parts(init_all[rows, :].astype(F32))
        unit[rows, :] = value
        normed[rows, :] = (value * query_gain[...]).astype(BF)
        query_rs.append(scale)
    copies[0].wait()
    for m in range(MATS):
        for r in range(4):
            for h in range(2):
                at = (r % 2) * (width // 2) + (r // 2) * 2 * LANES + h * LANES
                mats[m, at : at + LANES, :] = summed[r, 2 * m + h].astype(F32)
        put(mats.at[m], mat_outs[m])
    for copy in through:
        copy.wait()
    put(y_buf, y_out)
    put(lat_buf, lat_out)
    for copy in copies[1:3] + copies[4:]:
        copy.wait()
    fill_rest(wv_rest, wv)
    fill_rest(wk_rest, wk)
    my_cols = pl.ds(pl.multiple_of(j * LANES, LANES), LANES)

    for n in range(width // 256):
        cols = pl.ds(n * 256, 256)
        value = dot(small[:, :MAIN], wk[:MAIN, cols]) + dot(small[:, MAIN:FEAT_PAD], wk_rest[:, cols])
        total[:, cols] = (value * cross_scale).astype(BF)

    def put_turned(index, value):
        for n in range(width // LANES):
            mats[index, n * LANES : (n + 1) * LANES, :] = value[:, n * LANES : (n + 1) * LANES].T
        put(mats.at[index], mat_outs[index])
    put_turned(MATS, dot_tn(total[:, my_cols], normed[...]))
    outer = [
        [summed[2 * y + c, FEATURE_UNIT].astype(F32) for y in range(2)] for c in range(2)
    ]
    rests = small[pl.ds(pl.multiple_of(j * 16, 16), 16), FEAT_PAD:]
    value_out[:LANES, :] = outer[1][0]
    value_out[LANES:MAIN, :] = outer[1][1]
    value_out[MAIN:, :] = rests.astype(F32)[8 : 8 + features - MAIN]
    summed_c = jnp.concatenate(outer[0], axis=0).astype(BF)
    put_turned(MATS + 1, dot_tn(summed_c, wv[:MAIN, :]) + dot_tn(rests, wv_rest[:16, :]))
    my_queries = dot(normed[...], wq[:, my_cols]).astype(BF)
    key_turned = dot_tn(my_queries, small[:, :FEAT_PAD]) * cross_scale
    key_out[...] = jnp.concatenate(
        [key_turned[:, n * LANES : (n + 1) * LANES].T for n in range(3)], axis=0
    )[:features]
    for i in range(8):
        chunk = small[128 + 16 * i : 128 + 16 * (i + 1), FEAT_PAD:].astype(F32)
        for g in range(3):
            gain_outs[g][i : i + 1, :] = chunk[g : g + 1]
    scores = small[:, :FEAT_PAD].astype(F32)
    part = jnp.sum(fold[...].astype(F32) * scores, axis=0, keepdims=True)
    rest_sum = [small[128 + 16 * i : 128 + 16 * (i + 1), FEAT_PAD:].astype(F32)[3:4] for i in range(3)]
    whole = (part + jnp.concatenate(rest_sum, axis=1))[:, :features]
    pixel_gain_out[...] = (whole / pixel_gain[...].reshape(1, features)).reshape(features)
    own = pl.ds(pl.multiple_of(row * block, block), block)
    own_rs = query_rs[0]
    for r in range(1, 4):
        own_rs = jnp.where(row == r, query_rs[r], own_rs)
    sums = jnp.zeros((block, 1), F32)
    alongs = jnp.zeros((block, 1), F32)
    for n in range(width // 256):
        cols = pl.ds(n * 256, 256)
        back[:, cols] = dot_nt(total[...], wq[cols, :])
        row_sum = jnp.sum(back[:, cols] * unit[:, cols], axis=0, keepdims=True)
        for i in range(2):
            gain_outs[3][2 * n + i : 2 * n + i + 1, :] = row_sum[:, i * LANES : (i + 1) * LANES]
        scaled = back[own, cols] * query_gain[:, cols]
        sums = sums + jnp.sum(scaled, axis=1, keepdims=True)
        alongs = alongs + jnp.sum(scaled * unit[own, cols], axis=1, keepdims=True)
    scaled = back[own, my_cols] * query_gain[:, my_cols]
    query_in = own_rs * (scaled - sums * (1.0 / width) - unit[own, my_cols] * (alongs * (1.0 / width)))
    init_out[...] = init_sum[...].astype(F32) + query_in
    for copy in outs:
        copy.wait()


def finish(y, latents, summed, small, init_sum, fold, init_all, wq, wk, wv, query_gain, pixel_gain):
    features, width = wk.shape
    lat = init_all.shape[0]
    block = lat // 4
    vmem = pl.BlockSpec(memory_space=pltpu.VMEM)
    hbm = pl.BlockSpec(memory_space=pl.ANY)

    def f32(*shape):
        return jax.ShapeDtypeStruct(shape, F32)

    outs = pl.pallas_call(
        finish_kernel,
        out_shape=[f32(features, 2 * y.shape[2], LANES), jax.ShapeDtypeStruct(latents.shape, BF), f32(block, LANES),
                   f32(features), f32(features, LANES), f32(features, LANES)]
        + [f32(width // LANES, LANES)] * 4 + [f32(width, LANES)] * (MATS + 2),
        in_specs=[hbm] * 10 + [vmem] * 2,
        out_specs=[hbm] * 2 + [vmem] * 8 + [hbm] * (MATS + 2),
        scratch_shapes=[
            pltpu.VMEM(shape, BF)
            for shape in (summed.shape, small.shape, fold.shape, init_all.shape,
                          wq.shape, wk.shape, wv.shape, init_sum.shape)
        ]
        + [
            pltpu.VMEM((lat, width), F32),
            pltpu.VMEM((lat, width), BF),
            pltpu.VMEM((lat, width), BF),
            pltpu.VMEM((MATS + 2, width, LANES), F32),
            pltpu.VMEM((LANES, width), BF),
            pltpu.VMEM((LANES, width), BF),
            pltpu.VMEM((features, 2 * y.shape[2], LANES), F32),
            pltpu.VMEM(latents.shape, BF),
            pltpu.VMEM((lat, width), F32),
            pltpu.SemaphoreType.DMA((11,)),
            pltpu.SemaphoreType.DMA((MATS + 4,)),
        ],
        compiler_params=pltpu.CompilerParams(vmem_limit_bytes=VMEM_LIMIT),
    )(y, latents, summed, small, fold, init_all, wq, wk, wv, init_sum, query_gain[None],
      pixel_gain)
    y, latents, init_grad, pixel_gain_grad, key_grad, value_grad = outs[:6]
    return (y, latents, init_grad, outs[6:10], pixel_gain_grad, key_grad, value_grad, outs[10:])


def whole_stack(shards, z, pixel_gain, pseg, init, cots, seg, wk, wv, gains, weights):
    width = init.shape[1]
    block = init.shape[0]
    count = 2 * block
    lat = 2 * count
    share = width // shards
    half = width // 2
    bits = shards.bit_length() - 1
    orders = unit_orders(bits)
    nslots = 3
    features = wk.shape[0]
    group = z.shape[0] // features
    slots = group * LANES // 4
    small, size = [], lat
    for i in range(bits + 2):
        size = size // 2 if size > 16 else size
        small.append((size, 512))
    scratch = [
        ((nslots, width, width), BF),
        (wk.shape, BF),
        ((LANES, width), BF),
        ((2, block, width), BF),
        ((2, 2, block, FEAT_PAD), BF),
        ((2, block, FEAT_PAD), BF),
        ((2, block, FEAT_PAD), BF),
        ((count, FEAT_PAD), BF),
        ((count, FEAT_PAD), BF),
        ((2, 2, 2, block, FEAT_PAD), BF),
        ((lat, width), F32),
        ((3, count, LANES), F32),
        ((6 * count, width), BF),
        ((6, count, half), BF),
        ((2, count, width), BF),
        ((count, width), BF),
        ((2, 2, count, width), BF),
        ((2, lat, slots), BF),
        ((count, width), BF),
        ((2, count, width), BF),
        ((MATS, 2, count, width), BF),
        ((count, width), BF),
        ((FEATURE_UNIT + 1, share, LANES), BF),
        ((2, 2, 2, block, FEAT_PAD), BF),
        ((lat, FEAT_PAD), F32),
        ((16, width), F32),
        ((1, lat), F32),
        ((lat, 512), BF),
        ((2, CAT, slots), BF),
        (((MAIN + 8) * group // 2, LANES), F32),
        ((2, 8, slots), F32),
        ((group, LANES), F32),
        ((MAIN + 8, LANES), F32),
        ((MAIN + 8, LANES), F32),
        ((FEATURE_UNIT + 1, share, LANES), BF),
        ((UNITS * 4, width, LANES), BF),
    ]
    for order in orders:
        scratch += [(shape, BF) for shape in stage_shapes(order, width)]
    scratch += [(shape, BF) for shape in small]
    stages = sum(len(order) for order in orders)
    vmem = pl.BlockSpec(memory_space=pltpu.VMEM)
    hbm = pl.BlockSpec(memory_space=pl.ANY)
    return pl.pallas_call(
        functools.partial(
            main_kernel, (shards, width, count, dict(small_stages=len(small)))
        ),
        out_shape=[
            jax.ShapeDtypeStruct((2, block, width), BF),
            jax.ShapeDtypeStruct((lat, 512), BF),
            jax.ShapeDtypeStruct((4, FEATURE_UNIT + 1, share, LANES), BF),
            jax.ShapeDtypeStruct((share, LANES), BF),
            jax.ShapeDtypeStruct((lat, FEAT_PAD), BF),
            jax.ShapeDtypeStruct((4, block, width), BF),
            jax.ShapeDtypeStruct((2, features * group // 2, LANES), F32),
            jax.ShapeDtypeStruct((2, lat, slots), BF),
        ],
        in_specs=[hbm, pl.BlockSpec(memory_space=pltpu.SMEM), vmem, vmem, hbm, vmem]
        + [hbm] * 2 + [vmem] * 4 + [hbm] * 10,
        out_specs=[vmem, vmem, hbm, vmem, vmem, hbm, hbm, hbm],
        scratch_shapes=[pltpu.VMEM(shape, kind) for shape, kind in scratch]
        + [
            pltpu.SemaphoreType.DMA((nslots + 2 + 13,)),
            pltpu.SemaphoreType.DMA((nslots * 4,)),
            pltpu.SemaphoreType.DMA((-(-z.shape[0] // width),)),
            pltpu.SemaphoreType.DMA((stages,)),
            pltpu.SemaphoreType.DMA((stages,)),
            pltpu.SemaphoreType.DMA((80,)),
            pltpu.SemaphoreType.DMA((80,)),
        ],
        compiler_params=pltpu.CompilerParams(
            collective_id=0, has_side_effects=True, vmem_limit_bytes=VMEM_LIMIT
        ),
    )(z, pixel_gain, pseg, init, cots, seg, wk, wv, *[g[None] for g in gains], *weights)


VMEM_LIMIT = 63 * 1024 * 1024


def body(
    pixels, pixel_seg, latent_seg, latent_init, cotangent,
    pixel_gain, query_gain, query_weight, key_weight, value_weight, output_weight,
    mlp_gain, up_weight, down_weight,
    self_gain, self_query, self_key, self_value, self_output,
    second_gain, second_up, second_down,
):
    seqs, pix, features = pixels.shape
    block, width = latent_init.shape
    shards = lax.axis_size("seq")
    lat = block * lax.axis_size("row")
    row = lax.axis_index("row")
    cross_scale = 1.0 / math.sqrt(width)
    tiles = pix // LANES

    z = pixels.transpose(2, 0, 1).reshape(features, seqs, tiles, LANES)
    z = z.transpose(0, 2, 1, 3).reshape(features * seqs * tiles, LANES)
    latents, small, summed, init_sum, fold, init_all, y, unused = whole_stack(
        shards, z, pixel_gain, pixel_seg, latent_init, cotangent, latent_seg, key_weight, value_weight,
        (mlp_gain, self_gain, second_gain, query_gain),
        (query_weight, output_weight, up_weight, down_weight, self_query, self_key, self_value,
         self_output, second_up, second_down),
    )
    init_all = init_all.reshape(lat, width)
    y = y.reshape(2, features, tiles, LANES)
    if width // shards == LANES:
        y, latents, init_grad, gains, pixel_gain_grad, key_grad, value_grad, mats = finish(
            y, latents, summed, small, init_sum, fold, init_all, query_weight, key_weight,
            value_weight, query_gain, pixel_gain,
        )
    else:
        y = y.transpose(1, 0, 2, 3)
    pixel_grad = y.reshape(features, tiles, seqs, LANES).transpose(2, 1, 3, 0)
    pixel_grad = pixel_grad.reshape(seqs, pix, features)
    if width // shards == LANES:
        mlp_gain_grad, self_gain_grad, second_gain_grad, query_gain_grad = [
            g.reshape(width) for g in gains
        ]
        return (
            latents, pixel_grad, init_grad, pixel_gain_grad,
            query_gain_grad, mlp_gain_grad, self_gain_grad, second_gain_grad,
            mats[MATS], key_grad, value_grad, mats[MATS + 1], mats[UP1], mats[DOWN1],
            mats[SQ], mats[SK], mats[SV], mats[SOUT], mats[UP2], mats[DOWN2],
        )

    share = width // shards
    at = lax.axis_index("seq") * share

    def columns(arr):
        return lax.dynamic_slice_in_dim(arr, at, share, arr.ndim - 1)

    score_b = small[:, :features]
    side = small[:, FEAT_PAD:]
    rests = side[:128].reshape(8, 2, 8, LANES).transpose(1, 2, 0, 3).reshape(2, 8, width)
    sums = side[128:256].reshape(8, 16, LANES).transpose(1, 0, 2).reshape(16, width).astype(F32)
    pixel_gain_grad = (
        jnp.sum(fold[:, :features].astype(F32) * score_b.astype(F32), axis=0) + sums[3, :features]
    ) / pixel_gain
    units = summed.reshape(2, 2, FEATURE_UNIT + 1, share, LANES)
    mats = units[:, :, :FEATURE_UNIT].reshape(2, 2, MATS, 2, share, LANES)
    mats = mats.transpose(2, 1, 0, 3, 5, 4).reshape(MATS, width, share).astype(F32)
    outer = units[:, :, FEATURE_UNIT].transpose(1, 0, 3, 2).reshape(2, MAIN, share)
    outer = jnp.concatenate([outer, columns(rests)[:, : features - MAIN]], axis=1)
    value_grad = outer[1].astype(F32)
    output_grad = dot_tn(value_weight, outer[0])
    query_unit, query_rs = norm_parts(init_all.astype(F32))
    query_normed = (query_unit * query_gain).astype(BF)
    my_queries = dot(query_normed, columns(query_weight)).astype(BF)
    key_grad = dot_tn(score_b, my_queries) * cross_scale
    query_total = (dot(score_b, key_weight) * cross_scale).astype(BF)
    query_grad = dot_tn(query_normed, columns(query_total))
    query_in, query_gain_grad = norm_back(
        query_unit, query_rs, query_gain, dot_nt(query_total, query_weight)
    )
    init_grad = init_sum.T.astype(F32) + lax.dynamic_slice(query_in, (row * block, at), (block, share))
    return (
        latents, pixel_grad, init_grad,
        pixel_gain_grad, query_gain_grad, sums[0], sums[1], sums[2],
        query_grad, key_grad, value_grad, output_grad, mats[UP1], mats[DOWN1],
        mats[SQ], mats[SK], mats[SV], mats[SOUT], mats[UP2], mats[DOWN2],
    )


def solution(mesh):
    placed = (
        P("seq", "row", None), P("seq", "row"), P("seq", "row"), P("row", None),
        P("seq", "row", None),
    ) + (P(),) * 17
    cols = P(None, "seq")
    return jax.shard_map(
        body,
        mesh=mesh,
        in_specs=placed,
        out_specs=(P("seq", "row", None), P("seq", "row", None), P("row", "seq"))
        + (P(),) * 5 + (cols,) * 12,
        check_vma=False,
    )
```
